128 devices in a mesh: cp: 32 (over x, z, core), hd: 4 (over y).
Axes of the slice: x: 4, y: 4, z: 4, core: 2. Of those that a mesh axis runs over, the one named last changes fastest.
Arguments:
- queries: bfloat16 [16384, 4096], P('cp', 'hd'), may hold values from -100 to 100
- keys: bfloat16 [16384, 512], P('cp', 'hd'), may hold values from -5 to 5
- values: bfloat16 [16384, 512], P('cp', 'hd'), may hold values from -4.5 to 4.5
- attn_out: bfloat16 [16384, 4096], P('cp', 'hd'), may hold values from -4.5 to 4.5
- out_grad: bfloat16 [16384, 4096], P('cp', 'hd'), may hold values from -4.5 to 4.5
- out_weight: bfloat16 [4096, 4096], P('hd'), may hold values from -0.09375 to 0.09375
- segment: int32 [16384], replicated, may hold values from 0 to 15, never falling along the last dimension, each value on 1 to 2048 neighbouring positions
Outputs:
- query_grad: bfloat16 [16384, 4096], P('cp', 'hd')
- key_grad: bfloat16 [16384, 512], P('cp', 'hd')
- value_grad: bfloat16 [16384, 512], P('cp', 'hd')
The draws below stay inside these ranges and needn't reach their ends.
Inputs may be any that keep to these rules, and one draw needn't show every extreme that they name: `segment`: ids never fall along the sequence; every document holds 1 to 2048 tokens, and one holds exactly 2048.
All inputs are finite; a program needn't handle non-finite values.
Results may differ from the reference program's by a relative error of at most 0.006.
Values may be sent and summed in bfloat16 or wider, within the bound.
No kernel may reach another device: no remote copies, remote signals or barrier semaphores. Data moves between devices by JAX's collectives and lax.ppermute only.
A program may use at most 256 MiB of HBM per device.

```python
import math
import jax
import jax.numpy as jnp
import numpy as np
from jax import lax

DM = 4096
QUERY_HEADS = 32
KEY_VALUE_HEADS = 4
HEAD_WIDTH = 128
BS = 512
MOST_BLK = 4
HG = 8
PACKED_TOKENS = 16384
MOST = 2048
DOCS = 16


def shared_keys(key):
    return jnp.clip(jax.random.normal(key, (PACKED_TOKENS, KEY_VALUE_HEADS * HEAD_WIDTH), jnp.float32), -4.5, 4.5)


def draw_keys(key, part):
    base_offset = shared_keys(key)
    return base_offset.astype(jnp.bfloat16)


def draw_queries(key, part):
    key = jax.random.fold_in(key, 5)
    drawn = jnp.clip(jax.random.normal(key, (PACKED_TOKENS, QUERY_HEADS * HEAD_WIDTH), jnp.float32), -4.5, 4.5)
    return drawn.astype(jnp.bfloat16)


def levels(own_key, dims, shards, smallest, top_value):
    factor_of, own = 1.0, jax.random.fold_in(own_key, 6)
    for dim, shards_of in shards:
        draws = jnp.exp(jax.random.uniform(jax.random.fold_in(own, dim), (shards_of,), jnp.float32, smallest / len(shards), top_value / len(shards)))
        factor_of = factor_of * jnp.repeat(draws, dims[dim] // shards_of).reshape([-1 if axis == dim else 1 for axis in range(len(dims))])
    return factor_of


def split_up(number_of, total, reach, skew):
    weights = [(1 << 20) // math.isqrt(rank ** skew) + 1 for rank in range(2, number_of + 1)]
    rest, counts = total - reach - (number_of - 1), [1] * (number_of - 1)
    while rest > 0:
        movable = [i for i in range(number_of - 1) if counts[i] < reach]
        whole, remaining = sum([weights[i] for i in movable]), rest
        for i in movable:
            addition = min(reach - counts[i], max(1, remaining * weights[i] // whole), rest)
            counts[i] = counts[i] + addition
            rest = rest - addition
    return np.array([reach] + counts)


def ragged(key, count, total, limit, lean):
    if count == 2:
        one = jax.random.randint(key, (), max(1, total - limit), min(limit, total - 1) + 1)
        return jnp.stack([one, total - one])
    lengths = jnp.asarray(split_up(count, total, limit, lean), jnp.int32)
    twos = (count - 1) // 2
    source_of, receiver = lengths[1:1 + 2 * twos:2], lengths[2:2 + 2 * twos:2]
    room = jnp.minimum(source_of - 1, limit - receiver)
    passed = jax.random.randint(jax.random.fold_in(key, 1), (twos,), 0, 1 << 20) % (room + 1)
    lengths = lengths.at[1:1 + 2 * twos:2].set(source_of - passed).at[2:2 + 2 * twos:2].set(receiver + passed)
    return lengths[jax.random.permutation(jax.random.fold_in(key, 2), count)]


def normal_values(rng, shape, width, reach, shards=(), kind=jnp.bfloat16):
    level = levels(rng, shape, shards, -0.22, 0.18) if shards else 1.0
    entries = jax.random.normal(rng, shape, jnp.float32) * width * level
    return jnp.minimum(jnp.maximum(entries, -reach), reach).astype(kind)


def setup_inputs(seed: int = 0) -> dict:
    key_of = jax.random.split(jax.random.key(seed), 8)
    queries = draw_queries(jax.random.fold_in(key_of[7], 71), 0)
    keys = draw_keys(jax.random.fold_in(key_of[7], 71), 0)
    values = normal_values(key_of[2], (PACKED_TOKENS, KEY_VALUE_HEADS * HEAD_WIDTH), 1.0, 4.5, ((0, 32), (1, 4)))
    attn_out = normal_values(key_of[3], (PACKED_TOKENS, QUERY_HEADS * HEAD_WIDTH), 1.0, 4.5, ((0, 32), (1, 4)))
    out_grad = normal_values(key_of[4], (PACKED_TOKENS, DM), 1.0, 4.5, ((0, 32), (1, 4)))
    out_weight = normal_values(key_of[5], (QUERY_HEADS * HEAD_WIDTH, DM), DM ** -0.5, 0.09375, ((0, 4),))
    segment = jnp.searchsorted(jnp.cumsum(ragged(key_of[6], DOCS, PACKED_TOKENS, MOST, 1)), jnp.arange(PACKED_TOKENS), side="right").astype(jnp.int32)
    return {"queries": queries, "keys": keys, "values": values, "attn_out": attn_out, "out_grad": out_grad, "out_weight": out_weight, "segment": segment}


def reference(queries, keys, values, attn_out, out_grad, out_weight, segment):
    scale = HEAD_WIDTH ** -0.5
    dout = jnp.dot(out_grad, out_weight.T, preferred_element_type=jnp.float32).astype(jnp.bfloat16)
    delta = jnp.sum((dout.astype(jnp.float32) * attn_out.astype(jnp.float32)).reshape(PACKED_TOKENS, QUERY_HEADS, HEAD_WIDTH), axis=2)
    span = (MOST_BLK + 1) * BS
    margin = MOST_BLK * BS
    count = PACKED_TOKENS // BS
    padded_segments = jnp.concatenate([jnp.full((margin,), -1, jnp.int32), segment.astype(jnp.int32)])
    padded_positions = jnp.arange(PACKED_TOKENS + margin, dtype=jnp.int32) - margin
    query_parts = []
    key_parts = []
    value_parts = []
    for head_group in range(KEY_VALUE_HEADS):
        cols = slice(head_group * HG * HEAD_WIDTH, (head_group + 1) * HG * HEAD_WIDTH)
        group_queries = queries[:, cols].reshape(PACKED_TOKENS, HG, HEAD_WIDTH)
        group_grads = dout[:, cols].reshape(PACKED_TOKENS, HG, HEAD_WIDTH)
        group_delta = delta[:, head_group * HG:(head_group + 1) * HG]
        zero_rows = jnp.zeros((margin, HEAD_WIDTH), jnp.bfloat16)
        group_keys = jnp.concatenate([zero_rows, keys[:, head_group * HEAD_WIDTH:(head_group + 1) * HEAD_WIDTH]])
        group_values = jnp.concatenate([zero_rows, values[:, head_group * HEAD_WIDTH:(head_group + 1) * HEAD_WIDTH]])

        def advance(running, index, group_queries=group_queries, group_grads=group_grads,
                    group_delta=group_delta, group_keys=group_keys, group_values=group_values):
            start = (index * BS).astype(jnp.int32)
            query_block = lax.dynamic_slice_in_dim(group_queries, start, BS, 0).astype(jnp.float32)
            grad_block = lax.dynamic_slice_in_dim(group_grads, start, BS, 0).astype(jnp.float32)
            delta_block = lax.dynamic_slice_in_dim(group_delta, start, BS, 0).T[:, :, None]
            key_window = lax.dynamic_slice_in_dim(group_keys, start, span, 0).astype(jnp.float32)
            value_window = lax.dynamic_slice_in_dim(group_values, start, span, 0).astype(jnp.float32)
            key_segments = lax.dynamic_slice_in_dim(padded_segments, start, span, 0)
            key_positions = lax.dynamic_slice_in_dim(padded_positions, start, span, 0)
            query_segments = lax.dynamic_slice_in_dim(segment.astype(jnp.int32), start, BS, 0)
            query_positions = start + jnp.arange(BS, dtype=jnp.int32)
            visible = (key_segments[None, :] == query_segments[:, None]) & (key_positions[None, :] <= query_positions[:, None]) & (key_positions[None, :] >= 0)
            scores = jnp.einsum("qhd,kd->hqk", query_block, key_window) * scale
            top = jnp.max(jnp.where(visible, scores, -jnp.inf), axis=2, keepdims=True)
            total = jnp.sum(jnp.where(visible, jnp.exp(scores - top), 0.0), axis=2, keepdims=True)
            log_total = top + jnp.log(total)
            prob = jnp.where(visible, jnp.exp(scores - log_total), 0.0)
            prob_low = prob.astype(jnp.bfloat16)
            prob_grad = jnp.einsum("qhd,kd->hqk", grad_block, value_window)
            score_grad = (prob * (prob_grad - delta_block)).astype(jnp.bfloat16).astype(jnp.float32)
            query_part = jnp.einsum("hqk,kd->qhd", score_grad, key_window) * scale
            key_part = jnp.einsum("hqk,qhd->kd", score_grad, query_block) * scale
            value_part = jnp.einsum("hqk,qhd->kd", prob_low.astype(jnp.float32), grad_block)
            window = lax.dynamic_slice_in_dim(running, start, span, 0) + jnp.concatenate([key_part, value_part], axis=1)
            running = lax.dynamic_update_slice_in_dim(running, window, start, 0)
            return running, query_part.astype(jnp.bfloat16).reshape(BS, HG * HEAD_WIDTH)

        initial = jnp.zeros((PACKED_TOKENS + margin, 2 * HEAD_WIDTH), jnp.float32)
        running, query_blocks = lax.scan(advance, initial, jnp.arange(count, dtype=jnp.int32))
        query_parts.append(query_blocks.reshape(PACKED_TOKENS, HG * HEAD_WIDTH))
        key_parts.append(running[margin:, :HEAD_WIDTH].astype(jnp.bfloat16))
        value_parts.append(running[margin:, HEAD_WIDTH:].astype(jnp.bfloat16))
    return (jnp.concatenate(query_parts, axis=1), jnp.concatenate(key_parts, axis=1), jnp.concatenate(value_parts, axis=1))
```

```python
import functools

import jax
import jax.numpy as jnp
from jax import lax
from jax.experimental import pallas as pl
from jax.experimental.pallas import tpu as pltpu
from jax.sharding import PartitionSpec as P

HEAD_WIDTH = 128
HEADS = 8
BS = 512
MOST_BLK = 4
WINDOW = (MOST_BLK + 1) * BS
BEHIND = MOST_BLK * BS
TILE = 256
TILES = WINDOW // TILE
CHUNK = 256
SCALE = HEAD_WIDTH ** (-0.5)
LOG2E = 1.4426950408889634
HIDDEN = -1e30
PAIR = 2


def shifted(value, axis, by):
    length = lax.axis_size(axis)
    return lax.ppermute(value, axis, [(i, (i + by) % length) for i in range(length)])


def swapped(value):
    length = lax.axis_size("cp")
    return lax.ppermute(value, "cp", [(i, i ^ 1) for i in range(length)])


def nt(a, b):
    return lax.dot_general(a, b, (((1,), (1,)), ((), ())), preferred_element_type=jnp.float32)


def nn(a, b):
    return lax.dot_general(a, b, (((1,), (0,)), ((), ())), preferred_element_type=jnp.float32)


def tn(a, b):
    return lax.dot_general(a, b, (((0,), (0,)), ((), ())), preferred_element_type=jnp.float32)


def stats_kernel(row0, bounds, q_ref, k_ref, start_ref, p_ref, e_scr, m_scr):
    last = (BEHIND + row0) // TILE
    factor = SCALE * LOG2E
    lanes = PAIR * CHUNK

    def scores(tile):
        keys = k_ref[pl.ds(pl.multiple_of(tile * TILE, TILE), TILE), :]
        return jnp.concatenate(
            [
                nt(keys, q_ref[:, h * HEAD_WIDTH : (h + 1) * HEAD_WIDTH])
                for h in range(PAIR)
            ],
            axis=1,
        )

    def masked(tile, s):
        key = lax.broadcasted_iota(jnp.int32, (TILE, CHUNK), 0) + tile * TILE
        row = lax.broadcasted_iota(jnp.int32, (TILE, CHUNK), 1) + (BEHIND + row0)
        seen = (key >= start_ref[...]) & (key <= row)
        return jnp.where(jnp.concatenate([seen] * PAIR, axis=1), s, HIDDEN)

    def step(tile, state, edge):
        top, total = state
        s = scores(tile)
        if edge:
            s = masked(tile, s)
        new_top = jnp.maximum(top, jnp.max(s, axis=0, keepdims=True))
        e = jnp.exp2((s - new_top) * factor)
        e_scr[pl.ds(pl.multiple_of(tile * TILE, TILE), TILE), :] = e
        m_scr[pl.ds(pl.multiple_of(tile * 8, 8), 8), :] = jnp.broadcast_to(new_top, (8, lanes))
        total = total * jnp.exp2((top - new_top) * factor) + jnp.sum(e, axis=0, keepdims=True)
        return new_top, total

    low, full = bounds[0], bounds[1]
    state = (
        jnp.full((1, lanes), HIDDEN, jnp.float32),
        jnp.zeros((1, lanes), jnp.float32),
    )
    state = step(last, state, True)
    full = jnp.minimum(full, last)
    state = lax.fori_loop(0, last - full, lambda i, c: step(last - 1 - i, c, False), state)
    state = lax.fori_loop(0, full - low, lambda i, c: step(full - 1 - i, c, True), state)
    top, total = state
    inverse = 1.0 / total

    def finish(tile, carry):
        rows = pl.ds(pl.multiple_of(tile * TILE, TILE), TILE)
        then = m_scr[pl.ds(pl.multiple_of(tile * 8, 8), 8), :][:1, :]
        p_ref[rows, :] = (e_scr[rows, :] * (jnp.exp2((then - top) * factor) * inverse)).astype(
            jnp.bfloat16
        )
        return carry

    lax.fori_loop(low, last + 1, finish, 0)


def stats(row0, bounds, queries, keys, starts):
    lanes = PAIR * CHUNK
    grid_spec = pltpu.PrefetchScalarGridSpec(
        num_scalar_prefetch=1,
        grid=(HEADS // PAIR,),
        in_specs=[
            pl.BlockSpec((CHUNK, PAIR * HEAD_WIDTH), lambda g, b: (row0 // CHUNK, g)),
            pl.BlockSpec((WINDOW, HEAD_WIDTH), lambda g, b: (0, 0)),
            pl.BlockSpec((1, CHUNK), lambda g, b: (0, row0 // CHUNK)),
        ],
        out_specs=pl.BlockSpec((WINDOW, lanes), lambda g, b: (0, g)),
        scratch_shapes=[
            pltpu.VMEM((WINDOW, lanes), jnp.float32),
            pltpu.VMEM((TILES * 8, lanes), jnp.float32),
        ],
    )
    return pl.pallas_call(
        functools.partial(stats_kernel, row0),
        grid_spec=grid_spec,
        out_shape=jax.ShapeDtypeStruct((WINDOW, HEADS * CHUNK), jnp.bfloat16),
        compiler_params=pltpu.CompilerParams(vmem_limit_bytes=40 * 2**20),
        cost_estimate=pl.CostEstimate(
            flops=2 * 2 * HEADS * CHUNK * WINDOW * HEAD_WIDTH,
            bytes_accessed=2 * HEADS * CHUNK * WINDOW,
            transcendentals=HEADS * CHUNK * WINDOW,
        ),
        name=f"stats{row0}",
    )(bounds, queries, keys, starts)


def main_kernel(
    row0, first, bounds, *refs
):
    (p_ref, k_ref, v_ref, own_ref, prev_ref, next_ref, far_a, far_b, w_ref, q_ref, a_ref) = refs[:11]
    refs = refs[11:]
    if first:
        sum_ref, dq_ref, dout_scr, q_scr, delta_scr, ds_scr, dq_scr = refs
    else:
        before_ref, far_ref, here_ref, dq_ref, dout_scr, q_scr, delta_scr, ds_scr, dq_scr = refs
    tile = pl.program_id(0)
    low, place = bounds[0], bounds[2]
    last = (BEHIND + row0) // TILE

    @pl.when(tile == 0)
    def _():
        width = own_ref.shape[1]
        half = width // 2

        def columns(by, offset, size):
            return pl.ds(
                pl.multiple_of(lax.rem(place + by, 4) * width + offset, half), size
            )

        pieces = [
            (own_ref, columns(0, 0, width)),
            (prev_ref, columns(3, 0, width)),
            (next_ref, columns(1, 0, width)),
            (far_a, columns(2, 0, half)),
            (far_b, columns(2, half, half)),
        ]
        ones = jnp.ones((8, HEAD_WIDTH), jnp.float32)
        for pair in range(HEADS // 2):
            cols = slice(pair * 2 * HEAD_WIDTH, (pair + 1) * 2 * HEAD_WIDTH)
            total = None
            for ref, where in pieces:
                part = nt(ref[...], w_ref[cols, where])
                total = part if total is None else total + part
            dout = total.astype(jnp.bfloat16)
            product = dout.astype(jnp.float32) * a_ref[:, cols].astype(jnp.float32)
            for side in range(2):
                head = 2 * pair + side
                rows = slice(head * CHUNK, (head + 1) * CHUNK)
                part = slice(side * HEAD_WIDTH, (side + 1) * HEAD_WIDTH)
                dout_scr[rows, :] = dout[:, part]
                q_scr[rows, :] = q_ref[:, head * HEAD_WIDTH : (head + 1) * HEAD_WIDTH]
                delta_scr[:, rows] = lax.dot_general(
                    ones,
                    product[:, part],
                    (((1,), (1,)), ((), ())),
                    precision=lax.Precision.HIGHEST,
                    preferred_element_type=jnp.float32,
                )
        dq_scr[...] = jnp.zeros_like(dq_scr)

    def emit(dk, dv):
        both = jnp.concatenate([dk, dv], axis=1)
        if first:
            sum_ref[...] = both
        else:
            both = both + before_ref[...]

            @pl.when(tile < BEHIND // TILE)
            def _():
                far_ref[...] = both.astype(jnp.bfloat16)

            @pl.when(tile >= BEHIND // TILE)
            def _():
                here_ref[...] = both

    active = (tile >= low) & (tile <= last)

    @pl.when(active)
    def _():
        for head in range(HEADS):
            rows = slice(head * CHUNK, (head + 1) * CHUNK)
            dp = nt(v_ref[...], dout_scr[rows, :])
            prob = p_ref[:, rows].astype(jnp.float32)
            ds_scr[:, rows] = (prob * (dp - delta_scr[:1, rows])).astype(jnp.bfloat16)
        dv = nn(p_ref[...], dout_scr[...])
        dk = nn(ds_scr[...], q_scr[...]) * SCALE
        dq_scr[...] += tn(k_ref[...], ds_scr[...])
        emit(dk, dv)

    @pl.when(jnp.logical_not(active))
    def _():
        zero = jnp.zeros((TILE, HEAD_WIDTH), jnp.float32)
        emit(zero, zero)

    @pl.when(tile == TILES - 1)
    def _():
        for head in range(HEADS):
            rows = slice(head * CHUNK, (head + 1) * CHUNK)
            dq_ref[:, head * HEAD_WIDTH : (head + 1) * HEAD_WIDTH] = (
                jnp.transpose(dq_scr[:, rows]) * SCALE
            ).astype(jnp.bfloat16)


def main(row0, bounds, prob, keys, values, pieces, weight, queries, attn, before):
    first = before is None
    width = HEADS * HEAD_WIDTH
    chunk = row0 // CHUNK
    lanes = HEADS * CHUNK

    def active(t, b):
        return jnp.clip(t, b[0], (BEHIND + row0) // TILE)

    tile_of = lambda t, b: (active(t, b), 0)
    whole = pl.BlockSpec(memory_space=pltpu.VMEM)
    in_specs = [
        pl.BlockSpec((TILE, lanes), tile_of),
        pl.BlockSpec((TILE, HEAD_WIDTH), tile_of),
        pl.BlockSpec((TILE, HEAD_WIDTH), tile_of),
        pl.BlockSpec((CHUNK, width), lambda t, b: (chunk, 0)),
        whole,
        whole,
        whole,
        whole,
        whole,
        pl.BlockSpec((CHUNK, width), lambda t, b: (chunk, 0)),
        pl.BlockSpec((CHUNK, width), lambda t, b: (chunk, 0)),
    ]
    args = [prob, keys, values, *pieces, weight, queries, attn]
    dq_spec = pl.BlockSpec((CHUNK, width), lambda t, b: (0, 0))
    dq_shape = jax.ShapeDtypeStruct((CHUNK, width), jnp.bfloat16)
    if first:
        out_specs = [pl.BlockSpec((TILE, 2 * HEAD_WIDTH), lambda t, b: (t, 0)), dq_spec]
        out_shape = [jax.ShapeDtypeStruct((WINDOW, 2 * HEAD_WIDTH), jnp.float32), dq_shape]
    else:
        in_specs.append(pl.BlockSpec((TILE, 2 * HEAD_WIDTH), lambda t, b: (t, 0)))
        args.append(before)
        edge = BEHIND // TILE
        out_specs = [
            pl.BlockSpec((TILE, 2 * HEAD_WIDTH), lambda t, b: (jnp.minimum(t, edge - 1), 0)),
            pl.BlockSpec((TILE, 2 * HEAD_WIDTH), lambda t, b: (jnp.maximum(t - edge, 0), 0)),
            dq_spec,
        ]
        out_shape = [
            jax.ShapeDtypeStruct((BEHIND, 2 * HEAD_WIDTH), jnp.bfloat16),
            jax.ShapeDtypeStruct((BS, 2 * HEAD_WIDTH), jnp.float32),
            dq_shape,
        ]
    grid_spec = pltpu.PrefetchScalarGridSpec(
        num_scalar_prefetch=1,
        grid=(TILES,),
        in_specs=in_specs,
        out_specs=out_specs,
        scratch_shapes=[
            pltpu.VMEM((lanes, HEAD_WIDTH), jnp.bfloat16),
            pltpu.VMEM((lanes, HEAD_WIDTH), jnp.bfloat16),
            pltpu.VMEM((8, lanes), jnp.float32),
            pltpu.VMEM((TILE, lanes), jnp.bfloat16),
            pltpu.VMEM((HEAD_WIDTH, lanes), jnp.float32),
        ],
    )
    return pl.pallas_call(
        functools.partial(main_kernel, row0, first),
        grid_spec=grid_spec,
        out_shape=out_shape,
        compiler_params=pltpu.CompilerParams(vmem_limit_bytes=40 * 2**20),
        cost_estimate=pl.CostEstimate(
            flops=2 * 4 * 2 * lanes * WINDOW * HEAD_WIDTH,
            bytes_accessed=2 * lanes * WINDOW + 8 * 2**20,
            transcendentals=0,
        ),
        name=f"main{row0}",
    )(bounds, *args)


def body(queries, keys, values, attn_out, out_grad, out_weight, segment):
    place = lax.axis_index("hd")
    device = lax.axis_index("cp")
    odd = lax.rem(device, 2) == 1
    chunks = BS // CHUNK
    half = out_grad.shape[1] // 2

    grads = [out_grad[c * CHUNK : (c + 1) * CHUNK] for c in range(chunks)]
    near = [(shifted(g, "hd", 1), shifted(g, "hd", -1)) for g in grads]
    opposite = [
        (shifted(a[:, :half], "hd", 1), shifted(b[:, half:], "hd", -1)) for a, b in near
    ]

    here = jnp.concatenate([keys, values], axis=1)
    two = shifted(here, "cp", 2)
    four = shifted(here, "cp", 4)
    other = swapped(
        jnp.where(odd, jnp.concatenate([two, four], axis=0), jnp.concatenate([here, two], axis=0))
    )
    window = jnp.concatenate([four, other[BS:], two, other[:BS], here], axis=0)
    window_keys, window_values = window[:, :HEAD_WIDTH], window[:, HEAD_WIDTH:]

    padded = jnp.concatenate([jnp.full((BEHIND,), -1, jnp.int32), segment])
    around = lax.dynamic_slice_in_dim(padded, device * BS, WINDOW, 0)
    own = around[BEHIND:]
    starts = jnp.sum((around[:, None] < own[None, :]).astype(jnp.int32), axis=0)

    def bounds_of(row0):
        first, final = starts[row0], starts[row0 + CHUNK - 1]
        return jnp.stack([first // TILE, (final + TILE - 1) // TILE, place]).astype(jnp.int32)

    bounds = [bounds_of(c * CHUNK) for c in range(chunks)]
    starts = starts[None, :]
    probs = [
        stats(c * CHUNK, bounds[c], queries, window_keys, starts) for c in range(chunks)
    ]
    total, dq0 = main(
        0, bounds[0], probs[0], window_keys, window_values,
        (out_grad, *near[0], *opposite[0]), out_weight, queries, attn_out, None,
    )
    far, mine, dq1 = main(
        CHUNK, bounds[1], probs[1], window_keys, window_values,
        (out_grad, *near[1], *opposite[1]), out_weight, queries, attn_out, total,
    )

    back = swapped(jnp.concatenate([far[BS : 2 * BS], far[3 * BS :]], axis=0))
    back_three, back_one = back[:BS].astype(jnp.float32), back[BS:].astype(jnp.float32)
    to_four = far[:BS].astype(jnp.float32) + jnp.where(odd, back_three, 0.0)
    to_two = far[2 * BS : 3 * BS].astype(jnp.float32) + jnp.where(odd, back_one, back_three)
    mine = mine + jnp.where(odd, 0.0, back_one)
    from_four = shifted(to_four.astype(jnp.bfloat16), "cp", -4)
    from_two = shifted(to_two.astype(jnp.bfloat16), "cp", -2)
    mine = mine + from_four.astype(jnp.float32) + from_two.astype(jnp.float32)
    return (
        jnp.concatenate([dq0, dq1], axis=0),
        mine[:, :HEAD_WIDTH].astype(jnp.bfloat16),
        mine[:, HEAD_WIDTH:].astype(jnp.bfloat16),
    )


def solution(mesh):
    return jax.shard_map(
        body,
        mesh=mesh,
        in_specs=(
            P("cp", "hd"),
            P("cp", "hd"),
            P("cp", "hd"),
            P("cp", "hd"),
            P("cp", "hd"),
            P("hd", None),
            P(),
        ),
        out_specs=(P("cp", "hd"), P("cp", "hd"), P("cp", "hd")),
        check_vma=False,
    )
```

```python
import functools

import jax
import jax.numpy as jnp
from jax import lax
from jax.experimental import pallas as pl
from jax.experimental.pallas import tpu as pltpu
from jax.sharding import PartitionSpec as P

HEAD_WIDTH = 128
HEADS = 8
BS = 512
MOST_BLK = 4
BEHIND = MOST_BLK * BS
WINDOW = BEHIND + BS
TILE = 256
CHUNK = 256
TILES = BEHIND // TILE + 1
SPAN = TILES * TILE
LANES = HEADS * CHUNK
SCALE = HEAD_WIDTH ** (-0.5)
LOG2E = 1.4426950408889634
HIDDEN = -1e30
MIB = 2**20
WHOLE = pl.BlockSpec(memory_space=pltpu.VMEM)


def shifted(value, axis, by):
    length = lax.axis_size(axis)
    return lax.ppermute(value, axis, [(i, (i + by) % length) for i in range(length)])


def swapped(value):
    length = lax.axis_size("cp")
    return lax.ppermute(value, "cp", [(i, i ^ 1) for i in range(length)])


def nt(a, b):
    return lax.dot_general(a, b, (((1,), (1,)), ((), ())), preferred_element_type=jnp.float32)


def nn(a, b):
    return lax.dot_general(a, b, (((1,), (0,)), ((), ())), preferred_element_type=jnp.float32)


def tn(a, b):
    return lax.dot_general(a, b, (((0,), (0,)), ((), ())), preferred_element_type=jnp.float32)


def window_tile(refs, tile):
    four, other, two, here = refs
    block, part = divmod(tile, BS // TILE)
    ref, row = [(four, 0), (other, BS), (two, 0), (other, 0), (here, 0)][block]
    row = row + part * TILE
    return ref[row : row + TILE, :]


def head_lanes(head):
    return slice(head * CHUNK, (head + 1) * CHUNK)


def head_columns(head):
    return slice(head * HEAD_WIDTH, (head + 1) * HEAD_WIDTH)


def stats_kernel(chunk, q_ref, four, other, two, here, start_ref, e_ref, inv_ref, even, odd):
    keys = (four, other, two, here)
    held = (even, odd)
    rows = slice(chunk * CHUNK, (chunk + 1) * CHUNK)
    start = start_ref[:, rows]
    factor = SCALE * LOG2E

    def score(head, j, top):
        s = nt(window_tile(keys, chunk + j), q_ref[rows, head_columns(head)])
        key = lax.broadcasted_iota(jnp.int32, (TILE, CHUNK), 0)
        seen = key >= start - (chunk + j) * TILE
        if j == TILES - 1:
            seen = seen & (key <= lax.broadcasted_iota(jnp.int32, (TILE, CHUNK), 1))
        s = jnp.where(seen, s, HIDDEN)
        held[head % 2][j * TILE : (j + 1) * TILE, :] = s
        most = jnp.max(s.reshape(TILE // 8, 8, CHUNK), axis=0)
        return most if top is None else jnp.maximum(top, most)

    def weigh(head, j, top, total):
        at = slice(j * TILE, (j + 1) * TILE)
        e = jnp.exp2(held[head % 2][at, :] * factor - top)
        e_ref[at, head_lanes(head)] = e.astype(jnp.bfloat16)
        part = jnp.sum(e.reshape(TILE // 8, 8, CHUNK), axis=0)
        return part if total is None else total + part

    following = None
    for j in range(TILES):
        following = score(0, j, following)
    for head in range(HEADS):
        top = jnp.max(following, axis=0, keepdims=True) * factor
        following = total = None
        for j in range(TILES):
            if head + 1 < HEADS:
                following = score(head + 1, j, following)
            total = weigh(head, j, top, total)
        inv_ref[:, head_lanes(head)] = jnp.broadcast_to(
            1.0 / jnp.sum(total, axis=0, keepdims=True), (8, CHUNK)
        )


def stats(chunk, queries, keys, starts):
    return pl.pallas_call(
        functools.partial(stats_kernel, chunk),
        in_specs=[WHOLE] * 6,
        out_specs=[WHOLE] * 2,
        out_shape=[
            jax.ShapeDtypeStruct((SPAN, LANES), jnp.bfloat16),
            jax.ShapeDtypeStruct((8, LANES), jnp.float32),
        ],
        scratch_shapes=[pltpu.VMEM((SPAN, CHUNK), jnp.float32)] * 2,
        compiler_params=pltpu.CompilerParams(vmem_limit_bytes=14 * MIB),
        cost_estimate=pl.CostEstimate(
            flops=2 * LANES * SPAN * HEAD_WIDTH,
            bytes_accessed=8 * MIB,
            transcendentals=LANES * SPAN,
        ),
        name=f"stats{chunk}",
    )(queries, *keys, starts)


def main_kernel(chunk, *refs):
    place_ref, e_ref, inv_ref = refs[:3]
    keys, values = refs[3:7], refs[7:11]
    own_ref, prev_ref, next_ref, far_a, far_b, w_ref, q_ref, a_ref = refs[11:19]
    if chunk == 0:
        both_ref, dq_ref = refs[19:21]
    else:
        before_ref, far_ref, mine_ref, dq_ref = refs[19], *refs[21:24]
        both_ref = refs[-1]
    k_scr, ds_scr, dout_scr = refs[24:27] if chunk else refs[21:24]
    rows = slice(chunk * CHUNK, (chunk + 1) * CHUNK)
    place = place_ref[0]
    width = own_ref.shape[1]
    half = width // 2

    def columns(by, offset, size):
        return pl.ds(pl.multiple_of(lax.rem(place + by, 4) * width + offset, half), size)

    pieces = [
        (own_ref, rows, columns(0, 0, width)),
        (prev_ref, slice(None), columns(3, 0, width)),
        (next_ref, slice(None), columns(1, 0, width)),
        (far_a, slice(None), columns(2, 0, half)),
        (far_b, slice(None), columns(2, half, half)),
    ]
    for j in range(TILES):
        k_scr[j * TILE : (j + 1) * TILE, :] = window_tile(keys, chunk + j)

    for pair in range(HEADS // 2):
        cols = slice(2 * pair * HEAD_WIDTH, 2 * (pair + 1) * HEAD_WIDTH)
        acc = None
        for ref, at, where in pieces:
            part = nt(ref[at, :], w_ref[cols, where])
            acc = part if acc is None else acc + part
        dout = acc.astype(jnp.bfloat16).astype(jnp.float32)
        product = jnp.transpose(dout * a_ref[rows, cols].astype(jnp.float32))
        for side in range(2):
            head = 2 * pair + side
            inv = inv_ref[:1, head_lanes(head)]
            down = jnp.transpose(jnp.broadcast_to(inv, (HEAD_WIDTH, CHUNK)))
            scaled = (dout[:, head_columns(side)] * down).astype(jnp.bfloat16)
            dout_scr[head_lanes(side), :] = scaled
            delta = jnp.sum(product[head_columns(side), :], axis=0, keepdims=True) * inv
            for j in range(TILES):
                at = slice(j * TILE, (j + 1) * TILE)
                dp = nt(window_tile(values, chunk + j), scaled)
                prob = e_ref[at, head_lanes(head)].astype(jnp.float32)
                ds_scr[at, head_lanes(side)] = (prob * (dp - delta)).astype(jnp.bfloat16)
            dq = tn(k_scr[...], ds_scr[:, head_lanes(side)])
            dq_ref[:, head_columns(head)] = (jnp.transpose(dq) * SCALE).astype(jnp.bfloat16)
        lanes = slice(2 * pair * CHUNK, 2 * (pair + 1) * CHUNK)
        queries = jnp.concatenate(
            [q_ref[rows, head_columns(2 * pair)], q_ref[rows, head_columns(2 * pair + 1)]], axis=0
        )
        for j in range(TILES):
            at = slice(j * TILE, (j + 1) * TILE)
            dv = nn(e_ref[at, lanes], dout_scr[...])
            dk = nn(ds_scr[at, :], queries) * SCALE
            if pair == 0:
                if chunk == 0:
                    both_ref[at, :HEAD_WIDTH] = dk
                    both_ref[at, HEAD_WIDTH:] = dv
                    continue
                if j < TILES - 1:
                    old = before_ref[(j + 1) * TILE : (j + 2) * TILE, :]
                    dk, dv = dk + old[:, :HEAD_WIDTH], dv + old[:, HEAD_WIDTH:]
            else:
                dk, dv = dk + both_ref[at, :HEAD_WIDTH], dv + both_ref[at, HEAD_WIDTH:]
            last = chunk == 1 and pair == HEADS // 2 - 1
            tile = chunk + j
            if last and tile < BEHIND // TILE:
                to = slice(tile * TILE, (tile + 1) * TILE)
                far_ref[to, :HEAD_WIDTH] = dk.astype(jnp.bfloat16)
                far_ref[to, HEAD_WIDTH:] = dv.astype(jnp.bfloat16)
            elif last:
                to = slice(tile * TILE - BEHIND, (tile + 1) * TILE - BEHIND)
                mine_ref[to, :HEAD_WIDTH] = dk
                mine_ref[to, HEAD_WIDTH:] = dv
            else:
                both_ref[at, :HEAD_WIDTH] = dk
                both_ref[at, HEAD_WIDTH:] = dv
    if chunk == 1:
        far_ref[:TILE, :] = before_ref[:TILE, :].astype(jnp.bfloat16)


def main(chunk, place, stat, keys, values, pieces, weight, queries, attn, before, dq_before):
    width = HEADS * HEAD_WIDTH
    args = [place, *stat, *keys, *values, *pieces, weight, queries, attn]
    in_specs = [pl.BlockSpec(memory_space=pltpu.SMEM)] + [WHOLE] * (len(args) - 1)
    dq_spec = pl.BlockSpec((CHUNK, width), lambda i: (chunk, 0))
    dq_shape = jax.ShapeDtypeStruct((BS, width), jnp.bfloat16)
    scratch = [
        pltpu.VMEM((SPAN, HEAD_WIDTH), jnp.bfloat16),
        pltpu.VMEM((SPAN, 2 * CHUNK), jnp.bfloat16),
        pltpu.VMEM((2 * CHUNK, HEAD_WIDTH), jnp.bfloat16),
    ]
    aliases = {}
    if chunk == 0:
        out_specs = [WHOLE, dq_spec]
        out_shape = [jax.ShapeDtypeStruct((SPAN, 2 * HEAD_WIDTH), jnp.float32), dq_shape]
    else:
        args += [before, dq_before]
        in_specs += [WHOLE, pl.BlockSpec(memory_space=pl.ANY)]
        aliases = {len(args) - 1: 2}
        out_specs = [WHOLE, WHOLE, dq_spec]
        out_shape = [
            jax.ShapeDtypeStruct((BEHIND, 2 * HEAD_WIDTH), jnp.bfloat16),
            jax.ShapeDtypeStruct((BS, 2 * HEAD_WIDTH), jnp.float32),
            dq_shape,
        ]
        scratch.append(pltpu.VMEM((SPAN, 2 * HEAD_WIDTH), jnp.float32))
    return pl.pallas_call(
        functools.partial(main_kernel, chunk),
        grid=(1,),
        in_specs=in_specs,
        out_specs=out_specs,
        out_shape=out_shape,
        scratch_shapes=scratch,
        input_output_aliases=aliases,
        compiler_params=pltpu.CompilerParams(vmem_limit_bytes=16 * MIB),
        cost_estimate=pl.CostEstimate(
            flops=2 * 4 * LANES * SPAN * HEAD_WIDTH + 2 * CHUNK * 4 * width * width,
            bytes_accessed=8 * MIB,
            transcendentals=0,
        ),
        name=f"main{chunk}",
    )(*args)


def close_kernel(odd_ref, mine_ref, four_ref, two_ref, back_ref, dk_ref, dv_ref):
    total = mine_ref[...] + four_ref[...].astype(jnp.float32) + two_ref[...].astype(jnp.float32)
    back = back_ref[BS:, :].astype(jnp.float32)
    total = total + jnp.where(odd_ref[0] == 1, jnp.zeros_like(back), back)
    dk_ref[...] = total[:, :HEAD_WIDTH].astype(jnp.bfloat16)
    dv_ref[...] = total[:, HEAD_WIDTH:].astype(jnp.bfloat16)


def close(odd, mine, four, two, back):
    return pl.pallas_call(
        close_kernel,
        in_specs=[pl.BlockSpec(memory_space=pltpu.SMEM)] + [WHOLE] * 4,
        out_specs=[WHOLE] * 2,
        out_shape=[jax.ShapeDtypeStruct((BS, HEAD_WIDTH), jnp.bfloat16)] * 2,
        name="close",
    )(odd, mine, four, two, back)


def body(queries, keys, values, attn_out, out_grad, out_weight, segment):
    place = lax.axis_index("hd")
    device = lax.axis_index("cp")
    odd = (device & 1) == 1
    chunks = BS // CHUNK
    half = out_grad.shape[1] // 2

    def gather_window(here):
        two = shifted(here, "cp", 2)
        four = shifted(here, "cp", 4)
        other = swapped(
            jnp.where(
                odd, jnp.concatenate([two, four], axis=0), jnp.concatenate([here, two], axis=0)
            )
        )
        return four, other, two, here

    key_blocks = gather_window(keys)
    grads = [out_grad[c * CHUNK : (c + 1) * CHUNK] for c in range(chunks)]
    near = [(shifted(g, "hd", 1), shifted(g, "hd", -1)) for g in grads]
    value_blocks = gather_window(values)
    opposite = [(shifted(a[:, :half], "hd", 1), shifted(b[:, half:], "hd", -1)) for a, b in near]

    padded = jnp.concatenate([jnp.full((BEHIND,), -1, jnp.int32), segment])
    around = lax.dynamic_slice_in_dim(padded, device * BS, WINDOW, 0)
    starts = jnp.sum((around[:, None] < around[None, BEHIND:]).astype(jnp.int32), axis=0)[None, :]

    stat = [stats(c, queries, key_blocks, starts) for c in range(chunks)]
    place = place.astype(jnp.int32)[None]
    before, dq = main(
        0, place, stat[0], key_blocks, value_blocks, (out_grad, *near[0], *opposite[0]),
        out_weight, queries, attn_out, None, None,
    )
    far, mine, dq = main(
        1, place, stat[1], key_blocks, value_blocks, (out_grad, *near[1], *opposite[1]),
        out_weight, queries, attn_out, before, dq,
    )

    back = swapped(jnp.concatenate([far[BS : 2 * BS], far[3 * BS :]], axis=0))
    back_three, back_one = back[:BS].astype(jnp.float32), back[BS:].astype(jnp.float32)
    to_four = far[:BS].astype(jnp.float32) + jnp.where(odd, back_three, 0.0)
    to_two = far[2 * BS : 3 * BS].astype(jnp.float32) + jnp.where(odd, back_one, back_three)
    from_four = shifted(to_four.astype(jnp.bfloat16), "cp", -4)
    from_two = shifted(to_two.astype(jnp.bfloat16), "cp", -2)
    dk, dv = close(odd.astype(jnp.int32)[None], mine, from_four, from_two, back)
    return dq, dk, dv


def solution(mesh):
    return jax.shard_map(
        body,
        mesh=mesh,
        in_specs=(
            P("cp", "hd"),
            P("cp", "hd"),
            P("cp", "hd"),
            P("cp", "hd"),
            P("cp", "hd"),
            P("hd", None),
            P(),
        ),
        out_specs=(P("cp", "hd"), P("cp", "hd"), P("cp", "hd")),
        check_vma=False,
    )
```

```python
import functools

import jax
import jax.numpy as jnp
from jax import lax
from jax.experimental import pallas as pl
from jax.experimental.pallas import tpu as pltpu
from jax.sharding import PartitionSpec as P

HEAD_WIDTH = 128
HEADS = 8
BS = 512
MOST_BLK = 4
BEHIND = MOST_BLK * BS
TILE = 256
CHUNK = 256
EDGE = 4
LANES = HEADS * CHUNK
WIDTH = HEADS * HEAD_WIDTH
SCALE = HEAD_WIDTH ** (-0.5)
LOG2E = 1.4426950408889634
HIDDEN = -1e30
MIB = 2**20
DOCS = 16
WHOLE = pl.BlockSpec(memory_space=pltpu.VMEM)
SCALARS = pl.BlockSpec(memory_space=pltpu.SMEM)
ANYWHERE = pl.BlockSpec(memory_space=pl.ANY)


def shifted(value, axis, by):
    length = lax.axis_size(axis)
    return lax.ppermute(value, axis, [(i, (i + by) % length) for i in range(length)])


def swapped(value):
    length = lax.axis_size("cp")
    return lax.ppermute(value, "cp", [(i, i ^ 1) for i in range(length)])


def nt(a, b):
    return lax.dot_general(a, b, (((1,), (1,)), ((), ())), preferred_element_type=jnp.float32)


def nn(a, b):
    return lax.dot_general(a, b, (((1,), (0,)), ((), ())), preferred_element_type=jnp.float32)


def tn(a, b):
    return lax.dot_general(a, b, (((0,), (0,)), ((), ())), preferred_element_type=jnp.float32)


def tiles_of(chunk, near):
    last = BEHIND // TILE + chunk
    return range(EDGE, last + 1) if near else range(chunk, EDGE)


def window_tile(refs, tile):
    far, two, one, here = refs
    block, part = divmod(tile, BS // TILE)
    ref, row = [(far, BS), (far, 0), (two, 0), (one, 0), (here, 0)][block]
    row = row + part * TILE
    return ref[row : row + TILE, :]


def head_lanes(head):
    return slice(head * CHUNK, (head + 1) * CHUNK)


def head_columns(head):
    return slice(head * HEAD_WIDTH, (head + 1) * HEAD_WIDTH)


def at_tile(index):
    return slice(index * TILE, (index + 1) * TILE)


def split_kernel(whole_ref, low_ref, high_ref, sems):
    copies = [
        pltpu.make_async_copy(whole_ref.at[pl.ds(c * CHUNK, CHUNK)], to, sems.at[c])
        for c, to in enumerate((low_ref, high_ref))
    ]
    for copy in copies:
        copy.start()
    for copy in copies:
        copy.wait()


def split(whole):
    return pl.pallas_call(
        split_kernel,
        in_specs=[ANYWHERE],
        out_specs=[WHOLE] * 2,
        out_shape=[jax.ShapeDtypeStruct((CHUNK, WIDTH), jnp.bfloat16)] * 2,
        scratch_shapes=[pltpu.SemaphoreType.DMA((2,))],
        compiler_params=pltpu.CompilerParams(vmem_limit_bytes=4 * MIB),
        name="split",
    )(whole)


def stats_kernel(chunk, near, where_ref, segment_ref, q_ref, *refs):
    if near:
        keys = (None, *refs[:3])
        refs = refs[3:]
    else:
        keys = (refs[0], None, None, None)
        top_ref, total_ref = refs[1:3]
        refs = refs[3:]
    e_ref, out_a, out_b, even, odd = refs
    held = (even, odd)
    rows = slice(chunk * CHUNK, (chunk + 1) * CHUNK)
    factor = SCALE * LOG2E
    tiles = tiles_of(chunk, near)

    first = where_ref[0] * BS - BEHIND
    row = lax.broadcasted_iota(jnp.int32, (1, CHUNK), 1) + (BEHIND + chunk * CHUNK)
    start = jnp.zeros((1, CHUNK), jnp.int32) - first
    segments = segment_ref[...]
    for doc in range(1, DOCS):
        begin = jnp.sum((segments < doc).astype(jnp.int32), axis=(0, 1), keepdims=True) - first
        start = jnp.where(begin <= row, begin, start)

    def score(head, tile, top):
        s = nt(window_tile(keys, tile), q_ref[rows, head_columns(head)])
        key = lax.broadcasted_iota(jnp.int32, (TILE, CHUNK), 0)
        seen = key >= start - tile * TILE
        if near and tile == tiles[-1]:
            seen = seen & (key <= lax.broadcasted_iota(jnp.int32, (TILE, CHUNK), 1))
        s = jnp.where(seen, s, HIDDEN)
        held[head % 2][at_tile(tile - tiles[0]), :] = s
        most = jnp.max(s.reshape(TILE // 8, 8, CHUNK), axis=0)
        return most if top is None else jnp.maximum(top, most)

    def weigh(head, tile, top, total):
        at = at_tile(tile - tiles[0])
        e = jnp.exp2(held[head % 2][at, :] * factor - top)
        e_ref[at, head_lanes(head)] = e.astype(jnp.bfloat16)
        part = jnp.sum(e.reshape(TILE // 8, 8, CHUNK), axis=0)
        return part if total is None else total + part

    following = None
    for tile in tiles:
        following = score(0, tile, following)
    for head in range(HEADS):
        top = jnp.max(following, axis=0, keepdims=True) * factor
        following = total = None
        for tile in tiles:
            if head + 1 < HEADS:
                following = score(head + 1, tile, following)
            total = weigh(head, tile, top, total)
        total = jnp.sum(total, axis=0, keepdims=True)
        lanes = head_lanes(head)
        if near:
            out_a[:, lanes] = jnp.broadcast_to(top, (8, CHUNK))
            out_b[:, lanes] = jnp.broadcast_to(total, (8, CHUNK))
        else:
            other_top, other_total = top_ref[:1, lanes], total_ref[:1, lanes]
            highest = jnp.maximum(top, other_top)
            near_part, far_part = jnp.exp2(other_top - highest), jnp.exp2(top - highest)
            inverse = 1.0 / (near_part * other_total + far_part * total)
            out_a[:, lanes] = jnp.broadcast_to(near_part * inverse, (8, CHUNK))
            out_b[:, lanes] = jnp.broadcast_to(far_part * inverse, (8, CHUNK))


def stats(chunk, near, where, segments, queries, keys, known=()):
    span = len(tiles_of(chunk, near)) * TILE
    args = [where, segments, queries, *keys, *known]
    return pl.pallas_call(
        functools.partial(stats_kernel, chunk, near),
        in_specs=[SCALARS] + [WHOLE] * (len(args) - 1),
        out_specs=[WHOLE] * 3,
        out_shape=[
            jax.ShapeDtypeStruct((span, LANES), jnp.bfloat16),
            jax.ShapeDtypeStruct((8, LANES), jnp.float32),
            jax.ShapeDtypeStruct((8, LANES), jnp.float32),
        ],
        scratch_shapes=[pltpu.VMEM((span, CHUNK), jnp.float32)] * 2,
        compiler_params=pltpu.CompilerParams(vmem_limit_bytes=10 * MIB),
        cost_estimate=pl.CostEstimate(
            flops=2 * LANES * span * HEAD_WIDTH,
            bytes_accessed=4 * MIB,
            transcendentals=LANES * span,
        ),
        name=f"stats{chunk}{'near' if near else 'far'}",
    )(*args)


def main_kernel(chunk, part, names, *refs):
    r = dict(zip(names, refs, strict=True))
    rows = slice(chunk * CHUNK, (chunk + 1) * CHUNK)
    near_tiles = list(tiles_of(chunk, True)) if part != "far" else []
    far_tiles = list(tiles_of(chunk, False)) if part != "near" else []
    tiles = far_tiles + near_tiles
    keys = tuple(r.get("k_" + n) for n in ("far", "two", "one", "here"))
    values = tuple(r.get("v_" + n) for n in ("far", "two", "one", "here"))

    for index, tile in enumerate(tiles):
        r["k_scr"][at_tile(index), :] = window_tile(keys, tile)

    if part != "near":
        place = r["where"][1]
        for ref, at, by in (
            (r["own"], rows, 0),
            (r["prev"], slice(None), 3),
            (r["next"], slice(None), 1),
            (r["opposite"], slice(None), 2),
        ):
            to = pl.ds(pl.multiple_of(lax.rem(place + by, 4) * WIDTH, WIDTH), WIDTH)
            r["g_scr"][:, to] = ref[at, :]

    for pair in range(HEADS // 2):
        cols = slice(2 * pair * HEAD_WIDTH, 2 * (pair + 1) * HEAD_WIDTH)
        lanes = slice(2 * pair * CHUNK, 2 * (pair + 1) * CHUNK)
        if part != "near":
            acc = nt(r["g_scr"][...], r["weight"][cols, :])
            dout = acc.astype(jnp.bfloat16).astype(jnp.float32)
            product = jnp.transpose(dout * r["attn"][rows, cols].astype(jnp.float32))
        for side in range(2):
            head = 2 * pair + side
            here = head_lanes(side)
            sides = {}
            if part != "near":
                delta = jnp.sum(product[head_columns(side), :], axis=0, keepdims=True)
                for group in ("near", "far"):
                    inv = r["inv_" + group][:1, head_lanes(head)]
                    down = jnp.transpose(jnp.broadcast_to(inv, (HEAD_WIDTH, CHUNK)))
                    scaled = (dout[:, head_columns(side)] * down).astype(jnp.bfloat16)
                    sides[group] = (scaled, delta * inv)
                    if part == "far" and group == "near":
                        r["dout_near"][head_lanes(head), :] = scaled
                        r["delta_near"][:, head_lanes(head)] = jnp.broadcast_to(
                            delta * inv, (8, CHUNK)
                        )
                    else:
                        r["dout_scr_" + group][here, :] = scaled
            else:
                sides["near"] = (
                    r["dout_near"][head_lanes(head), :],
                    r["delta_near"][:1, head_lanes(head)],
                )
            for index, tile in enumerate(tiles):
                group = "far" if tile < EDGE else "near"
                scaled, delta = sides[group]
                e_at = at_tile(tile - (chunk if tile < EDGE else EDGE))
                dp = nt(window_tile(values, tile), scaled)
                prob = r["e_" + group][e_at, head_lanes(head)].astype(jnp.float32)
                r["ds_scr"][at_tile(index), here] = (prob * (dp - delta)).astype(jnp.bfloat16)
            dq = tn(r["k_scr"][...], r["ds_scr"][:, here])
            if part == "far":
                r["dq_part"][:, head_lanes(head)] = dq
            else:
                if part == "near":
                    dq = dq + r["dq_part"][:, head_lanes(head)]
                r["dq"][:, head_columns(head)] = (jnp.transpose(dq) * SCALE).astype(jnp.bfloat16)
        queries = jnp.concatenate(
            [r["queries"][rows, head_columns(2 * pair + side)] for side in range(2)], axis=0
        )
        for index, tile in enumerate(tiles):
            group = "far" if tile < EDGE else "near"
            e_at = at_tile(tile - (chunk if tile < EDGE else EDGE))
            if part == "near":
                scaled = r["dout_near"][lanes, :]
            else:
                scaled = r["dout_scr_" + group][...]
            both = jnp.concatenate(
                [
                    nn(r["ds_scr"][at_tile(index), :], queries) * SCALE,
                    nn(r["e_" + group][e_at, lanes], scaled),
                ],
                axis=1,
            )
            if pair > 0:
                both = both + r["sum"][at_tile(index), :]
            elif chunk == 1 and tile <= BEHIND // TILE:
                both = both + r["before"][at_tile(tile), :]
            if chunk == 0 or pair < HEADS // 2 - 1:
                r["sum"][at_tile(index), :] = both
                continue
            block, side = divmod(tile, BS // TILE)
            out = r[("out_four", "out_three", "out_two", "out_one", "mine")[block]]
            out[at_tile(side), :] = both.astype(out.dtype)
    if chunk == 1 and part == "far":
        r["out_four"][at_tile(0), :] = r["before"][at_tile(0), :].astype(jnp.bfloat16)


def main(chunk, part, given, before=None, dq_before=None):
    tiles = 0
    names, specs = [], []

    def need(name, spec=WHOLE):
        names.append(name)
        specs.append(spec)

    far, near = part != "near", part != "far"
    if far:
        need("where", SCALARS)
        for name in ("own", "prev", "next", "opposite", "weight", "attn"):
            need(name)
        for name in ("inv_near", "inv_far", "e_far", "k_far", "v_far"):
            need(name)
        tiles += len(tiles_of(chunk, False))
    if near:
        for name in ("e_near", "k_two", "k_one", "k_here", "v_two", "v_one", "v_here"):
            need(name)
        tiles += len(tiles_of(chunk, True))
    need("queries")
    if part == "near":
        for name in ("dout_near", "delta_near", "dq_part"):
            need(name)
    if chunk == 1:
        need("before")
        given = {**given, "before": before}
    aliases = {}
    if chunk == 1 and near:
        need("dq_before", ANYWHERE)
        given = {**given, "dq_before": dq_before}
        aliases = {len(names) - 1: 0}
    args = [given[name] for name in names]

    outs = {}
    dq_spec = pl.BlockSpec((CHUNK, WIDTH), lambda i: (chunk, 0))
    block = jax.ShapeDtypeStruct((BS, 2 * HEAD_WIDTH), jnp.bfloat16)
    if near:
        outs["dq"] = (dq_spec, jax.ShapeDtypeStruct((BS, WIDTH), jnp.bfloat16))
    if chunk == 0:
        shape = jax.ShapeDtypeStruct((tiles * TILE, 2 * HEAD_WIDTH), jnp.float32)
        outs["sum"] = (WHOLE, shape)
    else:
        if far:
            outs["out_four"] = outs["out_three"] = (WHOLE, block)
        if near:
            outs["out_two"] = outs["out_one"] = (WHOLE, block)
            outs["mine"] = (WHOLE, jax.ShapeDtypeStruct(block.shape, jnp.float32))
    if part == "far":
        outs["dout_near"] = (WHOLE, jax.ShapeDtypeStruct((LANES, HEAD_WIDTH), jnp.bfloat16))
        outs["delta_near"] = (WHOLE, jax.ShapeDtypeStruct((8, LANES), jnp.float32))
        outs["dq_part"] = (WHOLE, jax.ShapeDtypeStruct((HEAD_WIDTH, LANES), jnp.float32))
    scratch = {
        "k_scr": pltpu.VMEM((tiles * TILE, HEAD_WIDTH), jnp.bfloat16),
        "ds_scr": pltpu.VMEM((tiles * TILE, 2 * CHUNK), jnp.bfloat16),
    }
    if far:
        scratch["g_scr"] = pltpu.VMEM((CHUNK, 4 * WIDTH), jnp.bfloat16)
        scratch["dout_scr_far"] = pltpu.VMEM((2 * CHUNK, HEAD_WIDTH), jnp.bfloat16)
        if near:
            scratch["dout_scr_near"] = pltpu.VMEM((2 * CHUNK, HEAD_WIDTH), jnp.bfloat16)
    if chunk == 1:
        scratch["sum"] = pltpu.VMEM((tiles * TILE, 2 * HEAD_WIDTH), jnp.float32)
    flops = 2 * 4 * LANES * tiles * TILE * HEAD_WIDTH
    if far:
        flops += 2 * CHUNK * 4 * WIDTH * WIDTH
    results = pl.pallas_call(
        functools.partial(main_kernel, chunk, part, names + list(outs) + list(scratch)),
        grid=(1,),
        in_specs=specs,
        out_specs=[spec for spec, _ in outs.values()],
        out_shape=[shape for _, shape in outs.values()],
        scratch_shapes=list(scratch.values()),
        input_output_aliases=aliases,
        compiler_params=pltpu.CompilerParams(vmem_limit_bytes=14 * MIB),
        cost_estimate=pl.CostEstimate(
            flops=flops, bytes_accessed=8 * MIB, transcendentals=0
        ),
        name=f"main{chunk}{part}",
    )(*args)
    return dict(zip(outs, results, strict=True))


def close_kernel(mine_ref, four_ref, two_ref, one_ref, dk_ref, dv_ref):
    total = mine_ref[...] + four_ref[...].astype(jnp.float32)
    total = total + two_ref[...].astype(jnp.float32) + one_ref[...].astype(jnp.float32)
    dk_ref[...] = total[:, :HEAD_WIDTH].astype(jnp.bfloat16)
    dv_ref[...] = total[:, HEAD_WIDTH:].astype(jnp.bfloat16)


def close(mine, four, two, one):
    return pl.pallas_call(
        close_kernel,
        in_specs=[WHOLE] * 4,
        out_specs=[WHOLE] * 2,
        out_shape=[jax.ShapeDtypeStruct((BS, HEAD_WIDTH), jnp.bfloat16)] * 2,
        compiler_params=pltpu.CompilerParams(vmem_limit_bytes=6 * MIB),
        name="close",
    )(mine, four, two, one)


def body(queries, keys, values, attn_out, out_grad, out_weight, segment):
    device = lax.axis_index("cp")
    odd = (device & 1) == 1
    where = jnp.stack([device, lax.axis_index("hd")]).astype(jnp.int32)
    segments = segment.reshape(128, -1)

    key_one, key_two = shifted(keys, "cp", 1), shifted(keys, "cp", 2)
    low, high = split(out_grad)
    prev_low, next_low = shifted(low, "hd", 1), shifted(low, "hd", -1)
    prev_high, next_high = shifted(high, "hd", 1), shifted(high, "hd", -1)
    key_far = shifted(jnp.concatenate([key_one, key_two], axis=0), "cp", 2)
    far_low, far_high = shifted(prev_low, "hd", 1), shifted(next_high, "hd", -1)
    value_one, value_two = shifted(values, "cp", 1), shifted(values, "cp", 2)
    value_far = shifted(jnp.concatenate([value_one, value_two], axis=0), "cp", 2)

    given = {
        "where": where, "weight": out_weight, "attn": attn_out, "own": out_grad,
        "queries": queries, "k_far": key_far, "k_two": key_two, "k_one": key_one,
        "k_here": keys, "v_far": value_far, "v_two": value_two, "v_one": value_one,
        "v_here": values,
    }
    near = [
        stats(c, True, where, segments, queries, (key_two, key_one, keys)) for c in range(2)
    ]
    stat = []
    for c in range(2):
        e_near, top, total = near[c]
        e_far, inv_near, inv_far = stats(
            c, False, where, segments, queries, (key_far,), (top, total)
        )
        stat.append({"e_near": e_near, "e_far": e_far, "inv_near": inv_near, "inv_far": inv_far})

    first = main(
        0, "all",
        {**given, **stat[0], "prev": prev_low, "next": next_low, "opposite": far_low},
    )
    given = {**given, **stat[1], "prev": prev_high, "next": next_high, "opposite": far_high}
    early = main(1, "far", given, first["sum"])
    back = swapped(early["out_three"]).astype(jnp.float32)
    to_four = (early["out_four"].astype(jnp.float32) + jnp.where(odd, back, 0.0)).astype(
        jnp.bfloat16
    )
    from_four = shifted(to_four, "cp", -4)
    late = main(1, "near", {**given, **early}, first["sum"], first["dq"])
    from_one = shifted(late["out_one"], "cp", -1)
    to_two = (late["out_two"].astype(jnp.float32) + jnp.where(odd, 0.0, back)).astype(
        jnp.bfloat16
    )
    from_two = shifted(to_two, "cp", -2)
    dk, dv = close(late["mine"], from_four, from_two, from_one)
    return late["dq"], dk, dv


def solution(mesh):
    return jax.shard_map(
        body,
        mesh=mesh,
        in_specs=(
            P("cp", "hd"),
            P("cp", "hd"),
            P("cp", "hd"),
            P("cp", "hd"),
            P("cp", "hd"),
            P("hd", None),
            P(),
        ),
        out_specs=(P("cp", "hd"), P("cp", "hd"), P("cp", "hd")),
        check_vma=False,
    )
```

```python
import functools

import jax
import jax.numpy as jnp
from jax import lax
from jax.experimental import pallas as pl
from jax.experimental.pallas import tpu as pltpu
from jax.sharding import PartitionSpec as P

HEAD_WIDTH = 128
HEADS = 8
BS = 512
MOST_BLK = 4
BEHIND = MOST_BLK * BS
TILE = 256
CHUNK = 256
EDGE = 4
LANES = HEADS * CHUNK
WIDTH = HEADS * HEAD_WIDTH
SCALE = HEAD_WIDTH ** (-0.5)
LOG2E = 1.4426950408889634
HIDDEN = -1e30
MIB = 2**20
DOCS = 16
WHOLE = pl.BlockSpec(memory_space=pltpu.VMEM)
SCALARS = pl.BlockSpec(memory_space=pltpu.SMEM)
IN_HBM = pl.BlockSpec(memory_space=pltpu.HBM)


def shifted(value, axis, by):
    length = lax.axis_size(axis)
    return lax.ppermute(value, axis, [(i, (i + by) % length) for i in range(length)])


def swapped(value):
    length = lax.axis_size("cp")
    return lax.ppermute(value, "cp", [(i, i ^ 1) for i in range(length)])


def in_hbm(value):
    return pltpu.with_memory_space_constraint(value, pltpu.HBM)


def nt(a, b):
    return lax.dot_general(a, b, (((1,), (1,)), ((), ())), preferred_element_type=jnp.float32)


def nn(a, b):
    return lax.dot_general(a, b, (((1,), (0,)), ((), ())), preferred_element_type=jnp.float32)


def tn(a, b):
    return lax.dot_general(a, b, (((0,), (0,)), ((), ())), preferred_element_type=jnp.float32)


def tiles_of(chunk, near):
    last = BEHIND // TILE + chunk
    return range(EDGE, last + 1) if near else range(chunk, EDGE)


def window_tile(refs, tile):
    far, two, one, here = refs
    block, part = divmod(tile, BS // TILE)
    ref, row = [(far, BS), (far, 0), (two, 0), (one, 0), (here, 0)][block]
    row = row + part * TILE
    return ref[row : row + TILE, :]


def head_lanes(head):
    return slice(head * CHUNK, (head + 1) * CHUNK)


def head_columns(head):
    return slice(head * HEAD_WIDTH, (head + 1) * HEAD_WIDTH)


def at_tile(index):
    return slice(index * TILE, (index + 1) * TILE)


def fetch_kernel(*refs):
    count = (len(refs) - 1) // 2
    sources, targets, sems = refs[:count], refs[count:-1], refs[-1]
    low, high = targets[-2:]
    halves = [sources[-1].at[pl.ds(c * CHUNK, CHUNK)] for c in range(2)]
    moves = [*zip(halves, (low, high)), *zip(sources[:-1], targets[:-2], strict=True)]
    copies = [pltpu.make_async_copy(a, b, sems.at[i]) for i, (a, b) in enumerate(moves)]
    for copy in copies:
        copy.start()
    for copy in copies:
        copy.wait()


def fetch(*arrays):
    shapes = [jax.ShapeDtypeStruct(x.shape, x.dtype) for x in arrays[:-1]]
    last = arrays[-1]
    shapes += [jax.ShapeDtypeStruct((CHUNK, WIDTH), last.dtype)] * 2
    return pl.pallas_call(
        fetch_kernel,
        in_specs=[IN_HBM] * len(arrays),
        out_specs=[WHOLE] * len(shapes),
        out_shape=shapes,
        scratch_shapes=[pltpu.SemaphoreType.DMA((len(shapes),))],
        compiler_params=pltpu.CompilerParams(vmem_limit_bytes=6 * MIB),
        name="fetch",
    )(*(in_hbm(x) for x in arrays))


def stats_kernel(chunk, near, where_ref, segment_ref, q_ref, *refs):
    if near:
        keys = (None, *refs[:3])
        refs = refs[3:]
    else:
        keys = (refs[0], None, None, None)
        top_ref, total_ref = refs[1:3]
        refs = refs[3:]
    e_ref, out_a, out_b, even, odd = refs
    held = (even, odd)
    rows = slice(chunk * CHUNK, (chunk + 1) * CHUNK)
    factor = SCALE * LOG2E
    tiles = tiles_of(chunk, near)

    first = where_ref[0] * BS - BEHIND
    row = lax.broadcasted_iota(jnp.int32, (1, CHUNK), 1) + (BEHIND + chunk * CHUNK)
    start = jnp.zeros((1, CHUNK), jnp.int32) - first
    segments = segment_ref[...]
    for doc in range(1, DOCS):
        begin = jnp.sum((segments < doc).astype(jnp.int32), axis=(0, 1), keepdims=True) - first
        start = jnp.where(begin <= row, begin, start)

    def score(head, tile, top):
        s = nt(window_tile(keys, tile), q_ref[rows, head_columns(head)])
        key = lax.broadcasted_iota(jnp.int32, (TILE, CHUNK), 0)
        seen = key >= start - tile * TILE
        if near and tile == tiles[-1]:
            seen = seen & (key <= lax.broadcasted_iota(jnp.int32, (TILE, CHUNK), 1))
        s = jnp.where(seen, s, HIDDEN)
        held[head % 2][at_tile(tile - tiles[0]), :] = s
        most = jnp.max(s.reshape(TILE // 8, 8, CHUNK), axis=0)
        return most if top is None else jnp.maximum(top, most)

    def weigh(head, tile, top, total):
        at = at_tile(tile - tiles[0])
        e = jnp.exp2(held[head % 2][at, :] * factor - top)
        e_ref[at, head_lanes(head)] = e.astype(jnp.bfloat16)
        part = jnp.sum(e.reshape(TILE // 8, 8, CHUNK), axis=0)
        return part if total is None else total + part

    following = None
    for tile in tiles:
        following = score(0, tile, following)
    for head in range(HEADS):
        top = jnp.max(following, axis=0, keepdims=True) * factor
        following = total = None
        for tile in tiles:
            if head + 1 < HEADS:
                following = score(head + 1, tile, following)
            total = weigh(head, tile, top, total)
        total = jnp.sum(total, axis=0, keepdims=True)
        lanes = head_lanes(head)
        if near:
            out_a[:, lanes] = jnp.broadcast_to(top, (8, CHUNK))
            out_b[:, lanes] = jnp.broadcast_to(total, (8, CHUNK))
        else:
            other_top, other_total = top_ref[:1, lanes], total_ref[:1, lanes]
            highest = jnp.maximum(top, other_top)
            near_part, far_part = jnp.exp2(other_top - highest), jnp.exp2(top - highest)
            inverse = 1.0 / (near_part * other_total + far_part * total)
            out_a[:, lanes] = jnp.broadcast_to(near_part * inverse, (8, CHUNK))
            out_b[:, lanes] = jnp.broadcast_to(far_part * inverse, (8, CHUNK))


def stats(chunk, near, where, segments, queries, keys, known=()):
    span = len(tiles_of(chunk, near)) * TILE
    args = [where, segments, queries, *keys, *known]
    return pl.pallas_call(
        functools.partial(stats_kernel, chunk, near),
        in_specs=[SCALARS] + [WHOLE] * (len(args) - 1),
        out_specs=[WHOLE] * 3,
        out_shape=[
            jax.ShapeDtypeStruct((span, LANES), jnp.bfloat16),
            jax.ShapeDtypeStruct((8, LANES), jnp.float32),
            jax.ShapeDtypeStruct((8, LANES), jnp.float32),
        ],
        scratch_shapes=[pltpu.VMEM((span, CHUNK), jnp.float32)] * 2,
        compiler_params=pltpu.CompilerParams(vmem_limit_bytes=6 * MIB),
        cost_estimate=pl.CostEstimate(
            flops=2 * LANES * span * HEAD_WIDTH,
            bytes_accessed=4 * MIB,
            transcendentals=LANES * span,
        ),
        name=f"stats{chunk}{'near' if near else 'far'}",
    )(*args)


def main_kernel(chunk, part, names, *refs):
    r = dict(zip(names, refs, strict=True))
    rows = slice(chunk * CHUNK, (chunk + 1) * CHUNK)
    near_tiles = list(tiles_of(chunk, True)) if part != "far" else []
    far_tiles = list(tiles_of(chunk, False)) if part != "near" else []
    tiles = far_tiles + near_tiles
    values = tuple(r.get("v_" + n) for n in ("far", "two", "one", "here"))

    if part != "near":
        copies = []
        for pair in range(HEADS // 2):
            band = pl.ds(2 * pair * HEAD_WIDTH, 2 * HEAD_WIDTH)
            copies.append(
                pltpu.make_async_copy(
                    r["weight"].at[band], r["w_scr"].at[pair % 2], r["w_sems"].at[pair]
                )
            )
        copies[0].start()
        copies[1].start()
        place = r["where"][1]
        for name, by in (("own", 0), ("prev", 3), ("next", 1), ("opposite", 2)):
            to = pl.ds(pl.multiple_of(lax.rem(place + by, 4) * WIDTH, WIDTH), WIDTH)
            r["g_scr"][:, to] = r[name][...]

    for pair in range(HEADS // 2):
        cols = slice(2 * pair * HEAD_WIDTH, 2 * (pair + 1) * HEAD_WIDTH)
        lanes = slice(2 * pair * CHUNK, 2 * (pair + 1) * CHUNK)
        if part != "near":
            copies[pair].wait()
            acc = nt(r["g_scr"][...], r["w_scr"][pair % 2])
            if pair + 2 < len(copies):
                copies[pair + 2].start()
            dout = acc.astype(jnp.bfloat16).astype(jnp.float32)
            product = jnp.transpose(dout * r["attn"][rows, cols].astype(jnp.float32))
        for side in range(2):
            head = 2 * pair + side
            here = head_lanes(side)
            sides = {}
            if part != "near":
                delta = jnp.sum(product[head_columns(side), :], axis=0, keepdims=True)
                for group in ("near", "far"):
                    inv = r["inv_" + group][:1, head_lanes(head)]
                    down = jnp.transpose(jnp.broadcast_to(inv, (HEAD_WIDTH, CHUNK)))
                    scaled = (dout[:, head_columns(side)] * down).astype(jnp.bfloat16)
                    sides[group] = (scaled, delta * inv)
                    if part == "far" and group == "near":
                        r["dout_near"][head_lanes(head), :] = scaled
                        r["delta_near"][:, head_lanes(head)] = jnp.broadcast_to(
                            delta * inv, (8, CHUNK)
                        )
                    else:
                        r["dout_scr_" + group][here, :] = scaled
            else:
                sides["near"] = (
                    r["dout_near"][head_lanes(head), :],
                    r["delta_near"][:1, head_lanes(head)],
                )
            for index, tile in enumerate(tiles):
                group = "far" if tile < EDGE else "near"
                scaled, delta = sides[group]
                e_at = at_tile(tile - (chunk if tile < EDGE else EDGE))
                dp = nt(window_tile(values, tile), scaled)
                prob = r["e_" + group][e_at, head_lanes(head)].astype(jnp.float32)
                r["ds"][at_tile(index), head_lanes(head)] = (prob * (dp - delta)).astype(
                    jnp.bfloat16
                )
        queries = jnp.concatenate(
            [r["queries"][rows, head_columns(2 * pair + side)] for side in range(2)], axis=0
        )
        for index, tile in enumerate(tiles):
            group = "far" if tile < EDGE else "near"
            e_at = at_tile(tile - (chunk if tile < EDGE else EDGE))
            if part == "near":
                scaled = r["dout_near"][lanes, :]
            else:
                scaled = r["dout_scr_" + group][...]
            both = jnp.concatenate(
                [
                    nn(r["ds"][at_tile(index), lanes], queries) * SCALE,
                    nn(r["e_" + group][e_at, lanes], scaled),
                ],
                axis=1,
            )
            if pair > 0:
                both = both + r["sum"][at_tile(index), :]
            elif chunk == 1 and tile <= BEHIND // TILE:
                both = both + r["before"][at_tile(tile), :]
            if chunk == 0 or pair < HEADS // 2 - 1:
                r["sum"][at_tile(index), :] = both
                continue
            block, side = divmod(tile, BS // TILE)
            out = r[("out_four", "out_three", "out_two", "out_one", "mine")[block]]
            out[at_tile(side), :] = both.astype(out.dtype)
    if chunk == 1 and part == "far":
        r["out_four"][at_tile(0), :] = r["before"][at_tile(0), :].astype(jnp.bfloat16)


def main(chunk, part, given, before=None):
    tiles = 0
    names, specs = [], []

    def need(name, spec=WHOLE):
        names.append(name)
        specs.append(spec)

    far, near = part != "near", part != "far"
    if far:
        need("where", SCALARS)
        need("weight", IN_HBM)
        for name in ("own", "prev", "next", "opposite", "attn"):
            need(name)
        for name in ("inv_near", "inv_far", "e_far", "v_far"):
            need(name)
        tiles += len(tiles_of(chunk, False))
    if near:
        for name in ("e_near", "v_two", "v_one", "v_here"):
            need(name)
        tiles += len(tiles_of(chunk, True))
    need("queries")
    if part == "near":
        for name in ("dout_near", "delta_near"):
            need(name)
    if chunk == 1:
        need("before")
        given = {**given, "before": before}
    args = [in_hbm(given[name]) if name == "weight" else given[name] for name in names]

    outs = {"ds": (WHOLE, jax.ShapeDtypeStruct((tiles * TILE, LANES), jnp.bfloat16))}
    block = jax.ShapeDtypeStruct((BS, 2 * HEAD_WIDTH), jnp.bfloat16)
    if chunk == 0:
        shape = jax.ShapeDtypeStruct((tiles * TILE, 2 * HEAD_WIDTH), jnp.float32)
        outs["sum"] = (WHOLE, shape)
    else:
        if far:
            outs["out_four"] = outs["out_three"] = (WHOLE, block)
        if near:
            outs["out_two"] = outs["out_one"] = (WHOLE, block)
            outs["mine"] = (WHOLE, jax.ShapeDtypeStruct(block.shape, jnp.float32))
    if part == "far":
        outs["dout_near"] = (WHOLE, jax.ShapeDtypeStruct((LANES, HEAD_WIDTH), jnp.bfloat16))
        outs["delta_near"] = (WHOLE, jax.ShapeDtypeStruct((8, LANES), jnp.float32))
    scratch = {}
    if far:
        scratch["w_scr"] = pltpu.VMEM((2, 2 * HEAD_WIDTH, 4 * WIDTH), jnp.bfloat16)
        scratch["w_sems"] = pltpu.SemaphoreType.DMA((HEADS // 2,))
        scratch["g_scr"] = pltpu.VMEM((CHUNK, 4 * WIDTH), jnp.bfloat16)
        scratch["dout_scr_far"] = pltpu.VMEM((2 * CHUNK, HEAD_WIDTH), jnp.bfloat16)
        if near:
            scratch["dout_scr_near"] = pltpu.VMEM((2 * CHUNK, HEAD_WIDTH), jnp.bfloat16)
    if chunk == 1:
        scratch["sum"] = pltpu.VMEM((tiles * TILE, 2 * HEAD_WIDTH), jnp.float32)
    flops = 2 * 3 * LANES * tiles * TILE * HEAD_WIDTH
    if far:
        flops += 2 * CHUNK * 4 * WIDTH * WIDTH
    results = pl.pallas_call(
        functools.partial(main_kernel, chunk, part, names + list(outs) + list(scratch)),
        in_specs=specs,
        out_specs=[spec for spec, _ in outs.values()],
        out_shape=[shape for _, shape in outs.values()],
        scratch_shapes=list(scratch.values()),
        compiler_params=pltpu.CompilerParams(vmem_limit_bytes=(13 if far else 6) * MIB),
        cost_estimate=pl.CostEstimate(
            flops=flops, bytes_accessed=8 * MIB, transcendentals=0
        ),
        name=f"main{chunk}{part}",
    )(*args)
    return dict(zip(outs, results, strict=True))


def query_kernel(far_ref, two_ref, one_ref, here_ref, ds_zero, ds_far, ds_near, out_ref, k_scr):
    keys = (far_ref, two_ref, one_ref, here_ref)
    window = (BEHIND + BS) // TILE
    for tile in range(window):
        k_scr[at_tile(tile), :] = window_tile(keys, tile)
    edge, end = EDGE * TILE, window * TILE
    for chunk in range(2):
        rows = slice(chunk * CHUNK, (chunk + 1) * CHUNK)
        for head in range(HEADS):
            lanes = head_lanes(head)
            if chunk == 0:
                grad = tn(k_scr[: end - TILE, :], ds_zero[:, lanes])
            else:
                grad = tn(k_scr[TILE:edge, :], ds_far[:, lanes])
                grad = grad + tn(k_scr[edge:, :], ds_near[:, lanes])
            out_ref[rows, head_columns(head)] = (jnp.transpose(grad) * SCALE).astype(jnp.bfloat16)


def query_grad(keys, ds):
    return pl.pallas_call(
        query_kernel,
        in_specs=[WHOLE] * (len(keys) + len(ds)),
        out_specs=WHOLE,
        out_shape=jax.ShapeDtypeStruct((BS, WIDTH), jnp.bfloat16),
        scratch_shapes=[pltpu.VMEM((BEHIND + BS, HEAD_WIDTH), jnp.bfloat16)],
        compiler_params=pltpu.CompilerParams(vmem_limit_bytes=6 * MIB),
        cost_estimate=pl.CostEstimate(
            flops=4 * LANES * 9 * TILE * HEAD_WIDTH, bytes_accessed=MIB, transcendentals=0
        ),
        name="query_grad",
    )(*keys, *ds)


def close_kernel(mine_ref, four_ref, two_ref, one_ref, dk_ref, dv_ref):
    total = mine_ref[...] + four_ref[...].astype(jnp.float32)
    total = total + two_ref[...].astype(jnp.float32) + one_ref[...].astype(jnp.float32)
    dk_ref[...] = total[:, :HEAD_WIDTH].astype(jnp.bfloat16)
    dv_ref[...] = total[:, HEAD_WIDTH:].astype(jnp.bfloat16)


def close(mine, four, two, one):
    return pl.pallas_call(
        close_kernel,
        in_specs=[WHOLE] * 4,
        out_specs=[WHOLE] * 2,
        out_shape=[jax.ShapeDtypeStruct((BS, HEAD_WIDTH), jnp.bfloat16)] * 2,
        compiler_params=pltpu.CompilerParams(vmem_limit_bytes=6 * MIB),
        name="close",
    )(mine, four, two, one)


def body(queries, keys, values, attn_out, out_grad, out_weight, segment):
    device = lax.axis_index("cp")
    odd = (device & 1) == 1
    where = jnp.stack([device, lax.axis_index("hd")]).astype(jnp.int32)
    segments = segment.reshape(128, -1)

    key_one, key_two = shifted(keys, "cp", 1), shifted(keys, "cp", 2)
    queries, attn_out, key_here, value_here, segments, low, high = fetch(
        queries, attn_out, keys, values, segments, out_grad
    )
    prev_low, next_low = shifted(low, "hd", 1), shifted(low, "hd", -1)
    key_far = shifted(jnp.concatenate([key_one, key_two], axis=0), "cp", 2)
    key_near = (key_two, key_one, key_here)

    near_zero = stats(0, True, where, segments, queries, key_near)
    prev_low, high_later, values, near_zero = lax.optimization_barrier(
        (prev_low, high, values, near_zero)
    )
    far_low = shifted(prev_low, "hd", 1)
    prev_high, next_high = shifted(high_later, "hd", 1), shifted(high_later, "hd", -1)
    value_one, value_two = shifted(values, "cp", 1), shifted(values, "cp", 2)

    near_one = stats(1, True, where, segments, queries, key_near)
    value_one, value_two, near_one = lax.optimization_barrier((value_one, value_two, near_one))
    value_far = shifted(jnp.concatenate([value_one, value_two], axis=0), "cp", 2)
    stat = []
    for c, (e_near, top, total) in enumerate((near_zero, near_one)):
        e_far, inv_near, inv_far = stats(
            c, False, where, segments, queries, (key_far,), (top, total)
        )
        stat.append({"e_near": e_near, "e_far": e_far, "inv_near": inv_near, "inv_far": inv_far})
    next_high, stat = lax.optimization_barrier((next_high, stat))
    far_high = shifted(next_high, "hd", -1)

    given = {
        "where": where, "weight": out_weight, "attn": attn_out, "queries": queries,
        "v_far": value_far, "v_two": value_two, "v_one": value_one, "v_here": value_here,
    }
    first = main(
        0, "all",
        {**given, **stat[0], "own": low, "prev": prev_low, "next": next_low, "opposite": far_low},
    )
    given = {
        **given, **stat[1],
        "own": high, "prev": prev_high, "next": next_high, "opposite": far_high,
    }
    early = main(1, "far", given, first["sum"])
    back = swapped(early["out_three"]).astype(jnp.float32)
    to_four = (early["out_four"].astype(jnp.float32) + jnp.where(odd, back, 0.0)).astype(
        jnp.bfloat16
    )
    to_four, early["dout_near"] = lax.optimization_barrier((to_four, early["dout_near"]))
    from_four = shifted(to_four, "cp", -4)
    late = main(1, "near", {**given, **early}, first["sum"])
    to_one = late["out_one"]
    to_two = (late["out_two"].astype(jnp.float32) + jnp.where(odd, 0.0, back)).astype(
        jnp.bfloat16
    )
    to_one, to_two, ds_near = lax.optimization_barrier((to_one, to_two, late["ds"]))
    from_one, from_two = shifted(to_one, "cp", -1), shifted(to_two, "cp", -2)
    query_out = query_grad((key_far, *key_near), (first["ds"], early["ds"], ds_near))
    dk, dv = close(late["mine"], from_four, from_two, from_one)
    return query_out, dk, dv


def solution(mesh):
    return jax.shard_map(
        body,
        mesh=mesh,
        in_specs=(
            P("cp", "hd"),
            P("cp", "hd"),
            P("cp", "hd"),
            P("cp", "hd"),
            P("cp", "hd"),
            P("hd", None),
            P(),
        ),
        out_specs=(P("cp", "hd"), P("cp", "hd"), P("cp", "hd")),
        check_vma=False,
    )
```

```python
import functools

import jax
import jax.numpy as jnp
from jax import lax
from jax.experimental import pallas as pl
from jax.experimental.pallas import tpu as pltpu
from jax.sharding import PartitionSpec as P

HEAD_WIDTH = 128
HEADS = 8
BS = 512
MOST_BLK = 4
BEHIND = MOST_BLK * BS
TILE = 256
CHUNK = 256
EDGE = 4
LANES = HEADS * CHUNK
WIDTH = HEADS * HEAD_WIDTH
SCALE = HEAD_WIDTH ** (-0.5)
LOG2E = 1.4426950408889634
HIDDEN = -1e30
MIB = 2**20
DOCS = 16
BAND = 2 * HEAD_WIDTH
CUTS = 4
WHOLE = pl.BlockSpec(memory_space=pltpu.VMEM)
SCALARS = pl.BlockSpec(memory_space=pltpu.SMEM)
IN_HBM = pl.BlockSpec(memory_space=pltpu.HBM)


def shifted(value, axis, by):
    length = lax.axis_size(axis)
    return lax.ppermute(value, axis, [(i, (i + by) % length) for i in range(length)])


def swapped(value):
    length = lax.axis_size("cp")
    return lax.ppermute(value, "cp", [(i, i ^ 1) for i in range(length)])


def in_hbm(value):
    return pltpu.with_memory_space_constraint(value, pltpu.HBM)


def nt(a, b):
    return lax.dot_general(a, b, (((1,), (1,)), ((), ())), preferred_element_type=jnp.float32)


def nn(a, b):
    return lax.dot_general(a, b, (((1,), (0,)), ((), ())), preferred_element_type=jnp.float32)


def tn(a, b):
    return lax.dot_general(a, b, (((0,), (0,)), ((), ())), preferred_element_type=jnp.float32)


def tiles_of(chunk, near):
    last = BEHIND // TILE + chunk
    return range(EDGE, last + 1) if near else range(chunk, EDGE)


def window_tile(refs, tile):
    far, two, one, here = refs
    block, part = divmod(tile, BS // TILE)
    ref, row = [(far, BS), (far, 0), (two, 0), (one, 0), (here, 0)][block]
    row = row + part * TILE
    return ref[row : row + TILE, :]


def head_lanes(head):
    return slice(head * CHUNK, (head + 1) * CHUNK)


def head_columns(head):
    return slice(head * HEAD_WIDTH, (head + 1) * HEAD_WIDTH)


def at_tile(index):
    return slice(index * TILE, (index + 1) * TILE)


def fetch_kernel(halve, *refs):
    sources = refs[: len(halve)]
    targets, sems = refs[len(halve) : -1], refs[-1]
    moves, index = [], 0
    for source, cut in zip(sources, halve, strict=True):
        for part in range(2 if cut else 1):
            target = targets[index]
            index += 1
            size = max(target.shape[0] // 4, 16)
            for row in range(0, target.shape[0], size):
                moves.append(
                    (
                        source.at[pl.ds(part * CHUNK + row, size)],
                        target.at[pl.ds(row, size)],
                    )
                )
    copies = [pltpu.make_async_copy(a, b, sems.at[i]) for i, (a, b) in enumerate(moves)]
    for copy in copies:
        copy.start()
    for copy in copies:
        copy.wait()


def fetch(*arrays, halve=False):
    shapes = []
    for array in arrays:
        if halve:
            shapes += [jax.ShapeDtypeStruct((CHUNK, array.shape[1]), array.dtype)] * 2
        else:
            shapes.append(jax.ShapeDtypeStruct(array.shape, array.dtype))
    return pl.pallas_call(
        functools.partial(fetch_kernel, [halve] * len(arrays)),
        in_specs=[IN_HBM] * len(arrays),
        out_specs=[WHOLE] * len(shapes),
        out_shape=shapes,
        scratch_shapes=[pltpu.SemaphoreType.DMA((4 * len(shapes),))],
        compiler_params=pltpu.CompilerParams(vmem_limit_bytes=4 * MIB),
        cost_estimate=pl.CostEstimate(flops=0, bytes_accessed=4 * MIB, transcendentals=0),
        name="fetch_halves" if halve else "fetch",
    )(*(in_hbm(x) for x in arrays))


def stack_kernel(a_ref, b_ref, out_ref):
    out_ref[:BS, :] = a_ref[...]
    out_ref[BS:, :] = b_ref[...]


def stack(a, b):
    return pl.pallas_call(
        stack_kernel,
        in_specs=[WHOLE] * 2,
        out_specs=WHOLE,
        out_shape=jax.ShapeDtypeStruct((2 * BS, a.shape[1]), a.dtype),
        compiler_params=pltpu.CompilerParams(vmem_limit_bytes=2 * MIB),
        name="stack",
    )(a, b)


def add_kernel(parity, where_ref, a_ref, b_ref, out_ref):
    extra = b_ref[...].astype(jnp.float32)
    counts = (where_ref[0] & 1) == parity
    total = a_ref[...].astype(jnp.float32) + jnp.where(counts, extra, jnp.zeros_like(extra))
    out_ref[...] = total.astype(out_ref.dtype)


def add_where(parity, where, a, b):
    return pl.pallas_call(
        functools.partial(add_kernel, parity),
        in_specs=[SCALARS, WHOLE, WHOLE],
        out_specs=WHOLE,
        out_shape=jax.ShapeDtypeStruct(a.shape, a.dtype),
        compiler_params=pltpu.CompilerParams(vmem_limit_bytes=4 * MIB),
        name="add_where",
    )(where, a, b)


def weight_columns(where_ref, by):
    place = lax.rem(where_ref[1] + by, 4)
    return pl.ds(pl.multiple_of(place * WIDTH, WIDTH), WIDTH)


def band_copies(weight_ref, columns, target, sems, first):
    size = BAND // CUTS
    return [
        pltpu.make_async_copy(
            weight_ref.at[pl.ds(i * size, size), columns],
            target.at[i // CUTS, pl.ds(i % CUTS * size, size)],
            sems.at[first + i],
        )
        for i in range(WIDTH // size)
    ]


def dout_own_kernel(where_ref, weight_ref, low_ref, high_ref, sum_ref, g_scr, w_scr, sems):
    bands = HEADS // 2
    columns = weight_columns(where_ref, 0)
    copies = band_copies(weight_ref, columns, w_scr, sems, 0)
    for copy in copies:
        copy.start()
    g_scr[:CHUNK, :] = low_ref[...]
    g_scr[CHUNK:, :] = high_ref[...]
    for i in range(bands):
        for copy in copies[i * CUTS : (i + 1) * CUTS]:
            copy.wait()
        sum_ref[:, i * BAND : (i + 1) * BAND] = nt(g_scr[...], w_scr[i])


def dout_near_kernel(where_ref, weight_ref, *refs):
    pieces, (before_ref, sum_ref, kept_ref, g_scr, w_scr, sems) = refs[:4], refs[4:]
    bands = HEADS // 2
    sides = [weight_columns(where_ref, 3), weight_columns(where_ref, 1)]
    count = bands * CUTS
    copies = []
    for side, columns in enumerate(sides):
        copies += band_copies(weight_ref, columns, w_scr.at[side], sems, side * count)
    last = band_copies(weight_ref, weight_columns(where_ref, 2), kept_ref, sems, 2 * count)
    for copy in (*copies, *last):
        copy.start()
    for index, piece in enumerate(pieces):
        rows = slice(index % 2 * CHUNK, (index % 2 + 1) * CHUNK)
        g_scr[rows, index // 2 * WIDTH : (index // 2 + 1) * WIDTH] = piece[...]
    for side in range(2):
        for i in range(bands):
            for copy in copies[(side * bands + i) * CUTS : (side * bands + i + 1) * CUTS]:
                copy.wait()
            at = slice(i * BAND, (i + 1) * BAND)
            part = nt(g_scr[:, side * WIDTH : (side + 1) * WIDTH], w_scr[side, i])
            sum_ref[:, at] = part + (before_ref if side == 0 else sum_ref)[:, at]
    for copy in last:
        copy.wait()


def dout_last_kernel(*refs):
    low_ref, high_ref, kept_ref, before_ref, attn_ref = refs[:5]
    inverse = {"near": refs[5:7], "far": refs[7:9]}
    outs = {"near": refs[9:11], "far": refs[11:13]}
    g_scr, a_scr, sem = refs[13:]
    attn = pltpu.make_async_copy(attn_ref, a_scr, sem)
    attn.start()
    g_scr[:CHUNK, :] = low_ref[...]
    g_scr[CHUNK:, :] = high_ref[...]
    for i in range(HEADS // 2):
        cols = slice(i * BAND, (i + 1) * BAND)
        whole = nt(g_scr[...], kept_ref[i]) + before_ref[:, cols]
        if i == 0:
            attn.wait()
        for chunk in range(2):
            rows = slice(chunk * CHUNK, (chunk + 1) * CHUNK)
            dout = whole[rows, :].astype(jnp.bfloat16).astype(jnp.float32)
            product = jnp.transpose(dout * a_scr[rows, cols].astype(jnp.float32))
            for side in range(2):
                head = 2 * i + side
                delta = jnp.sum(product[head_columns(side), :], axis=0, keepdims=True)
                to = slice((chunk * HEADS + head) * CHUNK, (chunk * HEADS + head + 1) * CHUNK)
                for group in ("near", "far"):
                    inv = inverse[group][chunk][:1, head_lanes(head)]
                    down = jnp.transpose(jnp.broadcast_to(inv, (HEAD_WIDTH, CHUNK)))
                    dout_ref, delta_ref = outs[group]
                    dout_ref[to, :] = (dout[:, head_columns(side)] * down).astype(jnp.bfloat16)
                    delta_ref[:, to] = jnp.broadcast_to(delta * inv, (8, CHUNK))


def dout_own(where, weight, low, high):
    return pl.pallas_call(
        dout_own_kernel,
        in_specs=[SCALARS, IN_HBM, WHOLE, WHOLE],
        out_specs=WHOLE,
        out_shape=jax.ShapeDtypeStruct((BS, WIDTH), jnp.float32),
        scratch_shapes=[
            pltpu.VMEM((BS, WIDTH), jnp.bfloat16),
            pltpu.VMEM((HEADS // 2, BAND, WIDTH), jnp.bfloat16),
            pltpu.SemaphoreType.DMA((HEADS // 2 * CUTS,)),
        ],
        compiler_params=pltpu.CompilerParams(vmem_limit_bytes=5 * MIB),
        cost_estimate=pl.CostEstimate(
            flops=2 * BS * WIDTH * WIDTH, bytes_accessed=4 * MIB, transcendentals=0
        ),
        name="dout_own",
    )(where, in_hbm(weight), low, high)


def dout_near(where, weight, pieces, before):
    return pl.pallas_call(
        dout_near_kernel,
        in_specs=[SCALARS, IN_HBM, *[WHOLE] * 5],
        out_specs=[WHOLE] * 2,
        out_shape=[
            jax.ShapeDtypeStruct((BS, WIDTH), jnp.float32),
            jax.ShapeDtypeStruct((HEADS // 2, BAND, WIDTH), jnp.bfloat16),
        ],
        scratch_shapes=[
            pltpu.VMEM((BS, 2 * WIDTH), jnp.bfloat16),
            pltpu.VMEM((2, HEADS // 2, BAND, WIDTH), jnp.bfloat16),
            pltpu.SemaphoreType.DMA((3 * HEADS // 2 * CUTS,)),
        ],
        compiler_params=pltpu.CompilerParams(vmem_limit_bytes=11 * MIB),
        cost_estimate=pl.CostEstimate(
            flops=4 * BS * WIDTH * WIDTH, bytes_accessed=8 * MIB, transcendentals=0
        ),
        name="dout_near",
    )(where, in_hbm(weight), *pieces, before)


def dout_last(pieces, kept, before, attn, near, far):
    shapes = [
        jax.ShapeDtypeStruct((2 * LANES, HEAD_WIDTH), jnp.bfloat16),
        jax.ShapeDtypeStruct((8, 2 * LANES), jnp.float32),
    ] * 2
    return pl.pallas_call(
        dout_last_kernel,
        in_specs=[*[WHOLE] * 4, IN_HBM, *[WHOLE] * 4],
        out_specs=[WHOLE] * 4,
        out_shape=shapes,
        scratch_shapes=[
            pltpu.VMEM((BS, WIDTH), jnp.bfloat16),
            pltpu.VMEM((BS, WIDTH), jnp.bfloat16),
            pltpu.SemaphoreType.DMA,
        ],
        compiler_params=pltpu.CompilerParams(vmem_limit_bytes=8 * MIB),
        cost_estimate=pl.CostEstimate(
            flops=2 * BS * WIDTH * WIDTH, bytes_accessed=8 * MIB, transcendentals=0
        ),
        name="dout_last",
    )(*pieces, kept, before, in_hbm(attn), *near, *far)


def stats_kernel(chunk, near, where_ref, segment_ref, q_ref, *refs):
    if near:
        keys = (None, *refs[:3])
        refs = refs[3:]
    else:
        keys = (refs[0], None, None, None)
        top_ref, total_ref = refs[1:3]
        refs = refs[3:]
    e_ref, out_a, out_b, even, odd = refs
    held = (even, odd)
    rows = slice(chunk * CHUNK, (chunk + 1) * CHUNK)
    factor = SCALE * LOG2E
    tiles = tiles_of(chunk, near)

    first = where_ref[0] * BS - BEHIND
    row = lax.broadcasted_iota(jnp.int32, (1, CHUNK), 1) + (BEHIND + chunk * CHUNK)
    start = jnp.zeros((1, CHUNK), jnp.int32) - first
    segments = segment_ref[...]
    for doc in range(1, DOCS):
        begin = jnp.sum((segments < doc).astype(jnp.int32), axis=(0, 1), keepdims=True) - first
        start = jnp.where(begin <= row, begin, start)

    def score(head, tile, top):
        s = nt(window_tile(keys, tile), q_ref[rows, head_columns(head)])
        key = lax.broadcasted_iota(jnp.int32, (TILE, CHUNK), 0)
        seen = key >= start - tile * TILE
        if near and tile == tiles[-1]:
            seen = seen & (key <= lax.broadcasted_iota(jnp.int32, (TILE, CHUNK), 1))
        s = jnp.where(seen, s, HIDDEN)
        held[head % 2][at_tile(tile - tiles[0]), :] = s
        most = jnp.max(s.reshape(TILE // 8, 8, CHUNK), axis=0)
        return most if top is None else jnp.maximum(top, most)

    def weigh(head, tile, top, total):
        at = at_tile(tile - tiles[0])
        e = jnp.exp2(held[head % 2][at, :] * factor - top)
        e_ref[at, head_lanes(head)] = e.astype(jnp.bfloat16)
        part = jnp.sum(e.reshape(TILE // 8, 8, CHUNK), axis=0)
        return part if total is None else total + part

    following = None
    for tile in tiles:
        following = score(0, tile, following)
    for head in range(HEADS):
        top = jnp.max(following, axis=0, keepdims=True) * factor
        following = total = None
        for tile in tiles:
            if head + 1 < HEADS:
                following = score(head + 1, tile, following)
            total = weigh(head, tile, top, total)
        total = jnp.sum(total, axis=0, keepdims=True)
        lanes = head_lanes(head)
        if near:
            out_a[:, lanes] = jnp.broadcast_to(top, (8, CHUNK))
            out_b[:, lanes] = jnp.broadcast_to(total, (8, CHUNK))
        else:
            other_top, other_total = top_ref[:1, lanes], total_ref[:1, lanes]
            highest = jnp.maximum(top, other_top)
            near_part, far_part = jnp.exp2(other_top - highest), jnp.exp2(top - highest)
            inverse = 1.0 / (near_part * other_total + far_part * total)
            out_a[:, lanes] = jnp.broadcast_to(near_part * inverse, (8, CHUNK))
            out_b[:, lanes] = jnp.broadcast_to(far_part * inverse, (8, CHUNK))


def stats(chunk, near, where, segments, queries, keys, known=()):
    span = len(tiles_of(chunk, near)) * TILE
    args = [where, segments, queries, *keys, *known]
    return pl.pallas_call(
        functools.partial(stats_kernel, chunk, near),
        in_specs=[SCALARS] + [WHOLE] * (len(args) - 1),
        out_specs=[WHOLE] * 3,
        out_shape=[
            jax.ShapeDtypeStruct((span, LANES), jnp.bfloat16),
            jax.ShapeDtypeStruct((8, LANES), jnp.float32),
            jax.ShapeDtypeStruct((8, LANES), jnp.float32),
        ],
        scratch_shapes=[pltpu.VMEM((span, CHUNK), jnp.float32)] * 2,
        compiler_params=pltpu.CompilerParams(vmem_limit_bytes=6 * MIB),
        cost_estimate=pl.CostEstimate(
            flops=2 * LANES * span * HEAD_WIDTH,
            bytes_accessed=4 * MIB,
            transcendentals=LANES * span,
        ),
        name=f"stats{chunk}{'near' if near else 'far'}",
    )(*args)


def main_kernel(near, q_ref, dout_ref, delta_ref, *refs):
    count = 3 if near else 1
    values = (None, *refs[:3]) if near else (refs[0], None, None, None)
    refs = refs[count + 2 :]
    ds_refs, outs, sum_ref = refs[:2], refs[2:-1], refs[-1]
    window = list(tiles_of(1, True) if near else tiles_of(0, False))
    begun = set()
    for chunk in range(2):
        tiles = tiles_of(chunk, near)
        ds_ref = ds_refs[chunk]
        for pair in range(HEADS // 2):
            lanes = slice(2 * pair * CHUNK, 2 * (pair + 1) * CHUNK)
            first = (chunk * HEADS + 2 * pair) * CHUNK
            dout = dout_ref[first : first + 2 * CHUNK, :]
            queries = jnp.concatenate(
                [
                    q_ref[chunk * CHUNK : (chunk + 1) * CHUNK, head_columns(2 * pair + side)]
                    for side in range(2)
                ],
                axis=0,
            )
            at = {tile: at_tile(tile - tiles[0]) for tile in tiles}
            to = {tile: at_tile(tile - window[0]) for tile in tiles}
            more = {tile: tile in begun for tile in tiles}
            begun.update(tiles)
            last = pair == HEADS // 2 - 1

            def store(tile, side, value):
                columns = head_columns(side)
                if more[tile]:
                    value = value + sum_ref[to[tile], columns]
                if last and (chunk == 1 or tile not in tiles_of(1, near)):
                    block, part = divmod(tile, BS // TILE)
                    out = outs[block - 2 if near else block]
                    out[at_tile(part), columns] = value.astype(out.dtype)
                else:
                    sum_ref[to[tile], columns] = value

            for tile in tiles:
                store(tile, 1, nn(ds_ref[at[tile], lanes], dout))
            for side in range(2):
                here = head_lanes(2 * pair + side)
                row = first + side * CHUNK
                for tile in tiles:
                    dp = nt(window_tile(values, tile), dout[at_tile(side), :])
                    prob = ds_ref[at[tile], here].astype(jnp.float32)
                    ds_ref[at[tile], here] = (
                        prob * (dp - delta_ref[:1, row : row + CHUNK])
                    ).astype(jnp.bfloat16)
            for tile in tiles:
                store(tile, 0, nn(ds_ref[at[tile], lanes], queries) * SCALE)


def main(near, queries, dout, delta, values, e):
    blocks = 3 if near else 2
    shapes = [jax.ShapeDtypeStruct(x.shape, x.dtype) for x in e]
    block = jax.ShapeDtypeStruct((BS, 2 * HEAD_WIDTH), jnp.bfloat16)
    shapes += [block, block]
    if near:
        shapes.append(jax.ShapeDtypeStruct(block.shape, jnp.float32))
    args = [queries, dout, delta, *values, *e]
    tiles = sum(len(tiles_of(chunk, near)) for chunk in range(2))
    return pl.pallas_call(
        functools.partial(main_kernel, near),
        in_specs=[WHOLE] * len(args),
        out_specs=[WHOLE] * len(shapes),
        out_shape=shapes,
        scratch_shapes=[pltpu.VMEM((blocks * BS, 2 * HEAD_WIDTH), jnp.float32)],
        input_output_aliases={len(args) - 2: 0, len(args) - 1: 1},
        compiler_params=pltpu.CompilerParams(vmem_limit_bytes=6 * MIB),
        cost_estimate=pl.CostEstimate(
            flops=2 * 3 * LANES * tiles * TILE * HEAD_WIDTH,
            bytes_accessed=4 * MIB,
            transcendentals=0,
        ),
        name="main_near" if near else "main_far",
    )(*args)


def query_kernel(far_ref, two_ref, one_ref, here_ref, *refs):
    far_ds, near_ds, (out_ref, k_scr) = refs[:2], refs[2:4], refs[4:]
    keys = (far_ref, two_ref, one_ref, here_ref)
    window = (BEHIND + BS) // TILE
    for tile in range(window):
        k_scr[at_tile(tile), :] = window_tile(keys, tile)
    for chunk in range(2):
        rows = slice(chunk * CHUNK, (chunk + 1) * CHUNK)
        end = (BEHIND // TILE + chunk + 1) * TILE
        for head in range(HEADS):
            lanes = head_lanes(head)
            grad = tn(k_scr[chunk * TILE : EDGE * TILE, :], far_ds[chunk][:, lanes])
            grad = grad + tn(k_scr[EDGE * TILE : end, :], near_ds[chunk][:, lanes])
            out_ref[rows, head_columns(head)] = (jnp.transpose(grad) * SCALE).astype(jnp.bfloat16)


def query_grad(keys, ds):
    return pl.pallas_call(
        query_kernel,
        in_specs=[WHOLE] * (len(keys) + len(ds)),
        out_specs=WHOLE,
        out_shape=jax.ShapeDtypeStruct((BS, WIDTH), jnp.bfloat16),
        scratch_shapes=[pltpu.VMEM((BEHIND + BS, HEAD_WIDTH), jnp.bfloat16)],
        compiler_params=pltpu.CompilerParams(vmem_limit_bytes=6 * MIB),
        cost_estimate=pl.CostEstimate(
            flops=4 * LANES * 9 * TILE * HEAD_WIDTH, bytes_accessed=MIB, transcendentals=0
        ),
        name="query_grad",
    )(*keys, *ds)


def close_kernel(mine_ref, four_ref, two_ref, one_ref, dk_ref, dv_ref):
    total = mine_ref[...] + four_ref[...].astype(jnp.float32)
    total = total + two_ref[...].astype(jnp.float32) + one_ref[...].astype(jnp.float32)
    dk_ref[...] = total[:, :HEAD_WIDTH].astype(jnp.bfloat16)
    dv_ref[...] = total[:, HEAD_WIDTH:].astype(jnp.bfloat16)


def close(mine, four, two, one):
    return pl.pallas_call(
        close_kernel,
        in_specs=[WHOLE] * 4,
        out_specs=[WHOLE] * 2,
        out_shape=[jax.ShapeDtypeStruct((BS, HEAD_WIDTH), jnp.bfloat16)] * 2,
        compiler_params=pltpu.CompilerParams(vmem_limit_bytes=6 * MIB),
        name="close",
    )(mine, four, two, one)


def body(queries, keys, values, attn_out, out_grad, out_weight, segment):
    device = lax.axis_index("cp")
    where = jnp.stack([device, lax.axis_index("hd")]).astype(jnp.int32)
    segments = segment.reshape(128, -1)

    key_one, key_two = shifted(keys, "cp", 1), shifted(keys, "cp", 2)
    low, high = fetch(out_grad, halve=True)
    prev_low, next_high = shifted(low, "hd", 1), shifted(high, "hd", -1)
    next_low, prev_high = shifted(low, "hd", -1), shifted(high, "hd", 1)
    queries, key_here, value_here, segments = fetch(queries, keys, values, segments)
    partial = dout_own(where, out_weight, low, high)
    key_far = shifted(stack(key_one, key_two), "cp", 2)
    key_near = (key_two, key_one, key_here)

    partial, key_here = lax.optimization_barrier((partial, key_here))
    near_zero = stats(0, True, where, segments, queries, (key_two, key_one, key_here))
    prev_low, next_high, values, near_zero = lax.optimization_barrier(
        (prev_low, next_high, values, near_zero)
    )
    far_low, far_high = shifted(prev_low, "hd", 1), shifted(next_high, "hd", -1)
    value_one, value_two = shifted(values, "cp", 1), shifted(values, "cp", 2)

    near_one = stats(1, True, where, segments, queries, key_near)
    value_one, value_two, near_one = lax.optimization_barrier((value_one, value_two, near_one))
    value_far = shifted(stack(value_one, value_two), "cp", 2)
    e_near, e_far, inv_near, inv_far = [], [], [], []
    for c, (e, top, total) in enumerate((near_zero, near_one)):
        e_near.append(e)
        e, near, far = stats(c, False, where, segments, queries, (key_far,), (top, total))
        e_far.append(e)
        inv_near.append(near)
        inv_far.append(far)
    partial, inv_far = lax.optimization_barrier((partial, inv_far))
    partial, kept = dout_near(
        where, out_weight, (prev_low, prev_high, next_low, next_high), partial
    )
    dout_n, delta_n, dout_f, delta_f = dout_last(
        (far_low, far_high), kept, partial, attn_out, inv_near, inv_far
    )
    *ds_far, to_four, to_three = main(False, queries, dout_f, delta_f, (value_far,), e_far)
    back = swapped(to_three)
    to_four = add_where(1, where, to_four, back)
    to_four, dout_n = lax.optimization_barrier((to_four, dout_n))
    from_four = shifted(to_four, "cp", -4)
    *ds_near, to_two, to_one, mine = main(
        True, queries, dout_n, delta_n, (value_two, value_one, value_here), e_near
    )
    to_two = add_where(0, where, to_two, back)
    to_one, to_two, ds_near = lax.optimization_barrier((to_one, to_two, ds_near))
    from_one, from_two = shifted(to_one, "cp", -1), shifted(to_two, "cp", -2)
    query_out = query_grad((key_far, *key_near), (*ds_far, *ds_near))
    dk, dv = close(mine, from_four, from_two, from_one)
    return query_out, dk, dv


def solution(mesh):
    return jax.shard_map(
        body,
        mesh=mesh,
        in_specs=(
            P("cp", "hd"),
            P("cp", "hd"),
            P("cp", "hd"),
            P("cp", "hd"),
            P("cp", "hd"),
            P("hd", None),
            P(),
        ),
        out_specs=(P("cp", "hd"), P("cp", "hd"), P("cp", "hd")),
        check_vma=False,
    )
```

```python
import functools

import jax
import jax.numpy as jnp
from jax import lax
from jax.experimental import pallas as pl
from jax.experimental.pallas import tpu as pltpu
from jax.sharding import PartitionSpec as P

HEAD_WIDTH = 128
HEADS = 8
BS = 512
MOST_BLK = 4
BEHIND = MOST_BLK * BS
TILE = 256
CHUNK = 256
EDGE = 4
LANES = HEADS * CHUNK
WIDTH = HEADS * HEAD_WIDTH
SCALE = HEAD_WIDTH ** (-0.5)
LOG2E = 1.4426950408889634
HIDDEN = -1e30
MIB = 2**20
DOCS = 16
BAND = 2 * HEAD_WIDTH
KEY = slice(0, HEAD_WIDTH)
VALUE = slice(HEAD_WIDTH, 2 * HEAD_WIDTH)
WHOLE = pl.BlockSpec(memory_space=pltpu.VMEM)
SCALARS = pl.BlockSpec(memory_space=pltpu.SMEM)
IN_HBM = pl.BlockSpec(memory_space=pltpu.HBM)


def shifted(value, axis, by):
    length = lax.axis_size(axis)
    return lax.ppermute(value, axis, [(i, (i + by) % length) for i in range(length)])


def swapped(value):
    length = lax.axis_size("cp")
    return lax.ppermute(value, "cp", [(i, i ^ 1) for i in range(length)])


def in_hbm(value):
    return pltpu.with_memory_space_constraint(value, pltpu.HBM)


def nt(a, b):
    return lax.dot_general(a, b, (((1,), (1,)), ((), ())), preferred_element_type=jnp.float32)


def nn(a, b):
    return lax.dot_general(a, b, (((1,), (0,)), ((), ())), preferred_element_type=jnp.float32)


def tn(a, b):
    return lax.dot_general(a, b, (((0,), (0,)), ((), ())), preferred_element_type=jnp.float32)


def tiles_of(chunk, near):
    last = BEHIND // TILE + chunk
    return range(EDGE, last + 1) if near else range(chunk, EDGE)


def window_tile(refs, tile, columns):
    far, two, one, here = refs
    block, part = divmod(tile, BS // TILE)
    ref, row = [(far, BS), (far, 0), (two, 0), (one, 0), (here, 0)][block]
    row = row + part * TILE
    return ref[row : row + TILE, columns]


def head_lanes(head):
    return slice(head * CHUNK, (head + 1) * CHUNK)


def head_columns(head):
    return slice(head * HEAD_WIDTH, (head + 1) * HEAD_WIDTH)


def at_tile(index):
    return slice(index * TILE, (index + 1) * TILE)


def pull(moves, sems, pieces):
    copies = []
    for source, target in moves:
        size = target.shape[0] // pieces
        for row in range(0, target.shape[0], size):
            at = pl.ds(row, size)
            copies.append(
                pltpu.make_async_copy(source.at[at], target.at[at], sems.at[len(copies)])
            )
    for copy in copies:
        copy.start()
    return copies


def fetch_first_kernel(grad_ref, key_ref, value_ref, low_ref, high_ref, both_ref, sems):
    moves = [
        (grad_ref.at[pl.ds(0, CHUNK)], low_ref),
        (grad_ref.at[pl.ds(CHUNK, CHUNK)], high_ref),
        (key_ref, both_ref.at[:, pl.ds(0, HEAD_WIDTH)]),
        (value_ref, both_ref.at[:, pl.ds(HEAD_WIDTH, HEAD_WIDTH)]),
    ]
    for copy in pull(moves, sems, 4):
        copy.wait()


def fetch_first(grad, keys, values):
    return pl.pallas_call(
        fetch_first_kernel,
        in_specs=[IN_HBM] * 3,
        out_specs=[WHOLE] * 3,
        out_shape=[
            jax.ShapeDtypeStruct((CHUNK, WIDTH), jnp.bfloat16),
            jax.ShapeDtypeStruct((CHUNK, WIDTH), jnp.bfloat16),
            jax.ShapeDtypeStruct((BS, 2 * HEAD_WIDTH), jnp.bfloat16),
        ],
        scratch_shapes=[pltpu.SemaphoreType.DMA((16,))],
        compiler_params=pltpu.CompilerParams(vmem_limit_bytes=2 * MIB),
        name="fetch_first",
    )(in_hbm(grad), in_hbm(keys), in_hbm(values))


def fetch_kernel(count, *refs):
    for copy in pull(list(zip(refs[:count], refs[count:-1], strict=True)), refs[-1], 4):
        copy.wait()


def fetch(*arrays):
    return pl.pallas_call(
        functools.partial(fetch_kernel, len(arrays)),
        in_specs=[IN_HBM] * len(arrays),
        out_specs=[WHOLE] * len(arrays),
        out_shape=[jax.ShapeDtypeStruct(x.shape, x.dtype) for x in arrays],
        scratch_shapes=[pltpu.SemaphoreType.DMA((4 * len(arrays),))],
        compiler_params=pltpu.CompilerParams(vmem_limit_bytes=2 * MIB),
        name="fetch",
    )(*(in_hbm(x) for x in arrays))


def stack_kernel(a_ref, b_ref, out_ref):
    out_ref[:BS, :] = a_ref[...]
    out_ref[BS:, :] = b_ref[...]


def stack(a, b):
    return pl.pallas_call(
        stack_kernel,
        in_specs=[WHOLE] * 2,
        out_specs=WHOLE,
        out_shape=jax.ShapeDtypeStruct((2 * BS, a.shape[1]), a.dtype),
        compiler_params=pltpu.CompilerParams(vmem_limit_bytes=2 * MIB),
        name="stack",
    )(a, b)


def add_kernel(parity, where_ref, a_ref, b_ref, out_ref):
    extra = b_ref[...].astype(jnp.float32)
    if parity is not None:
        counts = (where_ref[0] & 1) == parity
        extra = jnp.where(counts, extra, jnp.zeros_like(extra))
    total = a_ref[...].astype(jnp.float32) + extra
    out_ref[...] = total.astype(out_ref.dtype)


def add_where(parity, where, a, b):
    return pl.pallas_call(
        functools.partial(add_kernel, parity),
        in_specs=[SCALARS, WHOLE, WHOLE],
        out_specs=WHOLE,
        out_shape=jax.ShapeDtypeStruct(a.shape, a.dtype),
        compiler_params=pltpu.CompilerParams(vmem_limit_bytes=4 * MIB),
        name="add_where",
    )(where, a, b)


def weight_columns(where_ref, by):
    place = lax.rem(where_ref[1] + by, 4)
    return pl.ds(pl.multiple_of(place * WIDTH, WIDTH), WIDTH)


def dout_own_kernel(where_ref, weight_ref, low_ref, high_ref, sum_ref, w_scr, sems):
    copies = pull([(weight_ref.at[:, weight_columns(where_ref, 0)], w_scr)], sems, 16)
    for copy in copies:
        copy.wait()
    for rows, g_ref in ((slice(0, CHUNK), low_ref), (slice(CHUNK, BS), high_ref)):
        for i in range(HEADS // 2):
            at = slice(i * BAND, (i + 1) * BAND)
            sum_ref[rows, at] = nt(g_ref[...], w_scr[at, :])


def dout_last_kernel(*refs):
    low_ref, high_ref, kept_ref, before_ref, attn_ref = refs[:5]
    inverse = {"near": refs[5:7], "far": refs[7:9]}
    outs = {"near": refs[9:11], "far": refs[11:13]}
    g_scr, a_scr, sem = refs[13:]
    attn = pltpu.make_async_copy(attn_ref, a_scr, sem)
    attn.start()
    g_scr[:CHUNK, :] = low_ref[...]
    g_scr[CHUNK:, :] = high_ref[...]
    for i in range(HEADS // 2):
        cols = slice(i * BAND, (i + 1) * BAND)
        whole = nt(g_scr[...], kept_ref[cols, :]) + before_ref[:, cols]
        if i == 0:
            attn.wait()
        for chunk in range(2):
            rows = slice(chunk * CHUNK, (chunk + 1) * CHUNK)
            dout = whole[rows, :].astype(jnp.bfloat16).astype(jnp.float32)
            product = jnp.transpose(dout * a_scr[rows, cols].astype(jnp.float32))
            for side in range(2):
                head = 2 * i + side
                delta = jnp.sum(product[head_columns(side), :], axis=0, keepdims=True)
                to = slice((chunk * HEADS + head) * CHUNK, (chunk * HEADS + head + 1) * CHUNK)
                for group in ("near", "far"):
                    inv = inverse[group][chunk][:1, head_lanes(head)]
                    down = jnp.transpose(jnp.broadcast_to(inv, (HEAD_WIDTH, CHUNK)))
                    dout_ref, delta_ref = outs[group]
                    dout_ref[to, :] = (dout[:, head_columns(side)] * down).astype(jnp.bfloat16)
                    delta_ref[:, to] = jnp.broadcast_to(delta * inv, (8, CHUNK))


def dout_own(where, weight, low, high):
    return pl.pallas_call(
        dout_own_kernel,
        in_specs=[SCALARS, IN_HBM, WHOLE, WHOLE],
        out_specs=WHOLE,
        out_shape=jax.ShapeDtypeStruct((BS, WIDTH), jnp.float32),
        scratch_shapes=[
            pltpu.VMEM((WIDTH, WIDTH), jnp.bfloat16),
            pltpu.SemaphoreType.DMA((16,)),
        ],
        compiler_params=pltpu.CompilerParams(vmem_limit_bytes=5 * MIB),
        cost_estimate=pl.CostEstimate(
            flops=2 * BS * WIDTH * WIDTH, bytes_accessed=4 * MIB, transcendentals=0
        ),
        name="dout_own",
    )(where, in_hbm(weight), low, high)


def dout_last(pieces, kept, before, attn, near, far):
    shapes = [
        jax.ShapeDtypeStruct((2 * LANES, HEAD_WIDTH), jnp.bfloat16),
        jax.ShapeDtypeStruct((8, 2 * LANES), jnp.float32),
    ] * 2
    return pl.pallas_call(
        dout_last_kernel,
        in_specs=[*[WHOLE] * 4, IN_HBM, *[WHOLE] * 4],
        out_specs=[WHOLE] * 4,
        out_shape=shapes,
        scratch_shapes=[
            pltpu.VMEM((BS, WIDTH), jnp.bfloat16),
            pltpu.VMEM((BS, WIDTH), jnp.bfloat16),
            pltpu.SemaphoreType.DMA,
        ],
        compiler_params=pltpu.CompilerParams(vmem_limit_bytes=8 * MIB),
        cost_estimate=pl.CostEstimate(
            flops=2 * BS * WIDTH * WIDTH, bytes_accessed=8 * MIB, transcendentals=0
        ),
        name="dout_last",
    )(*pieces, kept, before, in_hbm(attn), *near, *far)


def stats_kernel(chunk, near, sides, where_ref, segment_ref, q_ref, *refs):
    if near:
        keys = (None, *refs[:3])
        weight_ref, refs = refs[3], refs[4:]
        e_ref, out_a, out_b, *kept_refs, even, odd, sems = refs
        moves = [
            (weight_ref.at[:, weight_columns(where_ref, side)], kept)
            for side, kept in zip(sides, kept_refs, strict=True)
        ]
        copies = pull(moves, sems, 4)
    else:
        keys = (refs[0], None, None, None)
        top_ref, total_ref, low_ref, high_ref, kept_ref, before_ref = refs[1:7]
        e_ref, out_a, out_b, sum_ref, even, odd = refs[7:]
    held = (even, odd)
    rows = slice(chunk * CHUNK, (chunk + 1) * CHUNK)
    factor = SCALE * LOG2E
    tiles = tiles_of(chunk, near)

    first = where_ref[0] * BS - BEHIND
    row = lax.broadcasted_iota(jnp.int32, (1, CHUNK), 1) + (BEHIND + chunk * CHUNK)
    start = jnp.zeros((1, CHUNK), jnp.int32) - first
    segments = segment_ref[...]
    for doc in range(1, DOCS):
        begin = jnp.sum((segments < doc).astype(jnp.int32), axis=(0, 1), keepdims=True) - first
        start = jnp.where(begin <= row, begin, start)

    def score(head, tile, top):
        s = nt(window_tile(keys, tile, KEY), q_ref[rows, head_columns(head)])
        key = lax.broadcasted_iota(jnp.int32, (TILE, CHUNK), 0)
        seen = key >= start - tile * TILE
        if near and tile == tiles[-1]:
            seen = seen & (key <= lax.broadcasted_iota(jnp.int32, (TILE, CHUNK), 1))
        s = jnp.where(seen, s, HIDDEN)
        held[head % 2][at_tile(tile - tiles[0]), :] = s
        most = jnp.max(s.reshape(TILE // 8, 8, CHUNK), axis=0)
        return most if top is None else jnp.maximum(top, most)

    def weigh(head, tile, top, total):
        at = at_tile(tile - tiles[0])
        e = jnp.exp2(held[head % 2][at, :] * factor - top)
        e_ref[at, head_lanes(head)] = e.astype(jnp.bfloat16)
        part = jnp.sum(e.reshape(TILE // 8, 8, CHUNK), axis=0)
        return part if total is None else total + part

    jobs = []
    if not near:
        for part, g_ref in enumerate((low_ref, high_ref)):
            for band in range(HEADS // 2):
                jobs.append((g_ref, at_tile(part), slice(band * BAND, (band + 1) * BAND)))

    def work():
        g_ref, at, columns = jobs.pop(0)
        sum_ref[at, columns] = before_ref[at, columns] + nt(g_ref[...], kept_ref[columns, :])

    following = None
    for tile in tiles:
        following = score(0, tile, following)
    for head in range(HEADS):
        top = jnp.max(following, axis=0, keepdims=True) * factor
        following = total = None
        for tile in tiles:
            if head + 1 < HEADS:
                following = score(head + 1, tile, following)
            total = weigh(head, tile, top, total)
        if jobs:
            work()
        total = jnp.sum(total, axis=0, keepdims=True)
        lanes = head_lanes(head)
        if near:
            out_a[:, lanes] = jnp.broadcast_to(top, (8, CHUNK))
            out_b[:, lanes] = jnp.broadcast_to(total, (8, CHUNK))
        else:
            other_top, other_total = top_ref[:1, lanes], total_ref[:1, lanes]
            highest = jnp.maximum(top, other_top)
            near_part, far_part = jnp.exp2(other_top - highest), jnp.exp2(top - highest)
            inverse = 1.0 / (near_part * other_total + far_part * total)
            out_a[:, lanes] = jnp.broadcast_to(near_part * inverse, (8, CHUNK))
            out_b[:, lanes] = jnp.broadcast_to(far_part * inverse, (8, CHUNK))
    if near:
        for copy in copies:
            copy.wait()


def stats(chunk, near, where, segments, queries, keys, rest, sides=()):
    span = len(tiles_of(chunk, near)) * TILE
    args = [where, segments, queries, *keys, *rest]
    specs = [SCALARS] + [WHOLE] * (len(args) - 1)
    shapes = [
        jax.ShapeDtypeStruct((span, LANES), jnp.bfloat16),
        jax.ShapeDtypeStruct((8, LANES), jnp.float32),
        jax.ShapeDtypeStruct((8, LANES), jnp.float32),
    ]
    scratch = [pltpu.VMEM((span, CHUNK), jnp.float32)] * 2
    if near:
        specs[-1], args[-1] = IN_HBM, in_hbm(args[-1])
        shapes += [jax.ShapeDtypeStruct((WIDTH, WIDTH), jnp.bfloat16)] * len(sides)
        scratch.append(pltpu.SemaphoreType.DMA((4 * len(sides),)))
    else:
        shapes.append(jax.ShapeDtypeStruct((BS, WIDTH), jnp.float32))
    return pl.pallas_call(
        functools.partial(stats_kernel, chunk, near, sides),
        in_specs=specs,
        out_specs=[WHOLE] * len(shapes),
        out_shape=shapes,
        scratch_shapes=scratch,
        compiler_params=pltpu.CompilerParams(vmem_limit_bytes=6 * MIB),
        cost_estimate=pl.CostEstimate(
            flops=4 * LANES * span * HEAD_WIDTH,
            bytes_accessed=4 * MIB,
            transcendentals=LANES * span,
        ),
        name=f"stats{chunk}{'near' if near else 'far'}",
    )(*args)


def group_tiles(chunk, group):
    tiles = tiles_of(chunk, group != "far")
    own = BEHIND // TILE
    if group == "far":
        return tiles
    return [tile for tile in tiles if (tile >= own) == (group == "own")]


def main_kernel(group, q_ref, dout_ref, delta_ref, *refs):
    values = {
        "far": lambda: (refs[0], None, None, None),
        "mid": lambda: (None, refs[0], refs[1], None),
        "own": lambda: (None, None, None, refs[0]),
    }[group]()
    refs = refs[(2 if group == "mid" else 1) + 2 :]
    ds_refs, outs, sum_ref = refs[:2], refs[2:-1], refs[-1]
    window = group_tiles(0 if group == "far" else 1, group)
    begun = set()
    for chunk in range(2):
        tiles = group_tiles(chunk, group)
        base = tiles_of(chunk, group != "far")[0]
        ds_ref = ds_refs[chunk]
        for pair in range(HEADS // 2):
            lanes = slice(2 * pair * CHUNK, 2 * (pair + 1) * CHUNK)
            first = (chunk * HEADS + 2 * pair) * CHUNK
            dout = dout_ref[first : first + 2 * CHUNK, :]
            queries = jnp.concatenate(
                [
                    q_ref[chunk * CHUNK : (chunk + 1) * CHUNK, head_columns(2 * pair + side)]
                    for side in range(2)
                ],
                axis=0,
            )
            at = {tile: at_tile(tile - base) for tile in tiles}
            to = {tile: at_tile(tile - window[0]) for tile in tiles}
            more = {tile: tile in begun for tile in tiles}
            begun.update(tiles)
            last = pair == HEADS // 2 - 1

            def store(tile, side, value):
                columns = head_columns(side)
                if more[tile]:
                    value = value + sum_ref[to[tile], columns]
                if last and (chunk == 1 or tile not in group_tiles(1, group)):
                    block, part = divmod(tile - window[0], BS // TILE)
                    out = outs[block]
                    out[at_tile(part), columns] = value.astype(out.dtype)
                else:
                    sum_ref[to[tile], columns] = value

            for tile in tiles:
                store(tile, 1, nn(ds_ref[at[tile], lanes], dout))
            for side in range(2):
                here = head_lanes(2 * pair + side)
                row = first + side * CHUNK
                for tile in tiles:
                    dp = nt(window_tile(values, tile, VALUE), dout[at_tile(side), :])
                    prob = ds_ref[at[tile], here].astype(jnp.float32)
                    ds_ref[at[tile], here] = (
                        prob * (dp - delta_ref[:1, row : row + CHUNK])
                    ).astype(jnp.bfloat16)
            for tile in tiles:
                store(tile, 0, nn(ds_ref[at[tile], lanes], queries) * SCALE)


def main(group, queries, dout, delta, values, e):
    blocks = 1 if group == "own" else 2
    shapes = [jax.ShapeDtypeStruct(x.shape, x.dtype) for x in e]
    kind = jnp.float32 if group == "own" else jnp.bfloat16
    shapes += [jax.ShapeDtypeStruct((BS, 2 * HEAD_WIDTH), kind)] * blocks
    args = [queries, dout, delta, *values, *e]
    tiles = sum(len(group_tiles(chunk, group)) for chunk in range(2))
    return pl.pallas_call(
        functools.partial(main_kernel, group),
        in_specs=[WHOLE] * len(args),
        out_specs=[WHOLE] * len(shapes),
        out_shape=shapes,
        scratch_shapes=[pltpu.VMEM((blocks * BS, 2 * HEAD_WIDTH), jnp.float32)],
        input_output_aliases={len(args) - 2: 0, len(args) - 1: 1},
        compiler_params=pltpu.CompilerParams(vmem_limit_bytes=6 * MIB),
        cost_estimate=pl.CostEstimate(
            flops=2 * 3 * LANES * tiles * TILE * HEAD_WIDTH,
            bytes_accessed=4 * MIB,
            transcendentals=0,
        ),
        name=f"main_{group}",
    )(*args)


def query_kernel(far_ref, two_ref, one_ref, here_ref, *refs):
    far_ds, near_ds, (out_ref, k_scr) = refs[:2], refs[2:4], refs[4:]
    keys = (far_ref, two_ref, one_ref, here_ref)
    window = (BEHIND + BS) // TILE
    for tile in range(window):
        k_scr[at_tile(tile), :] = window_tile(keys, tile, KEY)
    for chunk in range(2):
        rows = slice(chunk * CHUNK, (chunk + 1) * CHUNK)
        end = (BEHIND // TILE + chunk + 1) * TILE
        for head in range(HEADS):
            lanes = head_lanes(head)
            grad = tn(k_scr[chunk * TILE : EDGE * TILE, :], far_ds[chunk][:, lanes])
            grad = grad + tn(k_scr[EDGE * TILE : end, :], near_ds[chunk][:, lanes])
            out_ref[rows, head_columns(head)] = (jnp.transpose(grad) * SCALE).astype(jnp.bfloat16)


def query_grad(keys, ds):
    return pl.pallas_call(
        query_kernel,
        in_specs=[WHOLE] * (len(keys) + len(ds)),
        out_specs=WHOLE,
        out_shape=jax.ShapeDtypeStruct((BS, WIDTH), jnp.bfloat16),
        scratch_shapes=[pltpu.VMEM((BEHIND + BS, HEAD_WIDTH), jnp.bfloat16)],
        compiler_params=pltpu.CompilerParams(vmem_limit_bytes=6 * MIB),
        cost_estimate=pl.CostEstimate(
            flops=4 * LANES * 9 * TILE * HEAD_WIDTH, bytes_accessed=MIB, transcendentals=0
        ),
        name="query_grad",
    )(*keys, *ds)


def close_kernel(mine_ref, two_ref, one_ref, dk_ref, dv_ref):
    total = mine_ref[...] + two_ref[...].astype(jnp.float32) + one_ref[...].astype(jnp.float32)
    dk_ref[...] = total[:, :HEAD_WIDTH].astype(jnp.bfloat16)
    dv_ref[...] = total[:, HEAD_WIDTH:].astype(jnp.bfloat16)


def close(mine, two, one):
    return pl.pallas_call(
        close_kernel,
        in_specs=[WHOLE] * 3,
        out_specs=[WHOLE] * 2,
        out_shape=[jax.ShapeDtypeStruct((BS, HEAD_WIDTH), jnp.bfloat16)] * 2,
        compiler_params=pltpu.CompilerParams(vmem_limit_bytes=6 * MIB),
        name="close",
    )(mine, two, one)


def body(queries, keys, values, attn_out, out_grad, out_weight, segment):
    device = lax.axis_index("cp")
    where = jnp.stack([device, lax.axis_index("hd")]).astype(jnp.int32)
    segments = segment.reshape(128, -1)

    barrier = lax.optimization_barrier

    low, high, here = fetch_first(out_grad, keys, values)
    one, two = shifted(here, "cp", 1), shifted(here, "cp", 2)
    prev_low, next_high = shifted(low, "hd", 1), shifted(high, "hd", -1)
    queries, segments = fetch(queries, segments)
    partial = dout_own(where, out_weight, low, high)
    far = shifted(stack(one, two), "cp", 2)
    partial, low, high, here = barrier((partial, low, high, here))
    prev_high, next_low = shifted(high, "hd", 1), shifted(low, "hd", -1)

    *near_zero, weight_prev = stats(
        0, True, where, segments, queries, (two, one, here), (out_weight,), (3,)
    )
    prev_low, next_high, near_zero = barrier((prev_low, next_high, near_zero))
    far_low, far_high = shifted(prev_low, "hd", 1), shifted(next_high, "hd", -1)
    *near_one, weight_next, weight_last = stats(
        1, True, where, segments, queries, (two, one, here), (out_weight,), (1, 2)
    )
    e_near = [near_zero[0], near_one[0]]
    far_zero, near_inv_zero, far_inv_zero, partial = stats(
        0, False, where, segments, queries, (far,),
        (*near_zero[1:], prev_low, prev_high, weight_prev, partial),
    )
    far_one, near_inv_one, far_inv_one, partial = stats(
        1, False, where, segments, queries, (far,),
        (*near_one[1:], next_low, next_high, weight_next, partial),
    )
    dout_n, delta_n, dout_f, delta_f = dout_last(
        (far_low, far_high), weight_last, partial, attn_out,
        (near_inv_zero, near_inv_one), (far_inv_zero, far_inv_one),
    )
    *ds_far, to_four, to_three = main("far", queries, dout_f, delta_f, (far,), (far_zero, far_one))
    back = swapped(to_three)
    to_four = add_where(1, where, to_four, back)
    to_four, dout_n = barrier((to_four, dout_n))
    from_four = shifted(to_four, "cp", -4)
    *ds_near, to_two, to_one = main("mid", queries, dout_n, delta_n, (two, one), e_near)
    to_two = add_where(0, where, to_two, back)
    to_one, to_two, ds_near = barrier((to_one, to_two, ds_near))
    from_one, from_two = shifted(to_one, "cp", -1), shifted(to_two, "cp", -2)
    *ds_near, mine = main("own", queries, dout_n, delta_n, (here,), ds_near)
    mine, ds_near = barrier((add_where(None, where, mine, from_four), ds_near))
    query_out = query_grad((far, two, one, here), (*ds_far, *ds_near))
    mine, query_out = barrier((mine, query_out))
    dk, dv = close(mine, from_two, from_one)
    return query_out, dk, dv


def solution(mesh):
    return jax.shard_map(
        body,
        mesh=mesh,
        in_specs=(
            P("cp", "hd"),
            P("cp", "hd"),
            P("cp", "hd"),
            P("cp", "hd"),
            P("cp", "hd"),
            P("hd", None),
            P(),
        ),
        out_specs=(P("cp", "hd"), P("cp", "hd"), P("cp", "hd")),
        check_vma=False,
    )
```

```python
import functools

import jax
import jax.numpy as jnp
from jax import lax
from jax.experimental import pallas as pl
from jax.experimental.pallas import tpu as pltpu
from jax.sharding import PartitionSpec as P

HEAD_WIDTH = 128
HEADS = 8
BS = 512
MOST_BLK = 4
BEHIND = MOST_BLK * BS
TILE = 256
CHUNK = 256
EDGE = 4
LANES = HEADS * CHUNK
WIDTH = HEADS * HEAD_WIDTH
SCALE = HEAD_WIDTH ** (-0.5)
LOG2E = 1.4426950408889634
HIDDEN = -1e30
MIB = 2**20
DOCS = 16
BAND = 2 * HEAD_WIDTH
KEY = slice(0, HEAD_WIDTH)
VALUE = slice(HEAD_WIDTH, 2 * HEAD_WIDTH)
WHOLE = pl.BlockSpec(memory_space=pltpu.VMEM)
IN_HBM = pl.BlockSpec(memory_space=pltpu.HBM)


def shifted(value, axis, by):
    length = lax.axis_size(axis)
    return lax.ppermute(value, axis, [(i, (i + by) % length) for i in range(length)])


def swapped(value):
    length = lax.axis_size("cp")
    return lax.ppermute(value, "cp", [(i, i ^ 1) for i in range(length)])


def in_hbm(value):
    return pltpu.with_memory_space_constraint(value, pltpu.HBM)


def nt(a, b):
    return lax.dot_general(a, b, (((1,), (1,)), ((), ())), preferred_element_type=jnp.float32)


def nn(a, b):
    return lax.dot_general(a, b, (((1,), (0,)), ((), ())), preferred_element_type=jnp.float32)


def tiles_of(chunk, near):
    last = BEHIND // TILE + chunk
    return range(EDGE, last + 1) if near else range(chunk, EDGE)


def window_tile(refs, tile, columns):
    far, two, one, here = refs
    block, part = divmod(tile, BS // TILE)
    ref, row = [(far, BS), (far, 0), (two, 0), (one, 0), (here, 0)][block]
    row = row + part * TILE
    return ref[row : row + TILE, columns]


def head_lanes(head):
    return slice(head * CHUNK, (head + 1) * CHUNK)


def head_columns(head):
    return slice(head * HEAD_WIDTH, (head + 1) * HEAD_WIDTH)


def at_tile(index):
    return slice(index * TILE, (index + 1) * TILE)


def pull(moves, sems, pieces):
    copies = []
    for source, target in moves:
        size = target.shape[0] // pieces
        for row in range(0, target.shape[0], size):
            at = pl.ds(row, size)
            copies.append(
                pltpu.make_async_copy(source.at[at], target.at[at], sems.at[len(copies)])
            )
    for copy in copies:
        copy.start()
    return copies


def fetch_first_kernel(grad_ref, key_ref, value_ref, low_ref, high_ref, both_ref, sems):
    moves = [
        (grad_ref.at[pl.ds(0, CHUNK)], low_ref),
        (grad_ref.at[pl.ds(CHUNK, CHUNK)], high_ref),
        (key_ref, both_ref.at[:, pl.ds(0, HEAD_WIDTH)]),
        (value_ref, both_ref.at[:, pl.ds(HEAD_WIDTH, HEAD_WIDTH)]),
    ]
    for copy in pull(moves, sems, 4):
        copy.wait()


def fetch_first(grad, keys, values):
    return pl.pallas_call(
        fetch_first_kernel,
        in_specs=[IN_HBM] * 3,
        out_specs=[WHOLE] * 3,
        out_shape=[
            jax.ShapeDtypeStruct((CHUNK, WIDTH), jnp.bfloat16),
            jax.ShapeDtypeStruct((CHUNK, WIDTH), jnp.bfloat16),
            jax.ShapeDtypeStruct((BS, 2 * HEAD_WIDTH), jnp.bfloat16),
        ],
        scratch_shapes=[pltpu.SemaphoreType.DMA((16,))],
        compiler_params=pltpu.CompilerParams(vmem_limit_bytes=2 * MIB),
        name="fetch_first",
    )(in_hbm(grad), in_hbm(keys), in_hbm(values))


def fetch_kernel(count, *refs):
    for copy in pull(list(zip(refs[:count], refs[count:-1], strict=True)), refs[-1], 4):
        copy.wait()


def fetch(*arrays):
    return pl.pallas_call(
        functools.partial(fetch_kernel, len(arrays)),
        in_specs=[IN_HBM] * len(arrays),
        out_specs=[WHOLE] * len(arrays),
        out_shape=[jax.ShapeDtypeStruct(x.shape, x.dtype) for x in arrays],
        scratch_shapes=[pltpu.SemaphoreType.DMA((4 * len(arrays),))],
        compiler_params=pltpu.CompilerParams(vmem_limit_bytes=2 * MIB),
        name="fetch",
    )(*(in_hbm(x) for x in arrays))


def stack_kernel(a_ref, b_ref, out_ref):
    out_ref[:BS, :] = a_ref[...]
    out_ref[BS:, :] = b_ref[...]


def stack(a, b):
    return pl.pallas_call(
        stack_kernel,
        in_specs=[WHOLE] * 2,
        out_specs=WHOLE,
        out_shape=jax.ShapeDtypeStruct((2 * BS, a.shape[1]), a.dtype),
        compiler_params=pltpu.CompilerParams(vmem_limit_bytes=2 * MIB),
        name="stack",
    )(a, b)


def add_kernel(parity, a_ref, b_ref, out_ref):
    extra = b_ref[...].astype(jnp.float32)
    counts = (lax.axis_index("cp") & 1) == parity
    total = a_ref[...].astype(jnp.float32) + jnp.where(counts, extra, jnp.zeros_like(extra))
    out_ref[...] = total.astype(out_ref.dtype)


def add_where(parity, a, b):
    return pl.pallas_call(
        functools.partial(add_kernel, parity),
        in_specs=[WHOLE, WHOLE],
        out_specs=WHOLE,
        out_shape=jax.ShapeDtypeStruct(a.shape, a.dtype),
        compiler_params=pltpu.CompilerParams(vmem_limit_bytes=4 * MIB),
        name="add_where",
    )(a, b)


def weight_columns(by):
    place = lax.rem(lax.axis_index("hd") + by, 4)
    return pl.ds(pl.multiple_of(place * WIDTH, WIDTH), WIDTH)


def dout_own_kernel(weight_ref, low_ref, high_ref, sum_ref, g_scr, w_scr, sems):
    copies = pull([(weight_ref.at[:, weight_columns(0)], w_scr)], sems, 16)
    g_scr[:CHUNK, :] = low_ref[...]
    g_scr[CHUNK:, :] = high_ref[...]
    for copy in copies:
        copy.wait()
    for i in range(HEADS // 2):
        at = slice(i * BAND, (i + 1) * BAND)
        sum_ref[:, at] = nt(g_scr[...], w_scr[at, :])


def dout_last_kernel(*refs):
    low_ref, high_ref, kept_ref, before_ref, attn_ref = refs[:5]
    inverse = {"near": refs[5:7], "far": refs[7:9]}
    outs = {"near": refs[9:11], "far": refs[11:13]}
    g_scr, a_scr, sem = refs[13:]
    attn = pltpu.make_async_copy(attn_ref, a_scr, sem)
    attn.start()
    g_scr[:CHUNK, :] = low_ref[...]
    g_scr[CHUNK:, :] = high_ref[...]
    for i in range(HEADS // 2):
        cols = slice(i * BAND, (i + 1) * BAND)
        whole = nt(g_scr[...], kept_ref[cols, :]) + before_ref[:, cols]
        if i == 0:
            attn.wait()
        for chunk in range(2):
            rows = slice(chunk * CHUNK, (chunk + 1) * CHUNK)
            dout = whole[rows, :].astype(jnp.bfloat16).astype(jnp.float32)
            product = jnp.transpose(dout * a_scr[rows, cols].astype(jnp.float32))
            for side in range(2):
                head = 2 * i + side
                delta = jnp.sum(product[head_columns(side), :], axis=0, keepdims=True)
                to = slice((chunk * HEADS + head) * CHUNK, (chunk * HEADS + head + 1) * CHUNK)
                for group in ("near", "far"):
                    inv = inverse[group][chunk][:1, head_lanes(head)]
                    down = jnp.transpose(jnp.broadcast_to(inv, (HEAD_WIDTH, CHUNK)))
                    dout_ref, delta_ref = outs[group]
                    dout_ref[to, :] = (dout[:, head_columns(side)] * down).astype(jnp.bfloat16)
                    delta_ref[:, to] = jnp.broadcast_to(delta * inv, (8, CHUNK))


def dout_own(weight, low, high):
    return pl.pallas_call(
        dout_own_kernel,
        in_specs=[IN_HBM, WHOLE, WHOLE],
        out_specs=WHOLE,
        out_shape=jax.ShapeDtypeStruct((BS, WIDTH), jnp.float32),
        scratch_shapes=[
            pltpu.VMEM((BS, WIDTH), jnp.bfloat16),
            pltpu.VMEM((WIDTH, WIDTH), jnp.bfloat16),
            pltpu.SemaphoreType.DMA((16,)),
        ],
        compiler_params=pltpu.CompilerParams(vmem_limit_bytes=6 * MIB),
        cost_estimate=pl.CostEstimate(
            flops=2 * BS * WIDTH * WIDTH, bytes_accessed=4 * MIB, transcendentals=0
        ),
        name="dout_own",
    )(in_hbm(weight), low, high)


def dout_last(pieces, kept, before, attn, near, far):
    shapes = [
        jax.ShapeDtypeStruct((2 * LANES, HEAD_WIDTH), jnp.bfloat16),
        jax.ShapeDtypeStruct((8, 2 * LANES), jnp.float32),
    ] * 2
    return pl.pallas_call(
        dout_last_kernel,
        in_specs=[*[WHOLE] * 4, IN_HBM, *[WHOLE] * 4],
        out_specs=[WHOLE] * 4,
        out_shape=shapes,
        scratch_shapes=[
            pltpu.VMEM((BS, WIDTH), jnp.bfloat16),
            pltpu.VMEM((BS, WIDTH), jnp.bfloat16),
            pltpu.SemaphoreType.DMA,
        ],
        compiler_params=pltpu.CompilerParams(vmem_limit_bytes=8 * MIB),
        cost_estimate=pl.CostEstimate(
            flops=2 * BS * WIDTH * WIDTH, bytes_accessed=8 * MIB, transcendentals=0
        ),
        name="dout_last",
    )(*pieces, kept, before, in_hbm(attn), *near, *far)


def stats_kernel(chunk, near, sides, segment_ref, q_ref, *refs):
    if near:
        keys = (None, *refs[:3])
        weight_ref, refs = refs[3], refs[4:]
        e_ref, out_a, out_b, *kept_refs, sems = refs
        moves = [
            (weight_ref.at[:, weight_columns(side)], kept)
            for side, kept in zip(sides, kept_refs, strict=True)
        ]
        copies = pull(moves, sems, 4)
    else:
        keys = (refs[0], None, None, None)
        top_ref, total_ref, low_ref, high_ref, kept_ref, before_ref = refs[1:7]
        e_ref, out_a, out_b, sum_ref = refs[7:]
    rows = slice(chunk * CHUNK, (chunk + 1) * CHUNK)
    factor = SCALE * LOG2E
    tiles = tiles_of(chunk, near)

    first = lax.axis_index("cp") * BS - BEHIND
    row = lax.broadcasted_iota(jnp.int32, (1, CHUNK), 1) + (BEHIND + chunk * CHUNK)
    start = jnp.zeros((1, CHUNK), jnp.int32) - first
    segments = segment_ref[...]
    for doc in range(1, DOCS):
        begin = jnp.sum((segments < doc).astype(jnp.int32), axis=(0, 1), keepdims=True) - first
        start = jnp.where(begin <= row, begin, start)

    def score(head, tile):
        s = nt(window_tile(keys, tile, KEY), q_ref[rows, head_columns(head)])
        key = lax.broadcasted_iota(jnp.int32, (TILE, CHUNK), 0)
        seen = key >= start - tile * TILE
        if near and tile == tiles[-1]:
            seen = seen & (key <= lax.broadcasted_iota(jnp.int32, (TILE, CHUNK), 1))
        return jnp.where(seen, s, HIDDEN)

    def highest(head, tile, top):
        most = jnp.max(score(head, tile).reshape(TILE // 8, 8, CHUNK), axis=0)
        return most if top is None else jnp.maximum(top, most)

    def weigh(head, tile, top, total):
        e = jnp.exp2(score(head, tile) * factor - top)
        e_ref[at_tile(tile - tiles[0]), head_lanes(head)] = e.astype(jnp.bfloat16)
        part = jnp.sum(e.reshape(TILE // 8, 8, CHUNK), axis=0)
        return part if total is None else total + part

    jobs = []
    if not near:
        for band in range(HEADS // 2):
            for part, piece_ref in enumerate((low_ref, high_ref)):
                columns = slice(band * BAND, (band + 1) * BAND)
                jobs.append((piece_ref, at_tile(part), columns))

    def work():
        piece_ref, at, columns = jobs.pop(0)
        sum_ref[at, columns] = before_ref[at, columns] + nt(piece_ref[...], kept_ref[columns, :])

    following = None
    for tile in tiles:
        following = highest(0, tile, following)
    for head in range(HEADS):
        top = jnp.max(following, axis=0, keepdims=True) * factor
        following = total = None
        for tile in tiles:
            if head + 1 < HEADS:
                following = highest(head + 1, tile, following)
            total = weigh(head, tile, top, total)
        if jobs:
            work()
        total = jnp.sum(total, axis=0, keepdims=True)
        lanes = head_lanes(head)
        if near:
            out_a[:, lanes] = jnp.broadcast_to(top, (8, CHUNK))
            out_b[:, lanes] = jnp.broadcast_to(total, (8, CHUNK))
        else:
            other_top, other_total = top_ref[:1, lanes], total_ref[:1, lanes]
            most = jnp.maximum(top, other_top)
            near_part, far_part = jnp.exp2(other_top - most), jnp.exp2(top - most)
            inverse = 1.0 / (near_part * other_total + far_part * total)
            out_a[:, lanes] = jnp.broadcast_to(near_part * inverse, (8, CHUNK))
            out_b[:, lanes] = jnp.broadcast_to(far_part * inverse, (8, CHUNK))
    if near:
        for copy in copies:
            copy.wait()


def stats(chunk, near, segments, queries, keys, rest, sides=()):
    span = len(tiles_of(chunk, near)) * TILE
    args = [segments, queries, *keys, *rest]
    specs = [WHOLE] * len(args)
    shapes = [
        jax.ShapeDtypeStruct((span, LANES), jnp.bfloat16),
        jax.ShapeDtypeStruct((8, LANES), jnp.float32),
        jax.ShapeDtypeStruct((8, LANES), jnp.float32),
    ]
    scratch = []
    if near:
        specs[-1], args[-1] = IN_HBM, in_hbm(args[-1])
        shapes += [jax.ShapeDtypeStruct((WIDTH, WIDTH), jnp.bfloat16)] * len(sides)
        scratch.append(pltpu.SemaphoreType.DMA((4 * len(sides),)))
    else:
        shapes.append(jax.ShapeDtypeStruct((BS, WIDTH), jnp.float32))
    return pl.pallas_call(
        functools.partial(stats_kernel, chunk, near, sides),
        in_specs=specs,
        out_specs=[WHOLE] * len(shapes),
        out_shape=shapes,
        scratch_shapes=scratch,
        compiler_params=pltpu.CompilerParams(vmem_limit_bytes=6 * MIB),
        cost_estimate=pl.CostEstimate(
            flops=4 * LANES * span * HEAD_WIDTH,
            bytes_accessed=4 * MIB,
            transcendentals=LANES * span,
        ),
        name=f"stats{chunk}{'near' if near else 'far'}",
    )(*args)


def group_tiles(chunk, group):
    begin, end = {"four": (0, 2), "three": (2, 4), "mid": (4, 8), "own": (8, 10)}[group]
    seen = (*tiles_of(chunk, False), *tiles_of(chunk, True))
    return [tile for tile in seen if begin <= tile < end]


def main_kernel(group, q_ref, dout_ref, delta_ref, *refs):
    values = {
        "four": lambda: (refs[0], None, None, None),
        "three": lambda: (refs[0], None, None, None),
        "mid": lambda: (None, refs[0], refs[1], None),
        "own": lambda: (None, None, None, refs[0]),
    }[group]()
    refs = refs[2 if group == "mid" else 1 :]
    if group == "mid":
        back_ref, refs = refs[0], refs[1:]
    refs = refs[2:]
    ds_refs, outs, sum_ref = refs[:2], refs[2:-1], refs[-1]
    begun = set()
    window = group_tiles(0, group)
    window = list(range(window[0], window[0] + (4 if group == "mid" else 2)))
    for chunk in range(2):
        tiles = group_tiles(chunk, group)
        base = tiles_of(chunk, group in ("mid", "own"))[0]
        ds_ref = ds_refs[chunk]
        for pair in range(HEADS // 2):
            lanes = slice(2 * pair * CHUNK, 2 * (pair + 1) * CHUNK)
            first = (chunk * HEADS + 2 * pair) * CHUNK
            dout = dout_ref[first : first + 2 * CHUNK, :]
            queries = jnp.concatenate(
                [
                    q_ref[chunk * CHUNK : (chunk + 1) * CHUNK, head_columns(2 * pair + side)]
                    for side in range(2)
                ],
                axis=0,
            )
            at = {tile: at_tile(tile - base) for tile in tiles}
            to = {tile: at_tile(tile - window[0]) for tile in tiles}
            more = {tile: tile in begun for tile in tiles}
            begun.update(tiles)
            last = pair == HEADS // 2 - 1

            def store(tile, side, value):
                columns = head_columns(side)
                if more[tile]:
                    value = value + sum_ref[to[tile], columns]
                if last and (chunk == 1 or tile not in group_tiles(1, group)):
                    block, part = divmod(tile - window[0], BS // TILE)
                    out = outs[block]
                    if group == "mid" and block == 0:
                        extra = back_ref[at_tile(part), columns].astype(jnp.float32)
                        even = (lax.axis_index("cp") & 1) == 0
                        value = value + jnp.where(even, extra, jnp.zeros_like(extra))
                    out[at_tile(part), columns] = value.astype(out.dtype)
                else:
                    sum_ref[to[tile], columns] = value

            for tile in tiles:
                store(tile, 1, nn(ds_ref[at[tile], lanes], dout))
            for side in range(2):
                here = head_lanes(2 * pair + side)
                row = first + side * CHUNK
                for tile in tiles:
                    dp = nt(window_tile(values, tile, VALUE), dout[at_tile(side), :])
                    prob = ds_ref[at[tile], here].astype(jnp.float32)
                    ds_ref[at[tile], here] = (
                        prob * (dp - delta_ref[:1, row : row + CHUNK])
                    ).astype(jnp.bfloat16)
            for tile in tiles:
                store(tile, 0, nn(ds_ref[at[tile], lanes], queries) * SCALE)


def main(group, queries, dout, delta, values, e, back=()):
    blocks = 2 if group == "mid" else 1
    shapes = [jax.ShapeDtypeStruct(x.shape, x.dtype) for x in e]
    kind = jnp.float32 if group == "own" else jnp.bfloat16
    shapes += [jax.ShapeDtypeStruct((BS, 2 * HEAD_WIDTH), kind)] * blocks
    args = [queries, dout, delta, *values, *back, *e]
    tiles = sum(len(group_tiles(chunk, group)) for chunk in range(2))
    return pl.pallas_call(
        functools.partial(main_kernel, group),
        in_specs=[WHOLE] * len(args),
        out_specs=[WHOLE] * len(shapes),
        out_shape=shapes,
        scratch_shapes=[pltpu.VMEM((blocks * BS, 2 * HEAD_WIDTH), jnp.float32)],
        input_output_aliases={len(args) - 2: 0, len(args) - 1: 1},
        compiler_params=pltpu.CompilerParams(vmem_limit_bytes=6 * MIB),
        cost_estimate=pl.CostEstimate(
            flops=2 * 3 * LANES * tiles * TILE * HEAD_WIDTH,
            bytes_accessed=4 * MIB,
            transcendentals=0,
        ),
        name=f"main_{group}",
    )(*args)


def query_kernel(far_ref, two_ref, one_ref, here_ref, *refs):
    far_ds, near_ds, (out_ref, k_scr) = refs[:2], refs[2:4], refs[4:]
    keys = (far_ref, two_ref, one_ref, here_ref)
    window = (BEHIND + BS) // TILE
    for tile in range(window):
        k_scr[:, at_tile(tile)] = jnp.transpose(window_tile(keys, tile, KEY))
    for chunk in range(2):
        rows = slice(chunk * CHUNK, (chunk + 1) * CHUNK)
        end = (BEHIND // TILE + chunk + 1) * TILE
        for head in range(HEADS):
            lanes = head_lanes(head)
            grad = nn(k_scr[:, chunk * TILE : EDGE * TILE], far_ds[chunk][:, lanes])
            grad = grad + nn(k_scr[:, EDGE * TILE : end], near_ds[chunk][:, lanes])
            out_ref[rows, head_columns(head)] = (jnp.transpose(grad) * SCALE).astype(jnp.bfloat16)


def query_grad(keys, ds):
    return pl.pallas_call(
        query_kernel,
        in_specs=[WHOLE] * (len(keys) + len(ds)),
        out_specs=WHOLE,
        out_shape=jax.ShapeDtypeStruct((BS, WIDTH), jnp.bfloat16),
        scratch_shapes=[pltpu.VMEM((HEAD_WIDTH, BEHIND + BS), jnp.bfloat16)],
        compiler_params=pltpu.CompilerParams(vmem_limit_bytes=6 * MIB),
        cost_estimate=pl.CostEstimate(
            flops=4 * LANES * 9 * TILE * HEAD_WIDTH, bytes_accessed=MIB, transcendentals=0
        ),
        name="query_grad",
    )(*keys, *ds)


def close_kernel(mine_ref, four_ref, two_ref, one_ref, dk_ref, dv_ref):
    total = mine_ref[...] + four_ref[...].astype(jnp.float32)
    total = total + two_ref[...].astype(jnp.float32) + one_ref[...].astype(jnp.float32)
    dk_ref[...] = total[:, :HEAD_WIDTH].astype(jnp.bfloat16)
    dv_ref[...] = total[:, HEAD_WIDTH:].astype(jnp.bfloat16)


def close(mine, four, two, one):
    return pl.pallas_call(
        close_kernel,
        in_specs=[WHOLE] * 4,
        out_specs=[WHOLE] * 2,
        out_shape=[jax.ShapeDtypeStruct((BS, HEAD_WIDTH), jnp.bfloat16)] * 2,
        compiler_params=pltpu.CompilerParams(vmem_limit_bytes=6 * MIB),
        name="close",
    )(mine, four, two, one)


def body(queries, keys, values, attn_out, out_grad, out_weight, segment):
    segments = segment.reshape(128, -1)

    barrier = lax.optimization_barrier

    low, high, here = fetch_first(out_grad, keys, values)
    prev_low, next_high = shifted(low, "hd", 1), shifted(high, "hd", -1)
    one, two = shifted(here, "cp", 1), shifted(here, "cp", 2)
    here, queries_in = barrier((here, queries))
    queries, segments = fetch(queries_in, segments)
    queries, weight_in = barrier((queries, out_weight))
    partial = dout_own(weight_in, low, high)
    one, two, partial, here, low, high = barrier((one, two, partial, here, low, high))
    far = shifted(stack(one, two), "cp", 2)
    prev_high, next_low = shifted(high, "hd", 1), shifted(low, "hd", -1)

    near = (two, one, here)
    *near_one, weight_next, weight_last = stats(
        1, True, segments, queries, near, (out_weight,), (1, 2)
    )
    prev_low, next_high, near_one, two = barrier((prev_low, next_high, near_one, two))
    far_low, far_high = shifted(prev_low, "hd", 1), shifted(next_high, "hd", -1)
    *near_zero, weight_prev = stats(
        0, True, segments, queries, (two, one, here), (out_weight,), (3,)
    )
    e_near = [near_zero[0], near_one[0]]
    prev_high, next_low, near_zero = barrier((prev_high, next_low, near_zero))
    far_zero, near_inv_zero, far_inv_zero, partial = stats(
        0, False, segments, queries, (far,),
        (*near_zero[1:], prev_low, prev_high, weight_prev, partial),
    )
    far_one, near_inv_one, far_inv_one, partial = stats(
        1, False, segments, queries, (far,),
        (*near_one[1:], next_low, next_high, weight_next, partial),
    )
    dout_n, delta_n, dout_f, delta_f = dout_last(
        (far_low, far_high), weight_last, partial, attn_out,
        (near_inv_zero, near_inv_one), (far_inv_zero, far_inv_one),
    )
    *ds_far, to_three = main(
        "three", queries, dout_f, delta_f, (far,), (far_zero, far_one)
    )
    back = swapped(to_three)
    *ds_far, to_four = main("four", queries, dout_f, delta_f, (far,), ds_far)
    to_four = add_where(1, to_four, back)
    to_four, dout_n = barrier((to_four, dout_n))
    from_four = shifted(to_four, "cp", -4)
    *ds_near, to_two, to_one = main(
        "mid", queries, dout_n, delta_n, (two, one), e_near, (back,)
    )
    to_one, to_two, ds_near = barrier((to_one, to_two, ds_near))
    from_one, from_two = shifted(to_one, "cp", -1), shifted(to_two, "cp", -2)
    *ds_near, mine = main("own", queries, dout_n, delta_n, (here,), ds_near)
    from_four, ds_near = barrier((from_four, ds_near))
    query_out = query_grad((far, two, one, here), (*ds_far, *ds_near))
    mine, query_out = barrier((mine, query_out))
    dk, dv = close(mine, from_four, from_two, from_one)
    return query_out, dk, dv


def solution(mesh):
    return jax.shard_map(
        body,
        mesh=mesh,
        in_specs=(
            P("cp", "hd"),
            P("cp", "hd"),
            P("cp", "hd"),
            P("cp", "hd"),
            P("cp", "hd"),
            P("hd", None),
            P(),
        ),
        out_specs=(P("cp", "hd"), P("cp", "hd"), P("cp", "hd")),
        check_vma=False,
    )
```

```python
import functools

import jax
import jax.numpy as jnp
from jax import lax
from jax.experimental import pallas as pl
from jax.experimental.pallas import tpu as pltpu
from jax.sharding import PartitionSpec as P

HEAD_WIDTH = 128
HEADS = 8
BS = 512
MOST_BLK = 4
BEHIND = MOST_BLK * BS
TILE = 256
CHUNK = 256
EDGE = 4
LANES = HEADS * CHUNK
WIDTH = HEADS * HEAD_WIDTH
SCALE = HEAD_WIDTH ** (-0.5)
LOG2E = 1.4426950408889634
HIDDEN = -1e30
MIB = 2**20
DOCS = 16
MARKS = 128
NEVER = 1 << 28
BAND = 2 * HEAD_WIDTH
KEY = slice(0, HEAD_WIDTH)
VALUE = slice(HEAD_WIDTH, 2 * HEAD_WIDTH)
WHOLE = pl.BlockSpec(memory_space=pltpu.VMEM)
IN_HBM = pl.BlockSpec(memory_space=pltpu.HBM)


def shifted(value, axis, by):
    length = lax.axis_size(axis)
    return lax.ppermute(value, axis, [(i, (i + by) % length) for i in range(length)])


def swapped(value):
    length = lax.axis_size("cp")
    return lax.ppermute(value, "cp", [(i, i ^ 1) for i in range(length)])


def in_hbm(value):
    return pltpu.with_memory_space_constraint(value, pltpu.HBM)


def nt(a, b):
    return lax.dot_general(a, b, (((1,), (1,)), ((), ())), preferred_element_type=jnp.float32)


def nn(a, b):
    return lax.dot_general(a, b, (((1,), (0,)), ((), ())), preferred_element_type=jnp.float32)


def tiles_of(chunk, near):
    last = BEHIND // TILE + chunk
    return range(EDGE, last + 1) if near else range(chunk, EDGE)


def window_tile(refs, tile, columns):
    far, two, one, here = refs
    block, part = divmod(tile, BS // TILE)
    ref, row = [(far, BS), (far, 0), (two, 0), (one, 0), (here, 0)][block]
    row = row + part * TILE
    return ref[row : row + TILE, columns]


def head_lanes(head):
    return slice(head * CHUNK, (head + 1) * CHUNK)


def head_columns(head):
    return slice(head * HEAD_WIDTH, (head + 1) * HEAD_WIDTH)


def at_tile(index):
    return slice(index * TILE, (index + 1) * TILE)


def pull(moves, sems, pieces):
    copies = []
    for source, target in moves:
        size = target.shape[0] // pieces
        for row in range(0, target.shape[0], size):
            at = pl.ds(row, size)
            copies.append(
                pltpu.make_async_copy(source.at[at], target.at[at], sems.at[len(copies)])
            )
    for copy in copies:
        copy.start()
    return copies


def fetch_first_kernel(grad_ref, key_ref, value_ref, low_ref, high_ref, both_ref, sems):
    moves = [
        (grad_ref.at[pl.ds(0, CHUNK)], low_ref),
        (grad_ref.at[pl.ds(CHUNK, CHUNK)], high_ref),
        (key_ref, both_ref.at[:, pl.ds(0, HEAD_WIDTH)]),
        (value_ref, both_ref.at[:, pl.ds(HEAD_WIDTH, HEAD_WIDTH)]),
    ]
    for copy in pull(moves, sems, 4):
        copy.wait()


def fetch_first(grad, keys, values):
    return pl.pallas_call(
        fetch_first_kernel,
        in_specs=[IN_HBM] * 3,
        out_specs=[WHOLE] * 3,
        out_shape=[
            jax.ShapeDtypeStruct((CHUNK, WIDTH), jnp.bfloat16),
            jax.ShapeDtypeStruct((CHUNK, WIDTH), jnp.bfloat16),
            jax.ShapeDtypeStruct((BS, 2 * HEAD_WIDTH), jnp.bfloat16),
        ],
        scratch_shapes=[pltpu.SemaphoreType.DMA((16,))],
        compiler_params=pltpu.CompilerParams(vmem_limit_bytes=2 * MIB),
        name="fetch_first",
    )(in_hbm(grad), in_hbm(keys), in_hbm(values))


def fetch_kernel(q_ref, segment_ref, q_out, key_marks, query_marks, segments, sems):
    copies = pull([(q_ref, q_out), (segment_ref, segments)], sems, 4)
    for copy in copies[4:]:
        copy.wait()
    first = lax.axis_index("cp") * BS - BEHIND
    lane = lax.broadcasted_iota(jnp.int32, (1, MARKS), 1)
    low = jnp.where(lane == 0, 0, NEVER)
    high = jnp.where(lane == DOCS - 1, NEVER, -NEVER)
    for doc in range(1, DOCS):
        begin = jnp.sum((segments[...] < doc).astype(jnp.int32), axis=(0, 1), keepdims=True)
        low = jnp.where(lane == doc, begin, low)
        high = jnp.where(lane == doc - 1, begin, high)
    low = jnp.where(lane == DOCS, -NEVER, low) - first
    high = jnp.where(lane == DOCS, 0, high) - first

    def inside(rows, begin):
        place = lax.broadcasted_iota(jnp.int32, (rows, MARKS), 0) + begin
        return (place >= low) & (place < high)

    for tile in range((BEHIND + BS) // TILE):
        key_marks[at_tile(tile), :] = jnp.where(inside(TILE, tile * TILE), 1.0, 0.0).astype(
            jnp.bfloat16
        )
    query_marks[...] = jnp.where(inside(BS, BEHIND), 0.0, HIDDEN).astype(jnp.bfloat16)
    for copy in copies[:4]:
        copy.wait()


def fetch(queries, segments):
    return pl.pallas_call(
        fetch_kernel,
        in_specs=[IN_HBM] * 2,
        out_specs=[WHOLE] * 3,
        out_shape=[
            jax.ShapeDtypeStruct(queries.shape, queries.dtype),
            jax.ShapeDtypeStruct((BEHIND + BS, MARKS), jnp.bfloat16),
            jax.ShapeDtypeStruct((BS, MARKS), jnp.bfloat16),
        ],
        scratch_shapes=[
            pltpu.VMEM(segments.shape, segments.dtype),
            pltpu.SemaphoreType.DMA((8,)),
        ],
        compiler_params=pltpu.CompilerParams(vmem_limit_bytes=4 * MIB),
        name="fetch",
    )(in_hbm(queries), in_hbm(segments))


def stack_kernel(a_ref, b_ref, out_ref):
    out_ref[:BS, :] = a_ref[...]
    out_ref[BS:, :] = b_ref[...]


def stack(a, b):
    return pl.pallas_call(
        stack_kernel,
        in_specs=[WHOLE] * 2,
        out_specs=WHOLE,
        out_shape=jax.ShapeDtypeStruct((2 * BS, a.shape[1]), a.dtype),
        compiler_params=pltpu.CompilerParams(vmem_limit_bytes=2 * MIB),
        name="stack",
    )(a, b)


def add_kernel(parity, a_ref, b_ref, out_ref):
    extra = b_ref[...].astype(jnp.float32)
    counts = (lax.axis_index("cp") & 1) == parity
    total = a_ref[...].astype(jnp.float32) + jnp.where(counts, extra, jnp.zeros_like(extra))
    out_ref[...] = total.astype(out_ref.dtype)


def add_where(parity, a, b):
    return pl.pallas_call(
        functools.partial(add_kernel, parity),
        in_specs=[WHOLE, WHOLE],
        out_specs=WHOLE,
        out_shape=jax.ShapeDtypeStruct(a.shape, a.dtype),
        compiler_params=pltpu.CompilerParams(vmem_limit_bytes=4 * MIB),
        name="add_where",
    )(a, b)


def weight_columns(by):
    place = lax.rem(lax.axis_index("hd") + by, 4)
    return pl.ds(pl.multiple_of(place * WIDTH, WIDTH), WIDTH)


def dout_own_kernel(weight_ref, low_ref, high_ref, sum_ref, g_scr, w_scr, sems):
    copies = pull([(weight_ref.at[:, weight_columns(0)], w_scr)], sems, 16)
    g_scr[:CHUNK, :] = low_ref[...]
    g_scr[CHUNK:, :] = high_ref[...]
    for copy in copies:
        copy.wait()
    for i in range(HEADS // 2):
        at = slice(i * BAND, (i + 1) * BAND)
        sum_ref[:, at] = nt(g_scr[...], w_scr[at, :])


def dout_last_kernel(*refs):
    low_ref, high_ref, kept_ref, before_ref, attn_ref = refs[:5]
    inverse = {"near": refs[5:7], "far": refs[7:9]}
    outs = {"near": refs[9:11], "far": refs[11:13]}
    g_scr, a_scr, sem = refs[13:]
    attn = pltpu.make_async_copy(attn_ref, a_scr, sem)
    attn.start()
    g_scr[:CHUNK, :] = low_ref[...]
    g_scr[CHUNK:, :] = high_ref[...]
    for i in range(HEADS // 2):
        cols = slice(i * BAND, (i + 1) * BAND)
        whole = nt(g_scr[...], kept_ref[cols, :]) + before_ref[:, cols]
        if i == 0:
            attn.wait()
        for chunk in range(2):
            rows = slice(chunk * CHUNK, (chunk + 1) * CHUNK)
            dout = whole[rows, :].astype(jnp.bfloat16).astype(jnp.float32)
            product = jnp.transpose(dout * a_scr[rows, cols].astype(jnp.float32))
            for side in range(2):
                head = 2 * i + side
                delta = jnp.sum(product[head_columns(side), :], axis=0, keepdims=True)
                to = slice((chunk * HEADS + head) * CHUNK, (chunk * HEADS + head + 1) * CHUNK)
                for group in ("near", "far"):
                    inv = inverse[group][chunk][:1, head_lanes(head)]
                    down = jnp.transpose(jnp.broadcast_to(inv, (HEAD_WIDTH, CHUNK)))
                    dout_ref, delta_ref = outs[group]
                    dout_ref[to, :] = (dout[:, head_columns(side)] * down).astype(jnp.bfloat16)
                    delta_ref[:, to] = jnp.broadcast_to(delta * inv, (8, CHUNK))


def dout_own(weight, low, high):
    return pl.pallas_call(
        dout_own_kernel,
        in_specs=[IN_HBM, WHOLE, WHOLE],
        out_specs=WHOLE,
        out_shape=jax.ShapeDtypeStruct((BS, WIDTH), jnp.float32),
        scratch_shapes=[
            pltpu.VMEM((BS, WIDTH), jnp.bfloat16),
            pltpu.VMEM((WIDTH, WIDTH), jnp.bfloat16),
            pltpu.SemaphoreType.DMA((16,)),
        ],
        compiler_params=pltpu.CompilerParams(vmem_limit_bytes=6 * MIB),
        cost_estimate=pl.CostEstimate(
            flops=2 * BS * WIDTH * WIDTH, bytes_accessed=4 * MIB, transcendentals=0
        ),
        name="dout_own",
    )(in_hbm(weight), low, high)


def dout_last(pieces, kept, before, attn, near, far):
    shapes = [
        jax.ShapeDtypeStruct((2 * LANES, HEAD_WIDTH), jnp.bfloat16),
        jax.ShapeDtypeStruct((8, 2 * LANES), jnp.float32),
    ] * 2
    return pl.pallas_call(
        dout_last_kernel,
        in_specs=[*[WHOLE] * 4, IN_HBM, *[WHOLE] * 4],
        out_specs=[WHOLE] * 4,
        out_shape=shapes,
        scratch_shapes=[
            pltpu.VMEM((BS, WIDTH), jnp.bfloat16),
            pltpu.VMEM((BS, WIDTH), jnp.bfloat16),
            pltpu.SemaphoreType.DMA,
        ],
        compiler_params=pltpu.CompilerParams(vmem_limit_bytes=8 * MIB),
        cost_estimate=pl.CostEstimate(
            flops=2 * BS * WIDTH * WIDTH, bytes_accessed=8 * MIB, transcendentals=0
        ),
        name="dout_last",
    )(*pieces, kept, before, in_hbm(attn), *near, *far)


def stats_kernel(chunk, near, sides, key_marks, query_marks, q_ref, *refs):
    if near:
        keys = (None, *refs[:3])
        weight_ref, refs = refs[3], refs[4:]
        e_ref, out_a, out_b, *kept_refs, sems = refs
        moves = [
            (weight_ref.at[:, weight_columns(side)], kept)
            for side, kept in zip(sides, kept_refs, strict=True)
        ]
        copies = pull(moves, sems, 4)
    else:
        keys = (refs[0], None, None, None)
        top_ref, total_ref, low_ref, high_ref, kept_ref, before_ref = refs[1:7]
        e_ref, out_a, out_b, sum_ref = refs[7:]
    rows = slice(chunk * CHUNK, (chunk + 1) * CHUNK)
    factor = SCALE * LOG2E
    tiles = tiles_of(chunk, near)

    def score(head, tile):
        keyed = jnp.concatenate([window_tile(keys, tile, KEY), key_marks[at_tile(tile), :]], axis=1)
        asked = jnp.concatenate([q_ref[rows, head_columns(head)], query_marks[rows, :]], axis=1)
        s = nt(keyed, asked)
        if near and tile == tiles[-1]:
            key = lax.broadcasted_iota(jnp.int32, (TILE, CHUNK), 0)
            s = jnp.where(key <= lax.broadcasted_iota(jnp.int32, (TILE, CHUNK), 1), s, HIDDEN)
        return s

    def highest(head, tile, top):
        most = jnp.max(score(head, tile).reshape(TILE // 8, 8, CHUNK), axis=0)
        return most if top is None else jnp.maximum(top, most)

    def weigh(head, tile, top, total):
        e = jnp.exp2(score(head, tile) * factor - top)
        e_ref[at_tile(tile - tiles[0]), head_lanes(head)] = e.astype(jnp.bfloat16)
        part = jnp.sum(e.reshape(TILE // 8, 8, CHUNK), axis=0)
        return part if total is None else total + part

    jobs = []
    if not near:
        for band in range(HEADS // 2):
            for part, piece_ref in enumerate((low_ref, high_ref)):
                columns = slice(band * BAND, (band + 1) * BAND)
                jobs.append((piece_ref, at_tile(part), columns))

    def work():
        piece_ref, at, columns = jobs.pop(0)
        sum_ref[at, columns] = before_ref[at, columns] + nt(piece_ref[...], kept_ref[columns, :])

    following = None
    for tile in tiles:
        following = highest(0, tile, following)
    for head in range(HEADS):
        top = jnp.max(following, axis=0, keepdims=True) * factor
        following = total = None
        for tile in tiles:
            if head + 1 < HEADS:
                following = highest(head + 1, tile, following)
            total = weigh(head, tile, top, total)
        if jobs:
            work()
        total = jnp.sum(total, axis=0, keepdims=True)
        lanes = head_lanes(head)
        if near:
            out_a[:, lanes] = jnp.broadcast_to(top, (8, CHUNK))
            out_b[:, lanes] = jnp.broadcast_to(total, (8, CHUNK))
        else:
            other_top, other_total = top_ref[:1, lanes], total_ref[:1, lanes]
            most = jnp.maximum(top, other_top)
            near_part, far_part = jnp.exp2(other_top - most), jnp.exp2(top - most)
            inverse = 1.0 / (near_part * other_total + far_part * total)
            out_a[:, lanes] = jnp.broadcast_to(near_part * inverse, (8, CHUNK))
            out_b[:, lanes] = jnp.broadcast_to(far_part * inverse, (8, CHUNK))
    if near:
        for copy in copies:
            copy.wait()


def stats(chunk, near, marks, queries, keys, rest, sides=()):
    span = len(tiles_of(chunk, near)) * TILE
    args = [*marks, queries, *keys, *rest]
    specs = [WHOLE] * len(args)
    shapes = [
        jax.ShapeDtypeStruct((span, LANES), jnp.bfloat16),
        jax.ShapeDtypeStruct((8, LANES), jnp.float32),
        jax.ShapeDtypeStruct((8, LANES), jnp.float32),
    ]
    scratch = []
    if near:
        specs[-1], args[-1] = IN_HBM, in_hbm(args[-1])
        shapes += [jax.ShapeDtypeStruct((WIDTH, WIDTH), jnp.bfloat16)] * len(sides)
        scratch.append(pltpu.SemaphoreType.DMA((4 * len(sides),)))
    else:
        shapes.append(jax.ShapeDtypeStruct((BS, WIDTH), jnp.float32))
    return pl.pallas_call(
        functools.partial(stats_kernel, chunk, near, sides),
        in_specs=specs,
        out_specs=[WHOLE] * len(shapes),
        out_shape=shapes,
        scratch_shapes=scratch,
        compiler_params=pltpu.CompilerParams(vmem_limit_bytes=6 * MIB),
        cost_estimate=pl.CostEstimate(
            flops=4 * LANES * span * HEAD_WIDTH,
            bytes_accessed=4 * MIB,
            transcendentals=LANES * span,
        ),
        name=f"stats{chunk}{'near' if near else 'far'}",
    )(*args)


def group_tiles(chunk, group):
    begin, end = {"four": (0, 2), "three": (2, 4), "mid": (4, 8), "own": (8, 10)}[group]
    seen = (*tiles_of(chunk, False), *tiles_of(chunk, True))
    return [tile for tile in seen if begin <= tile < end]


def main_kernel(group, q_ref, dout_ref, delta_ref, *refs):
    values = {
        "four": lambda: (refs[0], None, None, None),
        "three": lambda: (refs[0], None, None, None),
        "mid": lambda: (None, refs[0], refs[1], None),
        "own": lambda: (None, None, None, refs[0]),
    }[group]()
    refs = refs[2 if group == "mid" else 1 :]
    if group == "mid":
        back_ref, refs = refs[0], refs[1:]
    refs = refs[2:]
    ds_refs, outs, sum_ref = refs[:2], refs[2:-1], refs[-1]
    begun = set()
    window = group_tiles(0, group)
    window = list(range(window[0], window[0] + (4 if group == "mid" else 2)))
    for chunk in range(2):
        tiles = group_tiles(chunk, group)
        base = tiles_of(chunk, group in ("mid", "own"))[0]
        ds_ref = ds_refs[chunk]
        for pair in range(HEADS // 2):
            lanes = slice(2 * pair * CHUNK, 2 * (pair + 1) * CHUNK)
            first = (chunk * HEADS + 2 * pair) * CHUNK
            dout = dout_ref[first : first + 2 * CHUNK, :]
            queries = jnp.concatenate(
                [
                    q_ref[chunk * CHUNK : (chunk + 1) * CHUNK, head_columns(2 * pair + side)]
                    for side in range(2)
                ],
                axis=0,
            )
            at = {tile: at_tile(tile - base) for tile in tiles}
            to = {tile: at_tile(tile - window[0]) for tile in tiles}
            more = {tile: tile in begun for tile in tiles}
            begun.update(tiles)
            last = pair == HEADS // 2 - 1

            def store(tile, side, value):
                columns = head_columns(side)
                if more[tile]:
                    value = value + sum_ref[to[tile], columns]
                if last and (chunk == 1 or tile not in group_tiles(1, group)):
                    block, part = divmod(tile - window[0], BS // TILE)
                    out = outs[block]
                    if group == "mid" and block == 0:
                        extra = back_ref[at_tile(part), columns].astype(jnp.float32)
                        even = (lax.axis_index("cp") & 1) == 0
                        value = value + jnp.where(even, extra, jnp.zeros_like(extra))
                    out[at_tile(part), columns] = value.astype(out.dtype)
                else:
                    sum_ref[to[tile], columns] = value

            for tile in tiles:
                store(tile, 1, nn(ds_ref[at[tile], lanes], dout))
            for side in range(2):
                here = head_lanes(2 * pair + side)
                row = first + side * CHUNK
                for tile in tiles:
                    dp = nt(window_tile(values, tile, VALUE), dout[at_tile(side), :])
                    prob = ds_ref[at[tile], here].astype(jnp.float32)
                    ds_ref[at[tile], here] = (
                        prob * (dp - delta_ref[:1, row : row + CHUNK])
                    ).astype(jnp.bfloat16)
            for tile in tiles:
                store(tile, 0, nn(ds_ref[at[tile], lanes], queries) * SCALE)


def main(group, queries, dout, delta, values, e, back=()):
    blocks = 2 if group == "mid" else 1
    shapes = [jax.ShapeDtypeStruct(x.shape, x.dtype) for x in e]
    kind = jnp.float32 if group == "own" else jnp.bfloat16
    shapes += [jax.ShapeDtypeStruct((BS, 2 * HEAD_WIDTH), kind)] * blocks
    args = [queries, dout, delta, *values, *back, *e]
    tiles = sum(len(group_tiles(chunk, group)) for chunk in range(2))
    return pl.pallas_call(
        functools.partial(main_kernel, group),
        in_specs=[WHOLE] * len(args),
        out_specs=[WHOLE] * len(shapes),
        out_shape=shapes,
        scratch_shapes=[pltpu.VMEM((blocks * BS, 2 * HEAD_WIDTH), jnp.float32)],
        input_output_aliases={len(args) - 2: 0, len(args) - 1: 1},
        compiler_params=pltpu.CompilerParams(vmem_limit_bytes=6 * MIB),
        cost_estimate=pl.CostEstimate(
            flops=2 * 3 * LANES * tiles * TILE * HEAD_WIDTH,
            bytes_accessed=4 * MIB,
            transcendentals=0,
        ),
        name=f"main_{group}",
    )(*args)


def query_kernel(far_ref, two_ref, one_ref, here_ref, *refs):
    far_ds, near_ds, (out_ref, k_scr) = refs[:2], refs[2:4], refs[4:]
    keys = (far_ref, two_ref, one_ref, here_ref)
    window = (BEHIND + BS) // TILE
    for tile in range(window):
        k_scr[:, at_tile(tile)] = jnp.transpose(window_tile(keys, tile, KEY))
    for chunk in range(2):
        rows = slice(chunk * CHUNK, (chunk + 1) * CHUNK)
        end = (BEHIND // TILE + chunk + 1) * TILE
        for head in range(HEADS):
            lanes = head_lanes(head)
            grad = nn(k_scr[:, chunk * TILE : EDGE * TILE], far_ds[chunk][:, lanes])
            grad = grad + nn(k_scr[:, EDGE * TILE : end], near_ds[chunk][:, lanes])
            out_ref[rows, head_columns(head)] = (jnp.transpose(grad) * SCALE).astype(jnp.bfloat16)


def query_grad(keys, ds):
    return pl.pallas_call(
        query_kernel,
        in_specs=[WHOLE] * (len(keys) + len(ds)),
        out_specs=WHOLE,
        out_shape=jax.ShapeDtypeStruct((BS, WIDTH), jnp.bfloat16),
        scratch_shapes=[pltpu.VMEM((HEAD_WIDTH, BEHIND + BS), jnp.bfloat16)],
        compiler_params=pltpu.CompilerParams(vmem_limit_bytes=6 * MIB),
        cost_estimate=pl.CostEstimate(
            flops=4 * LANES * 9 * TILE * HEAD_WIDTH, bytes_accessed=MIB, transcendentals=0
        ),
        name="query_grad",
    )(*keys, *ds)


def close_kernel(mine_ref, four_ref, two_ref, one_ref, dk_ref, dv_ref):
    total = mine_ref[...] + four_ref[...].astype(jnp.float32)
    total = total + two_ref[...].astype(jnp.float32) + one_ref[...].astype(jnp.float32)
    dk_ref[...] = total[:, :HEAD_WIDTH].astype(jnp.bfloat16)
    dv_ref[...] = total[:, HEAD_WIDTH:].astype(jnp.bfloat16)


def close(mine, four, two, one):
    return pl.pallas_call(
        close_kernel,
        in_specs=[WHOLE] * 4,
        out_specs=[WHOLE] * 2,
        out_shape=[jax.ShapeDtypeStruct((BS, HEAD_WIDTH), jnp.bfloat16)] * 2,
        compiler_params=pltpu.CompilerParams(vmem_limit_bytes=6 * MIB),
        name="close",
    )(mine, four, two, one)


def body(queries, keys, values, attn_out, out_grad, out_weight, segment):
    segments = segment.reshape(128, -1)

    barrier = lax.optimization_barrier

    low, high, here = fetch_first(out_grad, keys, values)
    prev_low, next_high = shifted(low, "hd", 1), shifted(high, "hd", -1)
    one, two = shifted(here, "cp", 1), shifted(here, "cp", 2)
    here, queries_in = barrier((here, queries))
    queries, *marks = fetch(queries_in, segments)
    queries, weight_in = barrier((queries, out_weight))
    partial = dout_own(weight_in, low, high)
    partial, here, low, high = barrier((partial, here, low, high))
    prev_high, next_low = shifted(high, "hd", 1), shifted(low, "hd", -1)
    one, two, partial = barrier((one, two, partial))
    far = shifted(stack(one, two), "cp", 2)

    near = (two, one, here)
    *near_one, weight_next, weight_last = stats(
        1, True, marks, queries, near, (out_weight,), (1, 2)
    )
    prev_low, next_high, near_one, two = barrier((prev_low, next_high, near_one, two))
    far_low, far_high = shifted(prev_low, "hd", 1), shifted(next_high, "hd", -1)
    *near_zero, weight_prev = stats(
        0, True, marks, queries, (two, one, here), (out_weight,), (3,)
    )
    e_near = [near_zero[0], near_one[0]]
    prev_high, next_low, near_zero = barrier((prev_high, next_low, near_zero))
    far_zero, near_inv_zero, far_inv_zero, partial = stats(
        0, False, marks, queries, (far,),
        (*near_zero[1:], prev_low, prev_high, weight_prev, partial),
    )
    far_one, near_inv_one, far_inv_one, partial = stats(
        1, False, marks, queries, (far,),
        (*near_one[1:], next_low, next_high, weight_next, partial),
    )
    dout_n, delta_n, dout_f, delta_f = dout_last(
        (far_low, far_high), weight_last, partial, attn_out,
        (near_inv_zero, near_inv_one), (far_inv_zero, far_inv_one),
    )
    *ds_far, to_three = main(
        "three", queries, dout_f, delta_f, (far,), (far_zero, far_one)
    )
    back = swapped(to_three)
    *ds_far, to_four = main("four", queries, dout_f, delta_f, (far,), ds_far)
    to_four = add_where(1, to_four, back)
    to_four, dout_n = barrier((to_four, dout_n))
    from_four = shifted(to_four, "cp", -4)
    *ds_near, to_two, to_one = main(
        "mid", queries, dout_n, delta_n, (two, one), e_near, (back,)
    )
    to_one, to_two, ds_near = barrier((to_one, to_two, ds_near))
    from_one, from_two = shifted(to_one, "cp", -1), shifted(to_two, "cp", -2)
    *ds_near, mine = main("own", queries, dout_n, delta_n, (here,), ds_near)
    from_four, ds_near = barrier((from_four, ds_near))
    query_out = query_grad((far, two, one, here), (*ds_far, *ds_near))
    mine, query_out = barrier((mine, query_out))
    dk, dv = close(mine, from_four, from_two, from_one)
    return query_out, dk, dv


def solution(mesh):
    return jax.shard_map(
        body,
        mesh=mesh,
        in_specs=(
            P("cp", "hd"),
            P("cp", "hd"),
            P("cp", "hd"),
            P("cp", "hd"),
            P("cp", "hd"),
            P("hd", None),
            P(),
        ),
        out_specs=(P("cp", "hd"), P("cp", "hd"), P("cp", "hd")),
        check_vma=False,
    )
```

```python
import functools

import jax
import jax.numpy as jnp
from jax import lax
from jax.experimental import pallas as pl
from jax.experimental.pallas import tpu as pltpu
from jax.sharding import PartitionSpec as P

HEAD_WIDTH = 128
HEADS = 8
BS = 512
MOST_BLK = 4
BEHIND = MOST_BLK * BS
TILE = 256
CHUNK = 256
EDGE = 4
LANES = HEADS * CHUNK
WIDTH = HEADS * HEAD_WIDTH
SCALE = HEAD_WIDTH ** (-0.5)
LOG2E = 1.4426950408889634
HIDDEN = -1e30
MIB = 2**20
DOCS = 16
MARKS = 128
NEVER = 1 << 28
BAND = 2 * HEAD_WIDTH
KEY = slice(0, HEAD_WIDTH)
VALUE = slice(HEAD_WIDTH, 2 * HEAD_WIDTH)
WHOLE = pl.BlockSpec(memory_space=pltpu.VMEM)
IN_HBM = pl.BlockSpec(memory_space=pltpu.HBM)


def shifted(value, axis, by):
    length = lax.axis_size(axis)
    return lax.ppermute(value, axis, [(i, (i + by) % length) for i in range(length)])


def swapped(value):
    length = lax.axis_size("cp")
    return lax.ppermute(value, "cp", [(i, i ^ 1) for i in range(length)])


def in_hbm(value):
    return pltpu.with_memory_space_constraint(value, pltpu.HBM)


def nt(a, b):
    return lax.dot_general(a, b, (((1,), (1,)), ((), ())), preferred_element_type=jnp.float32)


def nn(a, b):
    return lax.dot_general(a, b, (((1,), (0,)), ((), ())), preferred_element_type=jnp.float32)


def tiles_of(chunk, near):
    last = BEHIND // TILE + chunk
    return range(EDGE, last + 1) if near else range(chunk, EDGE)


def window_tile(refs, tile, columns):
    far, two, one, here = refs
    block, part = divmod(tile, BS // TILE)
    ref, row = [(far, BS), (far, 0), (two, 0), (one, 0), (here, 0)][block]
    row = row + part * TILE
    return ref[row : row + TILE, columns]


def head_lanes(head):
    return slice(head * CHUNK, (head + 1) * CHUNK)


def head_columns(head):
    return slice(head * HEAD_WIDTH, (head + 1) * HEAD_WIDTH)


def at_tile(index):
    return slice(index * TILE, (index + 1) * TILE)


def pull(moves, sems, pieces):
    copies = []
    for source, target in moves:
        size = target.shape[0] // pieces
        for row in range(0, target.shape[0], size):
            at = pl.ds(row, size)
            copies.append(
                pltpu.make_async_copy(source.at[at], target.at[at], sems.at[len(copies)])
            )
    for copy in copies:
        copy.start()
    return copies


def fetch_first_kernel(grad_ref, key_ref, value_ref, low_ref, high_ref, both_ref, sems):
    moves = [
        (grad_ref.at[pl.ds(0, CHUNK)], low_ref),
        (grad_ref.at[pl.ds(CHUNK, CHUNK)], high_ref),
        (key_ref, both_ref.at[:, pl.ds(0, HEAD_WIDTH)]),
        (value_ref, both_ref.at[:, pl.ds(HEAD_WIDTH, HEAD_WIDTH)]),
    ]
    for copy in pull(moves, sems, 4):
        copy.wait()


def fetch_first(grad, keys, values):
    return pl.pallas_call(
        fetch_first_kernel,
        in_specs=[IN_HBM] * 3,
        out_specs=[WHOLE] * 3,
        out_shape=[
            jax.ShapeDtypeStruct((CHUNK, WIDTH), jnp.bfloat16),
            jax.ShapeDtypeStruct((CHUNK, WIDTH), jnp.bfloat16),
            jax.ShapeDtypeStruct((BS, 2 * HEAD_WIDTH), jnp.bfloat16),
        ],
        scratch_shapes=[pltpu.SemaphoreType.DMA((16,))],
        compiler_params=pltpu.CompilerParams(vmem_limit_bytes=2 * MIB),
        name="fetch_first",
    )(in_hbm(grad), in_hbm(keys), in_hbm(values))


def fetch_kernel(q_ref, segment_ref, q_out, key_marks, query_marks, segments, sems):
    copies = pull([(q_ref, q_out), (segment_ref, segments)], sems, 4)
    for copy in copies[4:]:
        copy.wait()
    first = lax.axis_index("cp") * BS - BEHIND
    lane = lax.broadcasted_iota(jnp.int32, (1, MARKS), 1)
    low = jnp.where(lane == 0, 0, NEVER)
    high = jnp.where(lane == DOCS - 1, NEVER, -NEVER)
    for doc in range(1, DOCS):
        begin = jnp.sum((segments[...] < doc).astype(jnp.int32), axis=(0, 1), keepdims=True)
        low = jnp.where(lane == doc, begin, low)
        high = jnp.where(lane == doc - 1, begin, high)
    low = jnp.where(lane == DOCS, -NEVER, low) - first
    high = jnp.where(lane == DOCS, 0, high) - first

    def inside(rows, begin):
        place = lax.broadcasted_iota(jnp.int32, (rows, MARKS), 0) + begin
        return (place >= low) & (place < high)

    for tile in range((BEHIND + BS) // TILE):
        key_marks[at_tile(tile), :] = jnp.where(inside(TILE, tile * TILE), 1.0, 0.0).astype(
            jnp.bfloat16
        )
    query_marks[...] = jnp.where(inside(BS, BEHIND), 0.0, HIDDEN).astype(jnp.bfloat16)
    for copy in copies[:4]:
        copy.wait()


def fetch(queries, segments):
    return pl.pallas_call(
        fetch_kernel,
        in_specs=[IN_HBM] * 2,
        out_specs=[WHOLE] * 3,
        out_shape=[
            jax.ShapeDtypeStruct(queries.shape, queries.dtype),
            jax.ShapeDtypeStruct((BEHIND + BS, MARKS), jnp.bfloat16),
            jax.ShapeDtypeStruct((BS, MARKS), jnp.bfloat16),
        ],
        scratch_shapes=[
            pltpu.VMEM(segments.shape, segments.dtype),
            pltpu.SemaphoreType.DMA((8,)),
        ],
        compiler_params=pltpu.CompilerParams(vmem_limit_bytes=4 * MIB),
        name="fetch",
    )(in_hbm(queries), in_hbm(segments))


def stack_kernel(a_ref, b_ref, out_ref):
    out_ref[:BS, :] = a_ref[...]
    out_ref[BS:, :] = b_ref[...]


def stack(a, b):
    return pl.pallas_call(
        stack_kernel,
        in_specs=[WHOLE] * 2,
        out_specs=WHOLE,
        out_shape=jax.ShapeDtypeStruct((2 * BS, a.shape[1]), a.dtype),
        compiler_params=pltpu.CompilerParams(vmem_limit_bytes=2 * MIB),
        name="stack",
    )(a, b)


def add_kernel(parity, a_ref, b_ref, out_ref):
    extra = b_ref[...].astype(jnp.float32)
    counts = (lax.axis_index("cp") & 1) == parity
    total = a_ref[...].astype(jnp.float32) + jnp.where(counts, extra, jnp.zeros_like(extra))
    out_ref[...] = total.astype(out_ref.dtype)


def add_where(parity, a, b):
    return pl.pallas_call(
        functools.partial(add_kernel, parity),
        in_specs=[WHOLE, WHOLE],
        out_specs=WHOLE,
        out_shape=jax.ShapeDtypeStruct(a.shape, a.dtype),
        compiler_params=pltpu.CompilerParams(vmem_limit_bytes=4 * MIB),
        name="add_where",
    )(a, b)


def weight_columns(by):
    place = lax.rem(lax.axis_index("hd") + by, 4)
    return pl.ds(pl.multiple_of(place * WIDTH, WIDTH), WIDTH)


def dout_own_kernel(weight_ref, low_ref, high_ref, sum_ref, g_scr, w_scr, sems):
    copies = pull([(weight_ref.at[:, weight_columns(0)], w_scr)], sems, 16)
    g_scr[:CHUNK, :] = low_ref[...]
    g_scr[CHUNK:, :] = high_ref[...]
    for copy in copies:
        copy.wait()
    for i in range(HEADS // 2):
        at = slice(i * BAND, (i + 1) * BAND)
        sum_ref[:, at] = nt(g_scr[...], w_scr[at, :])


def dout_last_kernel(*refs):
    low_ref, high_ref, kept_ref, before_ref, attn_ref = refs[:5]
    inverse = {"near": refs[5:7], "far": refs[7:9]}
    outs = {"near": refs[9:11], "far": refs[11:13]}
    g_scr = refs[13]
    g_scr[:CHUNK, :] = low_ref[...]
    g_scr[CHUNK:, :] = high_ref[...]
    for i in range(HEADS // 2):
        cols = slice(i * BAND, (i + 1) * BAND)
        whole = nt(g_scr[...], kept_ref[cols, :]) + before_ref[:, cols]
        for chunk in range(2):
            rows = slice(chunk * CHUNK, (chunk + 1) * CHUNK)
            dout = whole[rows, :].astype(jnp.bfloat16).astype(jnp.float32)
            product = jnp.transpose(dout * attn_ref[rows, cols].astype(jnp.float32))
            for side in range(2):
                head = 2 * i + side
                delta = jnp.sum(product[head_columns(side), :], axis=0, keepdims=True)
                to = slice((chunk * HEADS + head) * CHUNK, (chunk * HEADS + head + 1) * CHUNK)
                for group in ("near", "far"):
                    inv = inverse[group][chunk][:1, head_lanes(head)]
                    down = jnp.transpose(jnp.broadcast_to(inv, (HEAD_WIDTH, CHUNK)))
                    dout_ref, delta_ref = outs[group]
                    dout_ref[to, :] = (dout[:, head_columns(side)] * down).astype(jnp.bfloat16)
                    delta_ref[:, to] = jnp.broadcast_to(delta * inv, (8, CHUNK))


def dout_own(weight, low, high):
    return pl.pallas_call(
        dout_own_kernel,
        in_specs=[IN_HBM, WHOLE, WHOLE],
        out_specs=WHOLE,
        out_shape=jax.ShapeDtypeStruct((BS, WIDTH), jnp.float32),
        scratch_shapes=[
            pltpu.VMEM((BS, WIDTH), jnp.bfloat16),
            pltpu.VMEM((WIDTH, WIDTH), jnp.bfloat16),
            pltpu.SemaphoreType.DMA((16,)),
        ],
        compiler_params=pltpu.CompilerParams(vmem_limit_bytes=6 * MIB),
        cost_estimate=pl.CostEstimate(
            flops=2 * BS * WIDTH * WIDTH, bytes_accessed=4 * MIB, transcendentals=0
        ),
        name="dout_own",
    )(in_hbm(weight), low, high)


def dout_last(pieces, kept, before, attn, near, far):
    shapes = [
        jax.ShapeDtypeStruct((2 * LANES, HEAD_WIDTH), jnp.bfloat16),
        jax.ShapeDtypeStruct((8, 2 * LANES), jnp.float32),
    ] * 2
    return pl.pallas_call(
        dout_last_kernel,
        in_specs=[WHOLE] * 9,
        out_specs=[WHOLE] * 4,
        out_shape=shapes,
        scratch_shapes=[pltpu.VMEM((BS, WIDTH), jnp.bfloat16)],
        compiler_params=pltpu.CompilerParams(vmem_limit_bytes=8 * MIB),
        cost_estimate=pl.CostEstimate(
            flops=2 * BS * WIDTH * WIDTH, bytes_accessed=8 * MIB, transcendentals=0
        ),
        name="dout_last",
    )(*pieces, kept, before, attn, *near, *far)


def stats_kernel(chunk, near, sides, key_marks, query_marks, q_ref, *refs):
    if near:
        keys = (None, *refs[:3])
        weight_ref, attn_ref, refs = refs[3], refs[4], refs[5:]
        e_ref, out_a, out_b, *kept_refs, sems = refs
        moves = [
            (weight_ref.at[:, weight_columns(side)], kept)
            for side, kept in zip(sides, kept_refs)
        ]
        if len(kept_refs) > len(sides):
            moves.append((attn_ref, kept_refs[-1]))
        copies = pull(moves, sems, 4)
    else:
        keys = (refs[0], None, None, None)
        top_ref, total_ref, low_ref, high_ref, kept_ref, before_ref = refs[1:7]
        e_ref, out_a, out_b, sum_ref = refs[7:]
    rows = slice(chunk * CHUNK, (chunk + 1) * CHUNK)
    factor = SCALE * LOG2E
    tiles = tiles_of(chunk, near)

    def score(head, tile):
        keyed = jnp.concatenate([window_tile(keys, tile, KEY), key_marks[at_tile(tile), :]], axis=1)
        asked = jnp.concatenate([q_ref[rows, head_columns(head)], query_marks[rows, :]], axis=1)
        s = nt(keyed, asked)
        if near and tile == tiles[-1]:
            key = lax.broadcasted_iota(jnp.int32, (TILE, CHUNK), 0)
            s = jnp.where(key <= lax.broadcasted_iota(jnp.int32, (TILE, CHUNK), 1), s, HIDDEN)
        return s

    def highest(head, tile, top):
        most = jnp.max(score(head, tile).reshape(TILE // 8, 8, CHUNK), axis=0)
        return most if top is None else jnp.maximum(top, most)

    def weigh(head, tile, top, total):
        e = jnp.exp2(score(head, tile) * factor - top)
        e_ref[at_tile(tile - tiles[0]), head_lanes(head)] = e.astype(jnp.bfloat16)
        part = jnp.sum(e.reshape(TILE // 8, 8, CHUNK), axis=0)
        return part if total is None else total + part

    jobs = []
    if not near:
        for band in range(HEADS // 2):
            for part, piece_ref in enumerate((low_ref, high_ref)):
                columns = slice(band * BAND, (band + 1) * BAND)
                jobs.append((piece_ref, at_tile(part), columns))

    def work():
        piece_ref, at, columns = jobs.pop(0)
        sum_ref[at, columns] = before_ref[at, columns] + nt(piece_ref[...], kept_ref[columns, :])

    following = None
    for tile in tiles:
        following = highest(0, tile, following)
    for head in range(HEADS):
        top = jnp.max(following, axis=0, keepdims=True) * factor
        following = total = None
        for tile in tiles:
            if head + 1 < HEADS:
                following = highest(head + 1, tile, following)
            total = weigh(head, tile, top, total)
        if jobs:
            work()
        total = jnp.sum(total, axis=0, keepdims=True)
        lanes = head_lanes(head)
        if near:
            out_a[:, lanes] = jnp.broadcast_to(top, (8, CHUNK))
            out_b[:, lanes] = jnp.broadcast_to(total, (8, CHUNK))
        else:
            other_top, other_total = top_ref[:1, lanes], total_ref[:1, lanes]
            most = jnp.maximum(top, other_top)
            near_part, far_part = jnp.exp2(other_top - most), jnp.exp2(top - most)
            inverse = 1.0 / (near_part * other_total + far_part * total)
            out_a[:, lanes] = jnp.broadcast_to(near_part * inverse, (8, CHUNK))
            out_b[:, lanes] = jnp.broadcast_to(far_part * inverse, (8, CHUNK))
    if near:
        for copy in copies:
            copy.wait()


def stats(chunk, near, marks, queries, keys, rest, sides=()):
    span = len(tiles_of(chunk, near)) * TILE
    args = [*marks, queries, *keys, *rest]
    specs = [WHOLE] * len(args)
    shapes = [
        jax.ShapeDtypeStruct((span, LANES), jnp.bfloat16),
        jax.ShapeDtypeStruct((8, LANES), jnp.float32),
        jax.ShapeDtypeStruct((8, LANES), jnp.float32),
    ]
    scratch = []
    if near:
        specs[-2:], args[-2:] = [IN_HBM] * 2, [in_hbm(x) for x in args[-2:]]
        shapes += [jax.ShapeDtypeStruct((WIDTH, WIDTH), jnp.bfloat16)] * len(sides)
        if chunk == 0:
            shapes.append(jax.ShapeDtypeStruct((BS, WIDTH), jnp.bfloat16))
        scratch.append(pltpu.SemaphoreType.DMA((8,)))
    else:
        shapes.append(jax.ShapeDtypeStruct((BS, WIDTH), jnp.float32))
    return pl.pallas_call(
        functools.partial(stats_kernel, chunk, near, sides),
        in_specs=specs,
        out_specs=[WHOLE] * len(shapes),
        out_shape=shapes,
        scratch_shapes=scratch,
        compiler_params=pltpu.CompilerParams(vmem_limit_bytes=6 * MIB),
        cost_estimate=pl.CostEstimate(
            flops=4 * LANES * span * HEAD_WIDTH,
            bytes_accessed=4 * MIB,
            transcendentals=LANES * span,
        ),
        name=f"stats{chunk}{'near' if near else 'far'}",
    )(*args)


def group_tiles(chunk, group):
    begin, end = {"four": (0, 2), "three": (2, 4), "mid": (4, 8), "own": (8, 10)}[group]
    seen = (*tiles_of(chunk, False), *tiles_of(chunk, True))
    return [tile for tile in seen if begin <= tile < end]


def main_kernel(group, q_ref, dout_ref, delta_ref, *refs):
    values = {
        "four": lambda: (refs[0], None, None, None),
        "three": lambda: (refs[0], None, None, None),
        "mid": lambda: (None, refs[0], refs[1], None),
        "own": lambda: (None, None, None, refs[0]),
    }[group]()
    refs = refs[2 if group == "mid" else 1 :]
    if group == "mid":
        back_ref, refs = refs[0], refs[1:]
    refs = refs[2:]
    ds_refs, outs, sum_ref = refs[:2], refs[2:-1], refs[-1]
    begun = set()
    window = group_tiles(0, group)
    window = list(range(window[0], window[0] + (4 if group == "mid" else 2)))
    for chunk in range(2):
        tiles = group_tiles(chunk, group)
        base = tiles_of(chunk, group in ("mid", "own"))[0]
        ds_ref = ds_refs[chunk]
        for pair in range(HEADS // 2):
            lanes = slice(2 * pair * CHUNK, 2 * (pair + 1) * CHUNK)
            first = (chunk * HEADS + 2 * pair) * CHUNK
            dout = dout_ref[first : first + 2 * CHUNK, :]
            queries = jnp.concatenate(
                [
                    q_ref[chunk * CHUNK : (chunk + 1) * CHUNK, head_columns(2 * pair + side)]
                    for side in range(2)
                ],
                axis=0,
            )
            at = {tile: at_tile(tile - base) for tile in tiles}
            to = {tile: at_tile(tile - window[0]) for tile in tiles}
            more = {tile: tile in begun for tile in tiles}
            begun.update(tiles)
            last = pair == HEADS // 2 - 1

            def store(tile, side, value):
                columns = head_columns(side)
                if more[tile]:
                    value = value + sum_ref[to[tile], columns]
                if last and (chunk == 1 or tile not in group_tiles(1, group)):
                    block, part = divmod(tile - window[0], BS // TILE)
                    out = outs[block]
                    if group == "mid" and block == 0:
                        extra = back_ref[at_tile(part), columns].astype(jnp.float32)
                        even = (lax.axis_index("cp") & 1) == 0
                        value = value + jnp.where(even, extra, jnp.zeros_like(extra))
                    out[at_tile(part), columns] = value.astype(out.dtype)
                else:
                    sum_ref[to[tile], columns] = value

            for tile in tiles:
                store(tile, 1, nn(ds_ref[at[tile], lanes], dout))
            for side in range(2):
                here = head_lanes(2 * pair + side)
                row = first + side * CHUNK
                for tile in tiles:
                    dp = nt(window_tile(values, tile, VALUE), dout[at_tile(side), :])
                    prob = ds_ref[at[tile], here].astype(jnp.float32)
                    ds_ref[at[tile], here] = (
                        prob * (dp - delta_ref[:1, row : row + CHUNK])
                    ).astype(jnp.bfloat16)
            for tile in tiles:
                store(tile, 0, nn(ds_ref[at[tile], lanes], queries) * SCALE)


def main(group, queries, dout, delta, values, e, back=()):
    blocks = 2 if group == "mid" else 1
    shapes = [jax.ShapeDtypeStruct(x.shape, x.dtype) for x in e]
    kind = jnp.float32 if group == "own" else jnp.bfloat16
    shapes += [jax.ShapeDtypeStruct((BS, 2 * HEAD_WIDTH), kind)] * blocks
    args = [queries, dout, delta, *values, *back, *e]
    tiles = sum(len(group_tiles(chunk, group)) for chunk in range(2))
    return pl.pallas_call(
        functools.partial(main_kernel, group),
        in_specs=[WHOLE] * len(args),
        out_specs=[WHOLE] * len(shapes),
        out_shape=shapes,
        scratch_shapes=[pltpu.VMEM((blocks * BS, 2 * HEAD_WIDTH), jnp.float32)],
        input_output_aliases={len(args) - 2: 0, len(args) - 1: 1},
        compiler_params=pltpu.CompilerParams(vmem_limit_bytes=6 * MIB),
        cost_estimate=pl.CostEstimate(
            flops=2 * 3 * LANES * tiles * TILE * HEAD_WIDTH,
            bytes_accessed=4 * MIB,
            transcendentals=0,
        ),
        name=f"main_{group}",
    )(*args)


def query_kernel(far_ref, two_ref, one_ref, here_ref, *refs):
    far_ds, near_ds, (out_ref, k_scr) = refs[:2], refs[2:4], refs[4:]
    keys = (far_ref, two_ref, one_ref, here_ref)
    window = (BEHIND + BS) // TILE
    for tile in range(window):
        k_scr[:, at_tile(tile)] = jnp.transpose(window_tile(keys, tile, KEY))
    for chunk in range(2):
        rows = slice(chunk * CHUNK, (chunk + 1) * CHUNK)
        end = (BEHIND // TILE + chunk + 1) * TILE
        for head in range(HEADS):
            lanes = head_lanes(head)
            grad = nn(k_scr[:, chunk * TILE : EDGE * TILE], far_ds[chunk][:, lanes])
            grad = grad + nn(k_scr[:, EDGE * TILE : end], near_ds[chunk][:, lanes])
            out_ref[rows, head_columns(head)] = (jnp.transpose(grad) * SCALE).astype(jnp.bfloat16)


def query_grad(keys, ds):
    return pl.pallas_call(
        query_kernel,
        in_specs=[WHOLE] * (len(keys) + len(ds)),
        out_specs=WHOLE,
        out_shape=jax.ShapeDtypeStruct((BS, WIDTH), jnp.bfloat16),
        scratch_shapes=[pltpu.VMEM((HEAD_WIDTH, BEHIND + BS), jnp.bfloat16)],
        compiler_params=pltpu.CompilerParams(vmem_limit_bytes=6 * MIB),
        cost_estimate=pl.CostEstimate(
            flops=4 * LANES * 9 * TILE * HEAD_WIDTH, bytes_accessed=MIB, transcendentals=0
        ),
        name="query_grad",
    )(*keys, *ds)


def close_kernel(mine_ref, four_ref, two_ref, one_ref, dk_ref, dv_ref):
    total = mine_ref[...] + four_ref[...].astype(jnp.float32)
    total = total + two_ref[...].astype(jnp.float32) + one_ref[...].astype(jnp.float32)
    dk_ref[...] = total[:, :HEAD_WIDTH].astype(jnp.bfloat16)
    dv_ref[...] = total[:, HEAD_WIDTH:].astype(jnp.bfloat16)


def close(mine, four, two, one):
    return pl.pallas_call(
        close_kernel,
        in_specs=[WHOLE] * 4,
        out_specs=[WHOLE] * 2,
        out_shape=[jax.ShapeDtypeStruct((BS, HEAD_WIDTH), jnp.bfloat16)] * 2,
        compiler_params=pltpu.CompilerParams(vmem_limit_bytes=6 * MIB),
        name="close",
    )(mine, four, two, one)


def body(queries, keys, values, attn_out, out_grad, out_weight, segment):
    segments = segment.reshape(128, -1)

    barrier = lax.optimization_barrier

    low, high, here = fetch_first(out_grad, keys, values)
    prev_low, next_high = shifted(low, "hd", 1), shifted(high, "hd", -1)
    one, two = shifted(here, "cp", 1), shifted(here, "cp", 2)
    here, queries_in = barrier((here, queries))
    queries, *marks = fetch(queries_in, segments)
    queries, weight_in = barrier((queries, out_weight))
    partial = dout_own(weight_in, low, high)
    partial, here, low, high = barrier((partial, here, low, high))
    prev_high, next_low = shifted(high, "hd", 1), shifted(low, "hd", -1)
    one, two, partial = barrier((one, two, partial))
    far = shifted(stack(one, two), "cp", 2)

    near = (two, one, here)
    *near_one, weight_next, weight_last = stats(
        1, True, marks, queries, near, (out_weight, attn_out), (1, 2)
    )
    prev_low, next_high, near_one, two = barrier((prev_low, next_high, near_one, two))
    far_low, far_high = shifted(prev_low, "hd", 1), shifted(next_high, "hd", -1)
    *near_zero, weight_prev, attn = stats(
        0, True, marks, queries, (two, one, here), (out_weight, attn_out), (3,)
    )
    e_near = [near_zero[0], near_one[0]]
    prev_high, next_low, near_zero = barrier((prev_high, next_low, near_zero))
    far_zero, near_inv_zero, far_inv_zero, partial = stats(
        0, False, marks, queries, (far,),
        (*near_zero[1:], prev_low, prev_high, weight_prev, partial),
    )
    far_one, near_inv_one, far_inv_one, partial = stats(
        1, False, marks, queries, (far,),
        (*near_one[1:], next_low, next_high, weight_next, partial),
    )
    dout_n, delta_n, dout_f, delta_f = dout_last(
        (far_low, far_high), weight_last, partial, attn,
        (near_inv_zero, near_inv_one), (far_inv_zero, far_inv_one),
    )
    *ds_far, to_three = main(
        "three", queries, dout_f, delta_f, (far,), (far_zero, far_one)
    )
    back = swapped(to_three)
    *ds_far, to_four = main("four", queries, dout_f, delta_f, (far,), ds_far)
    to_four = add_where(1, to_four, back)
    to_four, dout_n = barrier((to_four, dout_n))
    from_four = shifted(to_four, "cp", -4)
    *ds_near, to_two, to_one = main(
        "mid", queries, dout_n, delta_n, (two, one), e_near, (back,)
    )
    to_one, to_two, ds_near = barrier((to_one, to_two, ds_near))
    from_one, from_two = shifted(to_one, "cp", -1), shifted(to_two, "cp", -2)
    *ds_near, mine = main("own", queries, dout_n, delta_n, (here,), ds_near)
    from_four, ds_near = barrier((from_four, ds_near))
    query_out = query_grad((far, two, one, here), (*ds_far, *ds_near))
    mine, query_out = barrier((mine, query_out))
    dk, dv = close(mine, from_four, from_two, from_one)
    return query_out, dk, dv


def solution(mesh):
    return jax.shard_map(
        body,
        mesh=mesh,
        in_specs=(
            P("cp", "hd"),
            P("cp", "hd"),
            P("cp", "hd"),
            P("cp", "hd"),
            P("cp", "hd"),
            P("hd", None),
            P(),
        ),
        out_specs=(P("cp", "hd"), P("cp", "hd"), P("cp", "hd")),
        check_vma=False,
    )
```
